32 devices in a mesh: narrow: 4 (over x, core), wide: 8 (over z, y).
Axes of the slice: x: 2, y: 2, z: 4, core: 2. Of those that a mesh axis runs over, the one named last changes fastest.
Arguments:
- token_ids: int32 [16384], P(('narrow', 'wide')), may hold values from 0 to 50303
- seq_lengths: int32 [32], P(('narrow', 'wide')), may hold values from 128 to 512, as said below
- loss_slots: int32 [1024], P(('narrow', 'wide')), may hold values from -1 to 511, as said below
- target_ids: int32 [1024], P(('narrow', 'wide')), may hold values from 0 to 50303
- step_count: int32 [], replicated, may hold values from 2 to 20
- w_qkv: float32 [2, 1024, 3072], P(None, ('narrow', 'wide')), may hold values from -0.1875 to 0.1875
- w_out: float32 [2, 1024, 1024], P(None, ('narrow', 'wide')), may hold values from -0.75 to 0.75
- w_fc: float32 [2, 1024, 4096], P(None, ('narrow', 'wide')), may hold values from -0.1875 to 0.1875
- w_proj: float32 [2, 4096, 1024], P(None, ('narrow', 'wide')), may hold values from -0.09375 to 0.09375
- vectors: float32 [26624], P(('narrow', 'wide'))
- pos_table: float32 [1024, 1024], P(('narrow', 'wide')), may hold values from -0.6 to 0.6
- embed_table: float32 [50304, 1024], P(('narrow', 'wide')), may hold values from -1 to 1
- mom_qkv: float32 [2, 1024, 3072], P(None, ('narrow', 'wide')), may hold values from -1.4305115e-06 to 1.4305115e-06
- mom_out: float32 [2, 1024, 1024], P(None, ('narrow', 'wide')), may hold values from -1.4305115e-06 to 1.4305115e-06
- mom_fc: float32 [2, 1024, 4096], P(None, ('narrow', 'wide')), may hold values from -1.4305115e-06 to 1.4305115e-06
- mom_proj: float32 [2, 4096, 1024], P(None, ('narrow', 'wide')), may hold values from -1.4305115e-06 to 1.4305115e-06
- mom_vectors: float32 [26624], P(('narrow', 'wide')), may hold values from -5.722046e-06 to 5.722046e-06
- mom_pos: float32 [1024, 1024], P(('narrow', 'wide')), may hold values from -1.4305115e-06 to 1.4305115e-06
- mom_embed: float32 [50304, 1024], P(('narrow', 'wide')), may hold values from -1.4305115e-06 to 1.4305115e-06
- sec_qkv: float32 [2, 1024, 3072], P(None, ('narrow', 'wide')), may hold values from 5.144541e-14 to 2.0578164e-13
- sec_out: float32 [2, 1024, 1024], P(None, ('narrow', 'wide')), may hold values from 5.144541e-14 to 2.0578164e-13
- sec_fc: float32 [2, 1024, 4096], P(None, ('narrow', 'wide')), may hold values from 5.144541e-14 to 2.0578164e-13
- sec_proj: float32 [2, 4096, 1024], P(None, ('narrow', 'wide')), may hold values from 5.144541e-14 to 2.0578164e-13
- sec_vectors: float32 [26624], P(('narrow', 'wide')), may hold values from 8.2312656e-13 to 3.2925062e-12
- sec_pos: float32 [1024, 1024], P(('narrow', 'wide')), may hold values from 5.144541e-14 to 2.0578164e-13
- sec_embed: float32 [50304, 1024], P(('narrow', 'wide')), may hold values from 5.144541e-14 to 2.0578164e-13
Outputs:
- loss: float32 [], replicated
- grad_norm: float32 [], replicated
- new_qkv: float32 [2, 1024, 3072], P(None, ('narrow', 'wide'))
- new_out: float32 [2, 1024, 1024], P(None, ('narrow', 'wide'))
- new_fc: float32 [2, 1024, 4096], P(None, ('narrow', 'wide'))
- new_proj: float32 [2, 4096, 1024], P(None, ('narrow', 'wide'))
- new_vectors: float32 [26624], P(('narrow', 'wide'))
- new_pos: float32 [1024, 1024], P(('narrow', 'wide'))
- new_embed: float32 [50304, 1024], P(('narrow', 'wide'))
- first_qkv: float32 [2, 1024, 3072], P(None, ('narrow', 'wide'))
- first_out: float32 [2, 1024, 1024], P(None, ('narrow', 'wide'))
- first_fc: float32 [2, 1024, 4096], P(None, ('narrow', 'wide'))
- first_proj: float32 [2, 4096, 1024], P(None, ('narrow', 'wide'))
- first_vectors: float32 [26624], P(('narrow', 'wide'))
- first_pos: float32 [1024, 1024], P(('narrow', 'wide'))
- first_embed: float32 [50304, 1024], P(('narrow', 'wide'))
- second_qkv: float32 [2, 1024, 3072], P(None, ('narrow', 'wide'))
- second_out: float32 [2, 1024, 1024], P(None, ('narrow', 'wide'))
- second_fc: float32 [2, 1024, 4096], P(None, ('narrow', 'wide'))
- second_proj: float32 [2, 4096, 1024], P(None, ('narrow', 'wide'))
- second_vectors: float32 [26624], P(('narrow', 'wide'))
- second_pos: float32 [1024, 1024], P(('narrow', 'wide'))
- second_embed: float32 [50304, 1024], P(('narrow', 'wide'))
The draws below stay inside these ranges and needn't reach their ends.
Inputs may be any that keep to these rules, and one draw needn't show every extreme that they name: `seq_lengths`: the last sequence has 512 tokens. `loss_slots`: each sequence owns 32 consecutive slots; a used slot holds a position below that sequence's length, an unused one holds -1; the first slot of every sequence is used and holds its last position; the last sequence uses all of its slots.
All inputs are finite; a program needn't handle non-finite values.
Results may differ from the reference program's by a relative error of at most 0.005.
The reference program's roundings to bfloat16 on the way count: a program that leaves them out, or rounds other values in their place, can miss the bound.
Values may be sent and summed in bfloat16 or wider, within the bound.
A program may use at most 384 MiB of HBM per device.

```python
import math
import jax
import jax.numpy as jnp
from jax import lax

D = 1024
HEADS = 16
HD = 64
FF = 4096
VOCAB = 50304
POS = 1024
LAYERS = 2
LEN = 512
LOWLEN = 128
LOSS_DEV = 32
SEQS = 32
TOKENS = 16384
NLOSS = 1024
SMALL = 26624
NPAR = 77752320


def lengths_from(key):
    device_ids = jnp.arange(SEQS)
    rising = LOWLEN + (LEN - LOWLEN) * device_ids // max(SEQS - 1, 1)
    lowered = jax.random.randint(jax.random.fold_in(key, 11), (SEQS,), 0, (LEN - LOWLEN) // 4 + 1)
    result_lengths = jnp.clip(rising - lowered, LOWLEN, LEN).at[SEQS - 1].set(LEN)
    return result_lengths.astype(jnp.int32)


def skewed_vocab(key, total_count):
    first_part = jax.random.randint(jax.random.fold_in(key, 1), (total_count,), 0, 32768)
    second_part = jax.random.randint(jax.random.fold_in(key, 2), (total_count,), 0, VOCAB)
    drawn = first_part * second_part // 32768
    return drawn.at[0].set(VOCAB - 1).at[1].set(0).astype(jnp.int32)


def draw_token_ids(key, part):
    return skewed_vocab(jax.random.fold_in(key, 21), TOKENS)


def draw_target_ids(key, part):
    return skewed_vocab(jax.random.fold_in(key, 22), NLOSS)


def draw_seq_lengths(key, part):
    return lengths_from(key)


def draw_loss_slots(key, part):
    seq_lengths = lengths_from(key)
    device_ids = jnp.arange(SEQS)
    counted = LOSS_DEV // 4 + (LOSS_DEV - LOSS_DEV // 4) * device_ids // max(SEQS - 1, 1)
    random_bits = jax.random.randint(jax.random.fold_in(key, 12), (SEQS, LOSS_DEV), 0, 1 << 20)
    positions = random_bits % seq_lengths[:, None]
    positions = positions.at[:, 0].set(seq_lengths - 1)
    slot_ids = jnp.arange(LOSS_DEV)[None, :]
    positions = jnp.where(slot_ids < counted[:, None], positions, -1)
    return positions.reshape(NLOSS).astype(jnp.int32)


def draw_vectors(key, part):
    slot_ids = jnp.arange(SMALL)
    per_layer = 8 * D + FF
    within_layer = slot_ids % per_layer
    layer_gain = (within_layer < D) | (within_layer >= 2 * D) & (within_layer < 3 * D)
    final_gain = (slot_ids >= LAYERS * per_layer) & (slot_ids < LAYERS * per_layer + D)
    is_gain = jnp.where(slot_ids < LAYERS * per_layer, layer_gain, final_gain)
    gain_values = jax.random.uniform(jax.random.fold_in(key, 31), (SMALL,), jnp.float32, 0.5, 1.5)
    shifts = 0.2 * jax.random.normal(jax.random.fold_in(key, 32), (SMALL,), jnp.float32)
    return jnp.where(is_gain, gain_values, shifts)


def draw_embed_table(key, part):
    row_frac = jnp.arange(VOCAB).astype(jnp.float32) / VOCAB
    row_scale = 0.02 * jnp.exp(row_frac * 2.0794415)
    jitter = jnp.exp(jax.random.uniform(jax.random.fold_in(key, 41), (VOCAB,), jnp.float32, -0.35, 0.35))
    entries = jnp.clip(jax.random.normal(jax.random.fold_in(key, 42), (VOCAB, D), jnp.float32), -4.0, 4.0)
    return entries * (row_scale * jitter)[:, None]


def level_of(own_key, extent, cuts, low, high):
    level = 1.0
    for axis_at, parts in cuts:
        steps = jax.random.uniform(jax.random.fold_in(jax.random.fold_in(own_key, 6), axis_at), (parts,), jnp.float32, low / len(cuts), high / len(cuts))
        level = level * jnp.repeat(jnp.exp(steps), extent[axis_at] // parts).reshape((-1,) + (1,) * (len(extent) - 1 - axis_at))
    return level


def noise(stream_key, shape, scale, most, split=(), kind=jnp.bfloat16):
    array = jax.random.normal(stream_key, shape, jnp.float32) * scale
    if len(split) > 0:
        array = level_of(stream_key, shape, split, -0.22, 0.18) * array
    return jnp.clip(array, min=-most, max=most).astype(kind)


def setup_inputs(seed: int = 0) -> dict:
    seeds = jax.random.split(jax.random.key(seed), 27)
    token_ids = draw_token_ids(jax.random.fold_in(seeds[26], 71), 0)
    seq_lengths = draw_seq_lengths(jax.random.fold_in(seeds[26], 71), 0)
    loss_slots = draw_loss_slots(jax.random.fold_in(seeds[26], 71), 0)
    target_ids = draw_target_ids(jax.random.fold_in(seeds[26], 71), 0)
    step_count = jax.random.randint(seeds[4], (), 2, 21).astype(jnp.int32)
    w_qkv = noise(seeds[5], (LAYERS, D, 3 * D), D ** -0.5, 0.1875, ((1, 32),), jnp.float32)
    w_out = noise(seeds[6], (LAYERS, D, D), (D // 16) ** -0.5, 0.75, ((1, 32),), jnp.float32)
    w_fc = noise(seeds[7], (LAYERS, D, FF), D ** -0.5, 0.1875, ((1, 32),), jnp.float32)
    w_proj = noise(seeds[8], (LAYERS, FF, D), FF ** -0.5, 0.09375, ((1, 32),), jnp.float32)
    vectors = draw_vectors(jax.random.fold_in(seeds[26], 71), 0)
    pos_table = noise(seeds[10], (POS, D), 0.1, 0.6, ((0, 32),), jnp.float32)
    embed_table = draw_embed_table(jax.random.fold_in(seeds[26], 71), 0)
    mom_qkv = noise(seeds[12], (LAYERS, D, 3 * D), (0.002 / NPAR ** 0.5), 1.430511474609375e-06, ((1, 32),), jnp.float32)
    mom_out = noise(seeds[13], (LAYERS, D, D), (0.002 / NPAR ** 0.5), 1.430511474609375e-06, ((1, 32),), jnp.float32)
    mom_fc = noise(seeds[14], (LAYERS, D, FF), (0.002 / NPAR ** 0.5), 1.430511474609375e-06, ((1, 32),), jnp.float32)
    mom_proj = noise(seeds[15], (LAYERS, FF, D), (0.002 / NPAR ** 0.5), 1.430511474609375e-06, ((1, 32),), jnp.float32)
    mom_vectors = noise(seeds[16], (SMALL,), (0.008 / NPAR ** 0.5), 5.7220458984375e-06, ((0, 32),), jnp.float32)
    mom_pos = noise(seeds[17], (POS, D), (0.002 / NPAR ** 0.5), 1.430511474609375e-06, ((0, 32),), jnp.float32)
    mom_embed = noise(seeds[18], (VOCAB, D), (0.002 / NPAR ** 0.5), 1.430511474609375e-06, ((0, 32),), jnp.float32)
    sec_qkv = jnp.clip(jnp.exp(math.log(2.0578164010038452e-13) - 1.3862944 * jax.random.uniform(seeds[19], (LAYERS, D, 3 * D), jnp.float32) ** level_of(seeds[19], (LAYERS, D, 3 * D), ((1, 32),), -0.2, 0.2)), 5.144541002509613e-14, 2.0578164010038452e-13)
    sec_out = jnp.clip(jnp.exp(math.log(2.0578164010038452e-13) - 1.3862944 * jax.random.uniform(seeds[20], (LAYERS, D, D), jnp.float32) ** level_of(seeds[20], (LAYERS, D, D), ((1, 32),), -0.2, 0.2)), 5.144541002509613e-14, 2.0578164010038452e-13)
    sec_fc = jnp.clip(jnp.exp(math.log(2.0578164010038452e-13) - 1.3862944 * jax.random.uniform(seeds[21], (LAYERS, D, FF), jnp.float32) ** level_of(seeds[21], (LAYERS, D, FF), ((1, 32),), -0.2, 0.2)), 5.144541002509613e-14, 2.0578164010038452e-13)
    sec_proj = jnp.clip(jnp.exp(math.log(2.0578164010038452e-13) - 1.3862944 * jax.random.uniform(seeds[22], (LAYERS, FF, D), jnp.float32) ** level_of(seeds[22], (LAYERS, FF, D), ((1, 32),), -0.2, 0.2)), 5.144541002509613e-14, 2.0578164010038452e-13)
    sec_vectors = jnp.clip(jnp.exp(math.log(3.2925062416061524e-12) - 1.3862944 * jax.random.uniform(seeds[23], (SMALL,), jnp.float32) ** level_of(seeds[23], (SMALL,), ((0, 32),), -0.2, 0.2)), 8.231265604015381e-13, 3.2925062416061524e-12)
    sec_pos = jnp.clip(jnp.exp(math.log(2.0578164010038452e-13) - 1.3862944 * jax.random.uniform(seeds[24], (POS, D), jnp.float32) ** level_of(seeds[24], (POS, D), ((0, 32),), -0.2, 0.2)), 5.144541002509613e-14, 2.0578164010038452e-13)
    sec_embed = jnp.clip(jnp.exp(math.log(2.0578164010038452e-13) - 1.3862944 * jax.random.uniform(seeds[25], (VOCAB, D), jnp.float32) ** level_of(seeds[25], (VOCAB, D), ((0, 32),), -0.2, 0.2)), 5.144541002509613e-14, 2.0578164010038452e-13)
    return {"token_ids": token_ids, "seq_lengths": seq_lengths, "loss_slots": loss_slots, "target_ids": target_ids, "step_count": step_count, "w_qkv": w_qkv, "w_out": w_out, "w_fc": w_fc, "w_proj": w_proj, "vectors": vectors, "pos_table": pos_table, "embed_table": embed_table, "mom_qkv": mom_qkv, "mom_out": mom_out, "mom_fc": mom_fc, "mom_proj": mom_proj, "mom_vectors": mom_vectors, "mom_pos": mom_pos, "mom_embed": mom_embed, "sec_qkv": sec_qkv, "sec_out": sec_out, "sec_fc": sec_fc, "sec_proj": sec_proj, "sec_vectors": sec_vectors, "sec_pos": sec_pos, "sec_embed": sec_embed}


@jax.custom_vjp
def low(v):
    return lax.optimization_barrier(v.astype(jnp.bfloat16)).astype(jnp.float32)

@jax.custom_vjp
def low_back(v):
    return v

def low_keep(v):
    return (low(v), None)

def low_pass(kept, grad):
    return (grad,)

def back_keep(v):
    return (v, None)

def back_low(kept, grad):
    return (low(grad),)
low.defvjp(low_keep, low_pass)
low_back.defvjp(back_keep, back_low)
CLIP_LIMIT = 0.002
RATE_MATRIX = 0.03
RATE_VECTOR = 0.3
DECAY_MATRIX = 0.1
HIGHEST = lax.Precision.HIGHEST

def matmul_high(left, right):
    return jnp.dot(left, right, precision=HIGHEST)

def layer_norm(values, gain, shift):
    center = values - lax.optimization_barrier(jnp.mean(values, axis=-1, keepdims=True))
    spread = lax.optimization_barrier(jnp.mean(center * center, axis=-1, keepdims=True))
    return center * lax.rsqrt(spread + 1e-05) * gain + shift

def attend_group(inputs):
    query_rows, key_rows, value_rows, group_lengths = inputs
    scores = low_back(jnp.einsum('gqhd,gkhd->ghqk', query_rows, key_rows, precision=HIGHEST) * 0.125)
    positions = jnp.arange(LEN)
    causal = positions[None, None, None, :] <= positions[None, None, :, None]
    inside = positions[None, None, None, :] < group_lengths[:, None, None, None]
    scores = jnp.where(causal & inside, scores, -1e+30)
    attn_probs = low(jax.nn.softmax(scores, axis=-1))
    return jnp.einsum('ghqk,gkhd->gqhd', attn_probs, value_rows, precision=HIGHEST)

def layer_forward(stream, weights, vector, seq_lengths):
    w_qkv, w_out, w_fc, w_proj = weights
    groups = SEQS // 8
    normed = low(layer_norm(stream, vector[0:D], vector[D:2 * D])).reshape(TOKENS, D)
    qkv_bias = jnp.concatenate([vector[4 * D:5 * D], jnp.zeros((D,), jnp.float32), vector[5 * D:6 * D]])
    projected = low(low_back(matmul_high(normed, w_qkv) + qkv_bias))
    shaped = projected.reshape(groups, 8, LEN, 3, HEADS, HD)
    mixed = lax.map(jax.checkpoint(attend_group), (shaped[:, :, :, 0], shaped[:, :, :, 1], shaped[:, :, :, 2], seq_lengths.reshape(groups, 8)))
    mixed = low(low_back(mixed.reshape(TOKENS, D)))
    stream = stream + low_back(matmul_high(mixed, w_out) + vector[6 * D:7 * D]).reshape(SEQS, LEN, D)
    normed_two = low(layer_norm(stream, vector[2 * D:3 * D], vector[3 * D:4 * D])).reshape(TOKENS, D)
    hidden_pre = low_back(matmul_high(normed_two, w_fc) + vector[8 * D:8 * D + FF])
    hidden = low(jax.nn.gelu(hidden_pre, approximate=True))
    return stream + low_back(matmul_high(hidden, w_proj) + vector[7 * D:8 * D]).reshape(SEQS, LEN, D)

def loss_block(inputs, table):
    row_block, target_block, valid_block = inputs
    logits = low_back(matmul_high(row_block, table.T))
    log_total = jax.nn.logsumexp(logits, axis=-1)
    target_logit = jnp.take_along_axis(logits, target_block[:, None], axis=-1)[:, 0]
    return jnp.sum((log_total - target_logit) * valid_block)

def total_loss(params, token_ids, seq_lengths, loss_slots, target_ids, token_total):
    w_qkv, w_out, w_fc, w_proj, vectors, pos_table, embed_table = jax.tree.map(low, params)
    per_layer = 8 * D + FF
    stream = embed_table[token_ids.reshape(SEQS, LEN)] + pos_table[:LEN][None]
    for layer_at in range(LAYERS):
        weights = (w_qkv[layer_at], w_out[layer_at], w_fc[layer_at], w_proj[layer_at])
        stream = layer_forward(stream, weights, vectors[layer_at * per_layer:(layer_at + 1) * per_layer], seq_lengths)
    tail_start = LAYERS * per_layer
    final_norm = layer_norm(stream, vectors[tail_start:tail_start + D], vectors[tail_start + D:tail_start + 2 * D])
    slot_table = loss_slots.reshape(SEQS, LOSS_DEV)
    is_valid = (slot_table >= 0).astype(jnp.float32)
    picked = low(final_norm[jnp.arange(SEQS)[:, None], jnp.maximum(slot_table, 0)])
    groups = SEQS // 8
    block_sums = lax.map(jax.checkpoint(lambda inputs: loss_block(inputs, embed_table)), (picked.reshape(groups, 8 * LOSS_DEV, D), target_ids.reshape(groups, 8 * LOSS_DEV), is_valid.reshape(groups, 8 * LOSS_DEV)))
    return jnp.sum(block_sums) / token_total

def adamw(weight, moment_one, moment_two, gradient, step_rate, decay_rate, step_float):
    one_new = 0.5 * moment_one + 0.5 * gradient
    two_new = 0.5 * moment_two + 0.5 * gradient * gradient
    fix_scale = 1.0 - jnp.power(0.5, step_float)
    update = one_new / fix_scale / (jnp.sqrt(two_new / fix_scale) + 1e-08)
    return (weight - step_rate * (update + decay_rate * weight), one_new, two_new)

def reference(token_ids, seq_lengths, loss_slots, target_ids, step_count, w_qkv, w_out, w_fc, w_proj, vectors, pos_table, embed_table, mom_qkv, mom_out, mom_fc, mom_proj, mom_vectors, mom_pos, mom_embed, sec_qkv, sec_out, sec_fc, sec_proj, sec_vectors, sec_pos, sec_embed):
    token_total = jnp.sum(seq_lengths).astype(jnp.float32)
    params = (w_qkv, w_out, w_fc, w_proj, vectors, pos_table, embed_table)
    loss_value, pullback = jax.vjp(lambda *values: total_loss(values, token_ids, seq_lengths, loss_slots, target_ids, token_total), *params)
    gradients = pullback(jnp.ones_like(loss_value))
    squares = jnp.sum(jnp.stack([jnp.sum(member * member) for member in gradients]))
    grad_norm = jnp.sqrt(squares)
    factor = CLIP_LIMIT / jnp.maximum(grad_norm, CLIP_LIMIT)
    step_float = step_count.astype(jnp.float32)
    moments_one = (mom_qkv, mom_out, mom_fc, mom_proj, mom_vectors, mom_pos, mom_embed)
    moments_two = (sec_qkv, sec_out, sec_fc, sec_proj, sec_vectors, sec_pos, sec_embed)
    step_rates = (RATE_MATRIX, RATE_MATRIX, RATE_MATRIX, RATE_MATRIX, RATE_VECTOR, RATE_MATRIX, RATE_MATRIX)
    decay_rates = (DECAY_MATRIX, DECAY_MATRIX, DECAY_MATRIX, DECAY_MATRIX, 0.0, DECAY_MATRIX, DECAY_MATRIX)
    results = [adamw(params[where_at], moments_one[where_at], moments_two[where_at], gradients[where_at] * factor, step_rates[where_at], decay_rates[where_at], step_float) for where_at in range(7)]
    return (loss_value, grad_norm, results[0][0], results[1][0], results[2][0], results[3][0], results[4][0], results[5][0], results[6][0], results[0][1], results[1][1], results[2][1], results[3][1], results[4][1], results[5][1], results[6][1], results[0][2], results[1][2], results[2][2], results[3][2], results[4][2], results[5][2], results[6][2])
```

```python
import jax
import jax.numpy as jnp
from jax import lax
from jax.sharding import PartitionSpec as P

D = 1024
HEADS = 16
HD = 64
FF = 4096
POS = 1024
LAYERS = 2
LEN = 512
LOSS_DEV = 32


CLIP_LIMIT = 0.002
RATE_MATRIX = 0.03
RATE_VECTOR = 0.3
DECAY_MATRIX = 0.1


class Net:
    def __init__(self):
        self.narrow_at = lax.axis_index("narrow")
        self.wide_at = lax.axis_index("wide")
        self.narrow_size = lax.axis_size("narrow")
        self.size = lax.axis_size("wide")
        size = self.size
        self.core = self.narrow_at % 2
        self.half = self.narrow_at // 2
        self.halves = self.narrow_size // 2
        self.place = jnp.where(
            self.wide_at % 2 == 0, self.wide_at // 2, size - 1 - (self.wide_at - 1) // 2
        )
        self.device = self.narrow_at * size + self.wide_at
        order = list(range(0, size, 2)) + list(range(size - 1, 0, -2))
        pairs = [(n, w) for n in range(self.narrow_size) for w in range(size)]
        self.core_pairs = [(n * size + w, (n ^ 1) * size + w) for n, w in pairs]
        self.half_pairs = [(n * size + w, (n ^ 2) * size + w) for n, w in pairs]
        self.right = [
            (n * size + order[i], n * size + order[(i + 1) % size])
            for n in range(self.narrow_size)
            for i in range(size)
        ]
        self.left = [(later, earlier) for earlier, later in self.right]

    def step(self, array, pairs):
        return lax.ppermute(array, ("narrow", "wide"), pairs)

    def swap_core(self, array):
        return self.step(array, self.core_pairs)

    def swap_half(self, array):
        return self.step(array, self.half_pairs)

    def flip(self, array, bit):
        size = self.size
        pairs = [
            (n * size + w, n * size + (w ^ bit))
            for n in range(self.narrow_size)
            for w in range(size)
        ]
        return self.step(array, pairs)

    def wide_of(self, offset):
        size = self.size
        at = lax.rem(self.place + offset, size)
        return jnp.where(at < size // 2, 2 * at, 2 * (size - 1 - at) + 1)

    def ring_gather(self, block):
        size = self.size
        far = size // 2
        cut = block.shape[0] // 2
        pieces = {0: block}
        going_right, going_left = block, block
        for at in range(1, far):
            going_right = self.step(going_right, self.right)
            pieces[size - at] = going_right
            going_left = self.step(going_left, self.left)
            pieces[at] = going_left
        pieces[far] = jnp.concatenate(
            [self.step(going_right[:cut], self.right), self.step(going_left[cut:], self.left)]
        )
        return [pieces[at] for at in range(size)]

    def ring_scatter(self, take, low):
        size = self.size
        far = size // 2
        block = take(far)
        cut = block.shape[0] // 2
        from_left = self.step(block[:cut].astype(low), self.right)
        from_right = self.step(block[cut:].astype(low), self.left)
        for at in range(far - 1, 0, -1):
            to_right = take(at).astype(jnp.float32)
            to_left = take(size - at).astype(jnp.float32)
            if at == far - 1:
                to_right = jnp.concatenate(
                    [to_right[:cut] + from_left.astype(jnp.float32), to_right[cut:]]
                )
                to_left = jnp.concatenate(
                    [to_left[:cut], to_left[cut:] + from_right.astype(jnp.float32)]
                )
            else:
                to_right = to_right + from_left.astype(jnp.float32)
                to_left = to_left + from_right.astype(jnp.float32)
            from_left = self.step(to_right.astype(low), self.right)
            from_right = self.step(to_left.astype(low), self.left)
        return (
            take(0).astype(jnp.float32)
            + from_left.astype(jnp.float32)
            + from_right.astype(jnp.float32)
        )

    def gather_rows(self, shard, ring_first):
        size, halves = self.size, self.halves
        rows, columns = shard.shape
        whole = jnp.zeros((halves, 2, size, rows, columns), shard.dtype)
        zero = jnp.int32(0)
        if ring_first:
            pieces = self.ring_gather(shard)
            for at in range(size):
                whole = lax.dynamic_update_slice(
                    whole,
                    pieces[at][None, None, None],
                    (self.half, self.core, self.wide_of(at), zero, zero),
                )
            mine = lax.dynamic_slice(
                whole, (self.half, self.core, zero, zero, zero), (1, 1, size, rows, columns)
            )
            whole = lax.dynamic_update_slice(
                whole, self.swap_half(mine), (1 - self.half, self.core, zero, zero, zero)
            )
        else:
            other = self.swap_half(shard)
            pair = jnp.where(
                self.half == 0, jnp.stack([shard, other]), jnp.stack([other, shard])
            )
            pieces = self.ring_gather(pair)
            for at in range(size):
                whole = lax.dynamic_update_slice(
                    whole,
                    pieces[at][:, None, None],
                    (zero, self.core, self.wide_of(at), zero, zero),
                )
        mine = lax.dynamic_slice(
            whole, (zero, self.core, zero, zero, zero), (halves, 1, size, rows, columns)
        )
        whole = lax.dynamic_update_slice(
            whole, self.swap_core(mine), (zero, 1 - self.core, zero, zero, zero)
        )
        return whole.reshape(halves * 2 * size * rows, columns)

    def reduce_rows(self, array, half_first, low):
        size, halves = self.size, self.halves
        rows = array.shape[0] // (halves * 2 * size)
        columns = array.shape[1]
        split = array.reshape(halves, 2, size, rows, columns)

        def pick(value, at, axis):
            return lax.dynamic_index_in_dim(value, at, axis, keepdims=False)

        def plus(one, two):
            return one.astype(jnp.float32) + two.astype(jnp.float32)

        chip = plus(
            pick(split, self.core, 1), self.swap_core(pick(split, 1 - self.core, 1).astype(low))
        ).astype(low)
        if half_first:
            pair = plus(
                pick(chip, self.half, 0), self.swap_half(pick(chip, 1 - self.half, 0))
            ).astype(low)
            return self.ring_scatter(lambda at: pick(pair, self.wide_of(at), 0), low)
        both = self.ring_scatter(lambda at: pick(chip, self.wide_of(at), 1), low)
        return plus(
            pick(both, self.half, 0), self.swap_half(pick(both, 1 - self.half, 0).astype(low))
        )

    def total(self, value):
        value = value + self.swap_core(value)
        value = value + self.swap_half(value)
        bit = 1
        while bit < self.size:
            value = value + self.flip(value, bit)
            bit *= 2
        return value


def fetch_layer(net, w_qkv, w_out, w_fc, w_proj, layer_at):
    return (
        net.gather_rows(w_qkv[layer_at].astype(jnp.bfloat16), True),
        net.gather_rows(w_out[layer_at].astype(jnp.bfloat16), False),
        net.gather_rows(w_fc[layer_at].astype(jnp.bfloat16), True),
        net.gather_rows(w_proj[layer_at].astype(jnp.bfloat16), False),
    )


def reduce_layer(net, grad_wqkv, grad_wout, grad_wfc, grad_wproj):
    low = jnp.bfloat16
    return (
        net.reduce_rows(grad_wqkv, True, low),
        net.reduce_rows(grad_wout, False, low),
        net.reduce_rows(grad_wfc, True, low),
        net.reduce_rows(grad_wproj, False, low),
    )


def layer_norm(values, gain, shift):
    center = values - jnp.mean(values, axis=-1, keepdims=True)
    spread = jnp.mean(center * center, axis=-1, keepdims=True)
    return center * lax.rsqrt(spread + 1e-05) * gain + shift


def gelu_tanh(values):
    return jax.nn.gelu(values, approximate=True)


def attention_mask(seq_length):
    positions = jnp.arange(LEN)
    return (positions[None, :] <= positions[:, None]) & (positions[None, :] < seq_length)


def attention_scores(query_rows, key_rows, allowed):
    scores = (
        jnp.einsum("qhd,khd->hqk", query_rows, key_rows, preferred_element_type=jnp.float32) * 0.125
    )
    return jnp.where(allowed[None], scores, -1e30)


def layer_forward(stream, weights, vector, allowed):
    w_qkv, w_out, w_fc, w_proj = weights
    normed_low = layer_norm(stream, vector[0:D], vector[D : 2 * D]).astype(jnp.bfloat16)
    qkv_bias = jnp.concatenate(
        [vector[4 * D : 5 * D], jnp.zeros((D,), jnp.float32), vector[5 * D : 6 * D]]
    )
    projected = (jnp.dot(normed_low, w_qkv, preferred_element_type=jnp.float32) + qkv_bias).astype(
        jnp.bfloat16
    )
    heads_view = projected.reshape(LEN, 3, HEADS, HD)
    scores = attention_scores(heads_view[:, 0], heads_view[:, 1], allowed)
    row_max = jnp.max(scores, axis=-1, keepdims=True)
    log_total = row_max + jnp.log(jnp.sum(jnp.exp(scores - row_max), axis=-1, keepdims=True))
    attn_probs = jnp.exp(scores - log_total).astype(jnp.bfloat16)
    mixed_low = jnp.einsum(
        "hqk,khd->qhd", attn_probs, heads_view[:, 2], preferred_element_type=jnp.float32
    )
    mixed_low = mixed_low.reshape(LEN, D).astype(jnp.bfloat16)
    stream_mid = (
        stream
        + jnp.dot(mixed_low, w_out, preferred_element_type=jnp.float32)
        + vector[6 * D : 7 * D]
    )
    normed_two = layer_norm(stream_mid, vector[2 * D : 3 * D], vector[3 * D : 4 * D]).astype(
        jnp.bfloat16
    )
    hidden_pre = (
        jnp.dot(normed_two, w_fc, preferred_element_type=jnp.float32) + vector[8 * D : 8 * D + FF]
    )
    hidden_low = gelu_tanh(hidden_pre).astype(jnp.bfloat16)
    stream_out = (
        stream_mid
        + jnp.dot(hidden_low, w_proj, preferred_element_type=jnp.float32)
        + vector[7 * D : 8 * D]
    )
    return (
        stream_out,
        (
            stream,
            normed_low,
            projected,
            log_total,
            mixed_low,
            stream_mid,
            normed_two,
            hidden_pre,
            hidden_low,
        ),
    )


def layer_backward(grad_out, saved_acts, weights, vector, allowed):
    (
        stream,
        normed_low,
        projected,
        log_total,
        mixed_low,
        stream_mid,
        normed_two,
        hidden_pre,
        hidden_low,
    ) = saved_acts
    w_qkv, w_out, w_fc, w_proj = weights
    branch_low = grad_out.astype(jnp.bfloat16)
    grad_wproj = jnp.dot(hidden_low.T, branch_low, preferred_element_type=jnp.bfloat16)
    grad_hidden = jnp.dot(branch_low, w_proj.T, preferred_element_type=jnp.float32)
    pre_low = jax.vjp(gelu_tanh, hidden_pre)[1](grad_hidden)[0].astype(jnp.bfloat16)
    grad_wfc = jnp.dot(normed_two.T, pre_low, preferred_element_type=jnp.bfloat16)
    grad_normed_two = jnp.dot(pre_low, w_fc.T, preferred_element_type=jnp.float32)
    grad_mid, grad_gain_two, grad_shift_two = jax.vjp(
        layer_norm, stream_mid, vector[2 * D : 3 * D], vector[3 * D : 4 * D]
    )[1](grad_normed_two)
    grad_mid = grad_mid + grad_out
    attn_low = grad_mid.astype(jnp.bfloat16)
    grad_wout = jnp.dot(mixed_low.T, attn_low, preferred_element_type=jnp.bfloat16)
    grad_mixed = (
        jnp.dot(attn_low, w_out.T, preferred_element_type=jnp.float32)
        .astype(jnp.bfloat16)
        .reshape(LEN, HEADS, HD)
    )
    heads_view = projected.reshape(LEN, 3, HEADS, HD)
    query_rows = heads_view[:, 0]
    key_rows = heads_view[:, 1]
    value_rows = heads_view[:, 2]
    attn_probs = jnp.exp(attention_scores(query_rows, key_rows, allowed) - log_total)
    grad_probs = jnp.einsum(
        "qhd,khd->hqk", grad_mixed, value_rows, preferred_element_type=jnp.float32
    )
    grad_values = jnp.einsum(
        "hqk,qhd->khd",
        attn_probs.astype(jnp.bfloat16),
        grad_mixed,
        preferred_element_type=jnp.float32,
    )
    row_dot = jnp.sum(grad_probs * attn_probs, axis=-1, keepdims=True)
    scores_low = (attn_probs * (grad_probs - row_dot)).astype(jnp.bfloat16)
    grad_queries = (
        jnp.einsum("hqk,khd->qhd", scores_low, key_rows, preferred_element_type=jnp.float32) * 0.125
    )
    grad_keys = (
        jnp.einsum("hqk,qhd->khd", scores_low, query_rows, preferred_element_type=jnp.float32)
        * 0.125
    )
    qkv_low = (
        jnp.stack([grad_queries, grad_keys, grad_values], axis=1)
        .reshape(LEN, 3 * D)
        .astype(jnp.bfloat16)
    )
    grad_wqkv = jnp.dot(normed_low.T, qkv_low, preferred_element_type=jnp.bfloat16)
    grad_normed = jnp.dot(qkv_low, w_qkv.T, preferred_element_type=jnp.float32)
    grad_input, grad_gain_one, grad_shift_one = jax.vjp(
        layer_norm, stream, vector[0:D], vector[D : 2 * D]
    )[1](grad_normed)
    bias_qkv = jnp.sum(qkv_low.astype(jnp.float32), axis=0)
    grad_vector = jnp.concatenate(
        [
            grad_gain_one,
            grad_shift_one,
            grad_gain_two,
            grad_shift_two,
            bias_qkv[0:D],
            bias_qkv[2 * D : 3 * D],
            jnp.sum(attn_low.astype(jnp.float32), axis=0),
            jnp.sum(branch_low.astype(jnp.float32), axis=0),
            jnp.sum(pre_low.astype(jnp.float32), axis=0),
        ]
    )
    return (grad_input + grad_mid, (grad_wqkv, grad_wout, grad_wfc, grad_wproj), grad_vector)


def combine_stats(earlier, later):
    max_one, total_one, target_one = earlier
    max_two, total_two, target_two = later
    joint_max = jnp.maximum(max_one, max_two)
    joint_total = total_one * jnp.exp(max_one - joint_max) + total_two * jnp.exp(
        max_two - joint_max
    )
    return (joint_max, joint_total, target_one + target_two)


def adamw(weight, moment_one, moment_two, gradient, step_rate, decay_rate, step_float):
    one_new = 0.5 * moment_one + 0.5 * gradient
    two_new = 0.5 * moment_two + 0.5 * gradient * gradient
    fix_scale = 1.0 - jnp.power(0.5, step_float)
    update = one_new / fix_scale / (jnp.sqrt(two_new / fix_scale) + 1e-08)
    return (weight - step_rate * (update + decay_rate * weight), one_new, two_new)


def on_device(
    token_ids,
    seq_lengths,
    loss_slots,
    target_ids,
    step_count,
    w_qkv,
    w_out,
    w_fc,
    w_proj,
    vectors,
    pos_table,
    embed_table,
    mom_qkv,
    mom_out,
    mom_fc,
    mom_proj,
    mom_vectors,
    mom_pos,
    mom_embed,
    sec_qkv,
    sec_out,
    sec_fc,
    sec_proj,
    sec_vectors,
    sec_pos,
    sec_embed,
):
    per_layer = 8 * D + FF
    net = Net()
    size, halves = net.size, net.halves
    same_core = halves * size
    devices = 2 * same_core
    low = jnp.bfloat16
    near = LEN * 9 // 16
    rest = LEN - near
    slots = loss_slots.shape[0]

    numbers = jnp.concatenate([token_ids, loss_slots, target_ids, seq_lengths])
    numbers = net.ring_gather(jnp.stack([numbers, net.swap_half(numbers)], axis=1))
    numbers = jnp.stack(numbers).transpose(2, 0, 1)
    group_tokens = numbers[:, :, :LEN]
    group_slots = numbers[:, :, LEN : LEN + slots].reshape(same_core * slots)
    group_targets = numbers[:, :, LEN + slots : LEN + 2 * slots].reshape(same_core * slots)
    core_total = jnp.sum(numbers[:, :, LEN + 2 * slots :].astype(jnp.float32))
    token_total = core_total + net.swap_core(core_total[None])[0]

    own_rows = embed_table.shape[0]
    table_own = embed_table.astype(low)
    table_low = jnp.concatenate([table_own, net.swap_core(table_own)])
    chip_rows = 2 * own_rows
    own_start = net.device * own_rows
    other_start = (net.device + (1 - 2 * net.core) * size) * own_rows

    def locate(ids):
        mine = ids - own_start
        other = ids - other_start
        return jnp.where(
            (mine >= 0) & (mine < own_rows),
            mine,
            jnp.where((other >= 0) & (other < own_rows), other + own_rows, -1),
        )

    def one_hot(ids):
        return (ids[:, None] == jnp.arange(chip_rows)[None, :]).astype(low)

    local_tokens = locate(group_tokens)

    def look_up(ids):
        return jnp.dot(
            one_hot(ids.reshape(-1)), table_low, preferred_element_type=jnp.float32
        ).astype(low)

    shared = pos_table.shape[0]
    vector_rows = -(-vectors.shape[0] // D)
    padded = jnp.pad(vectors, (0, vector_rows * D - vectors.shape[0])).reshape(vector_rows, D)
    small_low = net.gather_rows(jnp.concatenate([pos_table, padded]).astype(low), False)
    small_low = small_low.reshape(devices, shared + vector_rows, D)
    pos_low = small_low[:, :shared].reshape(devices * shared, D)
    vector_all = (
        small_low[:, shared:]
        .reshape(devices, vector_rows * D)[:, : vectors.shape[0]]
        .reshape(-1)
        .astype(jnp.float32)
    )

    near_other = look_up(local_tokens[1, :, :near])
    near_swapped = net.swap_half(near_other)
    rest_both = look_up(local_tokens[:, :, near:].transpose(1, 0, 2)).reshape(
        size, halves, rest, D
    )
    near_own = (look_up(local_tokens[0, :, :near]) + near_swapped).reshape(size, near, D)
    near_rows = net.ring_scatter(lambda at: near_own[at], low)
    rest_sum = net.ring_scatter(lambda at: rest_both[at], low)
    rest_rows = rest_sum[0] + net.swap_half(rest_sum[1].astype(low)).astype(jnp.float32)
    stream = jnp.concatenate([near_rows, rest_rows]) + pos_low[:LEN].astype(jnp.float32)

    allowed = attention_mask(seq_lengths[0])
    kept_weights = []
    saved_list = []
    for layer_at in range(LAYERS):
        weights = fetch_layer(net, w_qkv, w_out, w_fc, w_proj, layer_at)
        kept_weights.append(weights)
        stream, saved_acts = layer_forward(
            stream, weights, vector_all[layer_at * per_layer : (layer_at + 1) * per_layer], allowed
        )
        saved_list.append(saved_acts)
    tail_start = LAYERS * per_layer
    final_norm, final_pull = jax.vjp(
        layer_norm,
        stream,
        vector_all[tail_start : tail_start + D],
        vector_all[tail_start + D : tail_start + 2 * D],
    )
    slot_rows = jnp.maximum(loss_slots, 0)
    own_picked = final_norm[slot_rows].astype(low)
    group_rows = net.ring_gather(jnp.stack([own_picked, net.swap_half(own_picked)]))
    group_rows = jnp.stack(group_rows, axis=1).reshape(same_core * slots, D)
    logits = jnp.dot(group_rows, table_low.T, preferred_element_type=jnp.float32)
    target_onehot = locate(group_targets)[:, None] == jnp.arange(chip_rows)[None, :]
    row_max = jnp.max(logits, axis=-1)
    row_total = jnp.sum(jnp.exp(logits - row_max[:, None]), axis=-1)
    target_logit = jnp.sum(jnp.where(target_onehot, logits, 0.0), axis=-1)
    half_of = jnp.arange(halves)[:, None]
    wide_index = jnp.arange(size)[None, :]
    place_of = jnp.where(wide_index % 2 == 0, wide_index // 2, size - 1 - (wide_index - 1) // 2)
    to_device = ((half_of ^ net.half) * size + (place_of - net.place) % size).reshape(-1)
    offsets = (net.place + wide_index) % size
    wide_there = jnp.where(offsets < size // 2, 2 * offsets, 2 * (size - 1 - offsets) + 1)
    from_device = ((half_of ^ net.half) * size + wide_there).reshape(-1)
    stats = jnp.stack([row_max, row_total, target_logit], axis=-1)
    stats = jnp.take(stats.reshape(same_core, slots * 3), to_device, axis=0)
    stats = stats.reshape(same_core * slots, 3).T

    def merged(stats, there):
        return jnp.stack(combine_stats((stats[0], stats[1], stats[2]), (there[0], there[1], there[2])))

    stats = merged(stats, net.swap_half(stats))
    bit = 1
    while bit < size:
        stats = merged(stats, net.flip(stats, bit))
        bit *= 2
    stats = jnp.stack([stats[0] + jnp.log(stats[1]), stats[2]]).reshape(2, same_core, slots)
    stats = jnp.take(stats, from_device, axis=1).reshape(2, same_core * slots)
    log_total, merged_target = stats[0], stats[1]
    group_used = (group_slots >= 0).astype(jnp.float32)
    own_loss = jnp.sum(((log_total - merged_target) * group_used)[:slots])
    grad_logits = (
        (jnp.exp(logits - log_total[:, None]) - target_onehot.astype(jnp.float32))
        * (group_used / token_total)[:, None]
    ).astype(low)
    grad_rows = jnp.dot(grad_logits, table_low, preferred_element_type=jnp.float32)
    grad_rows = grad_rows.reshape(halves, size, slots, D)
    cut = D // 2
    pair = grad_rows[0, :, :, :cut] + net.swap_half(grad_rows[1, :, :, :cut])
    grad_one = net.ring_scatter(lambda at: pair[at], jnp.float32)
    both = net.ring_scatter(lambda at: grad_rows[:, at, :, cut:], jnp.float32)
    grad_two = both[0] + net.swap_half(both[1])
    grad_rows = jnp.concatenate([grad_one, grad_two], axis=1)
    grad_final = jnp.zeros((LEN, D), jnp.float32).at[slot_rows].add(grad_rows)
    grad_stream, grad_gain_final, grad_shift_final = final_pull(grad_final)
    layer_shards = []
    vector_grads = []
    for layer_at in reversed(range(LAYERS)):
        grad_stream, full_grads, grad_vector = layer_backward(
            grad_stream,
            saved_list[layer_at],
            kept_weights[layer_at],
            vector_all[layer_at * per_layer : (layer_at + 1) * per_layer],
            allowed,
        )
        grad_a, grad_b, grad_c, grad_d = full_grads
        layer_shards.insert(0, reduce_layer(net, grad_a, grad_b, grad_c, grad_d))
        vector_grads.insert(0, grad_vector)
    grad_low = grad_stream.astype(low)
    grad_near, grad_rest = grad_low[:near], grad_low[near:]
    near_own = jnp.stack(net.ring_gather(grad_near))
    near_other = net.swap_half(near_own)
    rest_all = jnp.stack(net.ring_gather(jnp.stack([grad_rest, net.swap_half(grad_rest)])))

    def spread(ids, rows):
        return jnp.dot(one_hot(ids.reshape(-1)).T, rows, preferred_element_type=jnp.float32)

    grad_table = jnp.dot(grad_logits.T, group_rows, preferred_element_type=jnp.float32)
    grad_table = grad_table + spread(local_tokens[0, :, :near], near_own.reshape(-1, D))
    grad_table = grad_table + spread(
        local_tokens[:, :, near:].transpose(1, 0, 2), rest_all.reshape(-1, D)
    )
    grad_table = grad_table + spread(local_tokens[1, :, :near], near_other.reshape(-1, D))
    table_shard = grad_table[:own_rows] + net.swap_core(grad_table[own_rows:])
    grad_pos = jnp.concatenate(
        [
            jnp.sum(near_own.astype(jnp.float32), axis=0)
            + jnp.sum(near_other.astype(jnp.float32), axis=0),
            jnp.sum(rest_all.astype(jnp.float32), axis=(0, 1)),
        ]
    )
    grad_pos = jnp.pad(grad_pos, ((0, POS - LEN), (0, 0)))
    other_device = net.device + (1 - 2 * net.core) * size
    pos_shard = lax.dynamic_slice_in_dim(grad_pos, net.device * shared, shared) + net.swap_core(
        lax.dynamic_slice_in_dim(grad_pos, other_device * shared, shared)
    )
    grad_small = jnp.concatenate(vector_grads + [grad_gain_final, grad_shift_final])
    small_shard = net.reduce_rows(
        grad_small.reshape(devices * 2, -1), False, jnp.float32
    ).reshape(-1)
    qkv_shard = jnp.stack([member[0] for member in layer_shards])
    out_shard = jnp.stack([member[1] for member in layer_shards])
    fc_shard = jnp.stack([member[2] for member in layer_shards])
    proj_shard = jnp.stack([member[3] for member in layer_shards])
    shards = (qkv_shard, out_shard, fc_shard, proj_shard, small_shard, pos_shard, table_shard)
    squares = jnp.sum(jnp.stack([jnp.sum(member * member) for member in shards]))
    loss_total, square_total = net.total(jnp.stack([own_loss, squares]))
    loss_value = loss_total / token_total
    grad_norm = jnp.sqrt(square_total)
    factor = CLIP_LIMIT / jnp.maximum(grad_norm, CLIP_LIMIT)
    step_float = step_count.astype(jnp.float32)
    params = (w_qkv, w_out, w_fc, w_proj, vectors, pos_table, embed_table)
    moments_one = (mom_qkv, mom_out, mom_fc, mom_proj, mom_vectors, mom_pos, mom_embed)
    moments_two = (sec_qkv, sec_out, sec_fc, sec_proj, sec_vectors, sec_pos, sec_embed)
    step_rates = (
        RATE_MATRIX,
        RATE_MATRIX,
        RATE_MATRIX,
        RATE_MATRIX,
        RATE_VECTOR,
        RATE_MATRIX,
        RATE_MATRIX,
    )
    decay_rates = (
        DECAY_MATRIX,
        DECAY_MATRIX,
        DECAY_MATRIX,
        DECAY_MATRIX,
        0.0,
        DECAY_MATRIX,
        DECAY_MATRIX,
    )
    results = [
        adamw(
            params[where_at],
            moments_one[where_at],
            moments_two[where_at],
            shards[where_at] * factor,
            step_rates[where_at],
            decay_rates[where_at],
            step_float,
        )
        for where_at in range(7)
    ]
    return (
        loss_value,
        grad_norm,
        results[0][0],
        results[1][0],
        results[2][0],
        results[3][0],
        results[4][0],
        results[5][0],
        results[6][0],
        results[0][1],
        results[1][1],
        results[2][1],
        results[3][1],
        results[4][1],
        results[5][1],
        results[6][1],
        results[0][2],
        results[1][2],
        results[2][2],
        results[3][2],
        results[4][2],
        results[5][2],
        results[6][2],
    )


def solution(mesh):
    return jax.shard_map(
        on_device,
        mesh=mesh,
        in_specs=(
            P(("narrow", "wide")),
            P(("narrow", "wide")),
            P(("narrow", "wide")),
            P(("narrow", "wide")),
            P(),
            P(None, ("narrow", "wide"), None),
            P(None, ("narrow", "wide"), None),
            P(None, ("narrow", "wide"), None),
            P(None, ("narrow", "wide"), None),
            P(("narrow", "wide")),
            P(("narrow", "wide"), None),
            P(("narrow", "wide"), None),
            P(None, ("narrow", "wide"), None),
            P(None, ("narrow", "wide"), None),
            P(None, ("narrow", "wide"), None),
            P(None, ("narrow", "wide"), None),
            P(("narrow", "wide")),
            P(("narrow", "wide"), None),
            P(("narrow", "wide"), None),
            P(None, ("narrow", "wide"), None),
            P(None, ("narrow", "wide"), None),
            P(None, ("narrow", "wide"), None),
            P(None, ("narrow", "wide"), None),
            P(("narrow", "wide")),
            P(("narrow", "wide"), None),
            P(("narrow", "wide"), None),
        ),
        out_specs=(
            P(),
            P(),
            P(None, ("narrow", "wide"), None),
            P(None, ("narrow", "wide"), None),
            P(None, ("narrow", "wide"), None),
            P(None, ("narrow", "wide"), None),
            P(("narrow", "wide")),
            P(("narrow", "wide"), None),
            P(("narrow", "wide"), None),
            P(None, ("narrow", "wide"), None),
            P(None, ("narrow", "wide"), None),
            P(None, ("narrow", "wide"), None),
            P(None, ("narrow", "wide"), None),
            P(("narrow", "wide")),
            P(("narrow", "wide"), None),
            P(("narrow", "wide"), None),
            P(None, ("narrow", "wide"), None),
            P(None, ("narrow", "wide"), None),
            P(None, ("narrow", "wide"), None),
            P(None, ("narrow", "wide"), None),
            P(("narrow", "wide")),
            P(("narrow", "wide"), None),
            P(("narrow", "wide"), None),
        ),
        check_vma=False,
    )
```

```python
import functools

import jax
import jax.numpy as jnp
from jax import lax
from jax.experimental import pallas as pl
from jax.experimental.pallas import tpu as pltpu
from jax.sharding import PartitionSpec as P

D = 1024
HEADS = 16
HD = 64
FF = 4096
POS = 1024
LAYERS = 2
LEN = 512
LOSS_DEV = 32


CLIP_LIMIT = 0.002
RATE_MATRIX = 0.03
RATE_VECTOR = 0.3
DECAY_MATRIX = 0.1


class Net:
    def __init__(self):
        self.narrow_at = lax.axis_index("narrow")
        self.wide_at = lax.axis_index("wide")
        self.narrow_size = lax.axis_size("narrow")
        self.size = lax.axis_size("wide")
        size = self.size
        self.core = self.narrow_at % 2
        self.half = self.narrow_at // 2
        self.halves = self.narrow_size // 2
        self.place = jnp.where(
            self.wide_at % 2 == 0, self.wide_at // 2, size - 1 - (self.wide_at - 1) // 2
        )
        self.device = self.narrow_at * size + self.wide_at
        order = list(range(0, size, 2)) + list(range(size - 1, 0, -2))
        pairs = [(n, w) for n in range(self.narrow_size) for w in range(size)]
        self.core_pairs = [(n * size + w, (n ^ 1) * size + w) for n, w in pairs]
        self.half_pairs = [(n * size + w, (n ^ 2) * size + w) for n, w in pairs]
        self.right = [
            (n * size + order[i], n * size + order[(i + 1) % size])
            for n in range(self.narrow_size)
            for i in range(size)
        ]
        self.left = [(later, earlier) for earlier, later in self.right]

    def step(self, array, pairs):
        return lax.ppermute(array, ("narrow", "wide"), pairs)

    def swap_core(self, array):
        return self.step(array, self.core_pairs)

    def swap_half(self, array):
        return self.step(array, self.half_pairs)

    def flip(self, array, bit):
        size = self.size
        pairs = [
            (n * size + w, n * size + (w ^ bit))
            for n in range(self.narrow_size)
            for w in range(size)
        ]
        return self.step(array, pairs)

    def wide_of(self, offset):
        size = self.size
        at = lax.rem(self.place + offset, size)
        return jnp.where(at < size // 2, 2 * at, 2 * (size - 1 - at) + 1)

    def ring_gather(self, block):
        size = self.size
        far = size // 2
        cut = block.shape[0] // 2
        pieces = {0: block}
        going_right, going_left = block, block
        for at in range(1, far):
            going_right = self.step(going_right, self.right)
            pieces[size - at] = going_right
            going_left = self.step(going_left, self.left)
            pieces[at] = going_left
        pieces[far] = jnp.concatenate(
            [self.step(going_right[:cut], self.right), self.step(going_left[cut:], self.left)]
        )
        return [pieces[at] for at in range(size)]

    def ring_scatter(self, take, low):
        size = self.size
        far = size // 2
        block = take(far)
        cut = block.shape[0] // 2
        from_left = self.step(block[:cut].astype(low), self.right)
        from_right = self.step(block[cut:].astype(low), self.left)
        for at in range(far - 1, 0, -1):
            to_right = take(at).astype(jnp.float32)
            to_left = take(size - at).astype(jnp.float32)
            if at == far - 1:
                to_right = jnp.concatenate(
                    [to_right[:cut] + from_left.astype(jnp.float32), to_right[cut:]]
                )
                to_left = jnp.concatenate(
                    [to_left[:cut], to_left[cut:] + from_right.astype(jnp.float32)]
                )
            else:
                to_right = to_right + from_left.astype(jnp.float32)
                to_left = to_left + from_right.astype(jnp.float32)
            from_left = self.step(to_right.astype(low), self.right)
            from_right = self.step(to_left.astype(low), self.left)
        return (
            take(0).astype(jnp.float32)
            + from_left.astype(jnp.float32)
            + from_right.astype(jnp.float32)
        )

    def reduce_rows(self, array, half_first, low):
        size, halves = self.size, self.halves
        rows = array.shape[0] // (halves * 2 * size)
        columns = array.shape[1]
        split = array.reshape(halves, 2, size, rows, columns)

        def pick(value, at, axis):
            return lax.dynamic_index_in_dim(value, at, axis, keepdims=False)

        def plus(one, two):
            return one.astype(jnp.float32) + two.astype(jnp.float32)

        chip = plus(
            pick(split, self.core, 1), self.swap_core(pick(split, 1 - self.core, 1).astype(low))
        ).astype(low)
        if half_first:
            pair = plus(
                pick(chip, self.half, 0), self.swap_half(pick(chip, 1 - self.half, 0))
            ).astype(low)
            return self.ring_scatter(lambda at: pick(pair, self.wide_of(at), 0), low)
        both = self.ring_scatter(lambda at: pick(chip, self.wide_of(at), 1), low)
        return plus(
            pick(both, self.half, 0), self.swap_half(pick(both, 1 - self.half, 0).astype(low))
        )

    def total(self, value):
        value = value + self.swap_core(value)
        value = value + self.swap_half(value)
        bit = 1
        while bit < self.size:
            value = value + self.flip(value, bit)
            bit *= 2
        return value


MESH = pl.DeviceIdType.MESH


class Spot:
    def __init__(self, size):
        self.size = size
        narrow, wide = lax.axis_index("narrow"), lax.axis_index("wide")
        odd = lax.rem(wide, 2)
        self.core, self.half = lax.rem(narrow, 2), lax.div(narrow, 2)
        self.wide = wide
        self.place = (1 - odd) * lax.div(wide, 2) + odd * (size - 1 - lax.div(wide, 2))
        self.to_core = (narrow + 1 - 2 * self.core, wide)
        self.to_half = (narrow + 2 - 4 * self.half, wide)
        self.right = (narrow, self.wide_of(1))
        self.left = (narrow, self.wide_of(size - 1))

    def wide_of(self, offset):
        at = lax.rem(self.place + offset, self.size)
        late = lax.div(at, self.size // 2)
        return (1 - late) * 2 * at + late * (2 * (self.size - 1 - at) + 1)

    def index(self, turned, other_core, offset):
        half = self.half + turned * (1 - 2 * self.half)
        core = self.core + other_core * (1 - 2 * self.core)
        return (2 * half + core) * self.size + self.wide_of(offset)

    def meet(self, with_core):
        barrier = pltpu.get_barrier_semaphore()
        peers = [self.to_half, self.right, self.left] + ([self.to_core] if with_core else [])
        for peer in peers:
            pl.semaphore_signal(barrier, inc=1, device_id=peer, device_id_type=MESH)
        pl.semaphore_wait(barrier, len(peers))


def cut_of(rows):
    return rows // 2 if rows % 32 == 0 else rows


def gather_body(size, ring_first, across, *refs):
    count = len(ring_first)
    shards, wholes = refs[:count], refs[count : 2 * count]
    ring_sem, half_sem, core_sem, send_sem, local_sem = refs[2 * count :]
    spot = Spot(size)
    far = size // 2

    def index(turned, offset, toward=None):
        if across:
            return spot.index(turned, 0, offset % size)
        if toward == "half":
            turned = 1 - turned
        offset = offset + {"right": -1, "left": 1}.get(toward, 0)
        return turned * size + offset % size

    def send(at, source, turned, offset, toward, sem, rows=None):
        target = wholes[at].at[index(turned, offset, toward)]
        if rows is not None:
            source, target = source.at[rows], target.at[rows]
        device = {
            "half": spot.to_half,
            "right": spot.right,
            "left": spot.left,
            "core": spot.to_core,
        }[toward]
        pltpu.make_async_remote_copy(
            src_ref=source,
            dst_ref=target,
            send_sem=send_sem.at[at],
            recv_sem=sem,
            device_id=device,
            device_id_type=MESH,
        ).start()

    def landed(region, sem):
        pltpu.make_async_copy(region, region, sem).wait()

    def piece(at, turned, offset):
        return wholes[at].at[index(turned, offset)]

    def on_core(at, source, turned, offset):
        if across:
            send(at, source, turned, offset, "core", core_sem.at[at])

    def on_ring(at, turned, source, offset, way, step, rows=None):
        toward = ("right", "left")[way]
        send(at, source, turned, offset, toward, ring_sem.at[at, turned, way, step], rows)

    spot.meet(across)
    locals_ = []
    for at in range(count):
        copy = pltpu.make_async_copy(shards[at], piece(at, 0, 0), local_sem.at[at])
        copy.start()
        locals_.append(copy)
    for at in range(count):
        if not ring_first[at]:
            send(at, shards[at], 0, 0, "half", half_sem.at[at, 0])
    for at in range(count):
        if ring_first[at]:
            on_ring(at, 0, shards[at], 0, 0, 1)
            on_ring(at, 0, shards[at], 0, 1, 1)
            send(at, shards[at], 0, 0, "half", half_sem.at[at, 0])
    for at in range(count):
        on_core(at, shards[at], 0, 0)
    for at in range(count):
        if not ring_first[at]:
            landed(piece(at, 1, 0), half_sem.at[at, 0])
            for way in (0, 1):
                on_ring(at, 0, shards[at], 0, way, 1)
                on_ring(at, 1, piece(at, 1, 0), 0, way, 1)
            on_core(at, piece(at, 1, 0), 1, 0)

    def turned_arrivals(at, step):
        offsets = (0,) if step == 0 else (far,) if step == far else (-step, step)
        for offset in offsets:
            landed(piece(at, 1, offset), half_sem.at[at, offset % size])
            on_core(at, piece(at, 1, offset), 1, offset)

    for step in range(1, far + 1):
        for at in range(count):
            rows = shards[at].shape[0]
            cut = cut_of(rows)
            if ring_first[at]:
                if step < far:
                    for way in (0, 1):
                        offset = (-step, step)[way]
                        here = piece(at, 0, offset)
                        landed(here, ring_sem.at[at, 0, way, step])
                        if step < far - 1:
                            on_ring(at, 0, here, offset, way, step + 1)
                        elif way == 0:
                            on_ring(at, 0, here, offset, way, step + 1, pl.ds(0, cut))
                        elif cut < rows:
                            on_ring(at, 0, here, offset, way, step + 1, pl.ds(cut, rows - cut))
                        send(at, here, 0, offset, "half", half_sem.at[at, offset % size])
                        on_core(at, here, 0, offset)
                else:
                    here = piece(at, 0, far)
                    landed(here.at[pl.ds(0, cut)], ring_sem.at[at, 0, 0, step])
                    if cut < rows:
                        landed(here.at[pl.ds(cut, rows - cut)], ring_sem.at[at, 0, 1, step])
                    send(at, here, 0, far, "half", half_sem.at[at, far])
                    on_core(at, here, 0, far)
                turned_arrivals(at, step - 1)
            else:
                for way in (0, 1):
                    for turned in (0, 1):
                        if step == far and turned != way:
                            continue
                        offset = (-step, step)[way]
                        here = piece(at, turned, offset)
                        landed(here, ring_sem.at[at, turned, way, step])
                        if step < far - 1 or (step == far - 1 and turned == way):
                            on_ring(at, turned, here, offset, way, step + 1)
                        on_core(at, here, turned, offset)
    for at in range(count):
        if ring_first[at]:
            turned_arrivals(at, far)
    for at in range(count):
        locals_[at].wait()
        if across:
            landed(wholes[at].at[pl.ds(0, 2 * size)], core_sem.at[at])
        sent = 4 * size - 1 if across else 2 * size - 1
        landed(wholes[at].at[pl.ds(0, sent)], send_sem.at[at])


def gather_call(size, shards, ring_first, across, number):
    count = len(shards)
    total = (4 if across else 2) * size
    half_waits = size
    outs = [jax.ShapeDtypeStruct((total,) + a.shape, a.dtype) for a in shards]
    return pl.pallas_call(
        functools.partial(gather_body, size, ring_first, across),
        out_shape=outs,
        in_specs=[pl.BlockSpec(memory_space=pl.ANY)] * count,
        out_specs=[pl.BlockSpec(memory_space=pl.ANY)] * count,
        scratch_shapes=[
            pltpu.SemaphoreType.DMA((count, 2, 2, size // 2 + 1)),
            pltpu.SemaphoreType.DMA((count, half_waits)),
            pltpu.SemaphoreType.DMA((count,)),
            pltpu.SemaphoreType.DMA((count,)),
            pltpu.SemaphoreType.DMA((count,)),
        ],
        compiler_params=pltpu.CompilerParams(collective_id=number, has_side_effects=True),
    )(*shards)


def scatter_body(size, half_first, across, *refs):
    count = len(half_first)
    arrays, outs = refs[:count], refs[count : 2 * count]
    own, core_in, half_in, ring_in = (
        refs[(2 + part) * count : (3 + part) * count] for part in range(4)
    )
    local_sem, core_sem, half_sem, ring_sem, send_sem = refs[6 * count :]
    spot = Spot(size)
    far = size // 2
    slots = [far] + [o for at in range(far - 1, 0, -1) for o in (at, -at)] + [0]
    sent = []

    def landed(region, sem):
        pltpu.make_async_copy(region, region, sem).wait()

    def send(source, target, device, number, at, sem):
        copy = pltpu.make_async_remote_copy(
            src_ref=source,
            dst_ref=target,
            send_sem=send_sem.at[at, number],
            recv_sem=sem,
            device_id=device,
            device_id_type=MESH,
        )
        copy.start()
        sent.append(copy)

    def source_of(at, turned, other_core, offset):
        if across:
            return arrays[at].at[spot.index(turned, other_core, offset % size)]
        return arrays[at].at[turned * size + offset % size]

    def add(target, parts):
        rows, columns = target.shape
        width = 512 if columns % 512 == 0 else 256 if columns % 256 == 0 else 128

        def one(step, nothing):
            window = pl.ds(pl.multiple_of(step * width, width), width)
            total = parts[0][0][:, window].astype(jnp.float32)
            for part, first, last in parts[1:]:
                if first == 0 and last == rows:
                    total = total + part[:, window].astype(jnp.float32)
            target[:, window] = total.astype(target.dtype)
            for part, first, last in parts[1:]:
                if first != 0 or last != rows:
                    span = pl.ds(first, last - first)
                    target[span, window] = (
                        total[first:last] + part[span, window].astype(jnp.float32)
                    ).astype(target.dtype)
            return nothing

        lax.fori_loop(0, columns // width, one, 0)

    def ring_slot(way, step):
        return way * far + step - 1

    def base(at, turned, offset):
        k = offset % size
        rows = own[at].shape[1]
        here = own[at].at[turned * size + k]
        landed(here, local_sem.at[at, turned * size + k])
        parts = [(here, 0, rows)]
        if across:
            there = core_in[at].at[turned * size + k]
            landed(there, core_sem.at[at, turned * size + k])
            parts.append((there, 0, rows))
        return here, parts

    def ring_parts(at, turned, offset):
        parts = []
        rows = own[at].shape[1]
        cut = cut_of(rows)
        ways = (0, 1) if offset == 0 else (0,) if offset > 0 else (1,)
        for way in ways:
            step = far - abs(offset)
            slot = ring_slot(way, step)
            if half_first[at]:
                if step == 1:
                    first, last = (0, cut) if way == 0 else (cut, rows)
                else:
                    first, last = 0, rows
                if first == last:
                    continue
                region = ring_in[at].at[slot]
                span = region if (first, last) == (0, rows) else region.at[pl.ds(first, last - first)]
                landed(span, ring_sem.at[at, slot])
                parts.append((region, first, last))
            else:
                if step == 1 and turned != way:
                    continue
                region = ring_in[at].at[turned * 2 * far + slot]
                landed(region, ring_sem.at[at, turned * 2 * far + slot])
                parts.append((region, 0, rows))
        return parts

    def ring_send(at, turned, offset):
        here = own[at].at[turned * size + offset % size]
        rows = own[at].shape[1]
        cut = cut_of(rows)
        step = far - abs(offset) + 1
        if offset == far:
            if half_first[at]:
                spans = [(0, pl.ds(0, cut))] + ([(1, pl.ds(cut, rows - cut))] if cut < rows else [])
                for way, span in spans:
                    slot = ring_slot(way, 1)
                    send(
                        here.at[span],
                        ring_in[at].at[slot].at[span],
                        (spot.right, spot.left)[way],
                        slot,
                        at,
                        ring_sem.at[at, slot],
                    )
                return
            ways = (turned,)
        else:
            ways = (0,) if offset > 0 else (1,)
        for way in ways:
            slot = ring_slot(way, step) + (0 if half_first[at] else turned * 2 * far)
            send(
                here,
                ring_in[at].at[slot],
                (spot.right, spot.left)[way],
                slot,
                at,
                ring_sem.at[at, slot],
            )

    spot.meet(across)
    core_base = 4 * far + size
    for offset in slots:
        k = offset % size
        for turned in (1, 0):
            for at in range(count):
                if across:
                    send(
                        source_of(at, turned, 1, offset),
                        core_in[at].at[turned * size + k],
                        spot.to_core,
                        core_base + turned * size + k,
                        at,
                        core_sem.at[at, turned * size + k],
                    )
                pltpu.make_async_copy(
                    source_of(at, turned, 0, offset),
                    own[at].at[turned * size + k],
                    local_sem.at[at, turned * size + k],
                ).start()

    def turned_half(offset):
        for at in range(count):
            if half_first[at]:
                here, parts = base(at, 1, offset)
                k = offset % size
                if across:
                    add(here, parts)
                send(here, half_in[at].at[k], spot.to_half, 4 * far + k, at, half_sem.at[at, k])

    def straight(offset):
        for at in range(count):
            if half_first[at]:
                here, parts = base(at, 0, offset)
                k = offset % size
                landed(half_in[at].at[k], half_sem.at[at, k])
                parts.append((half_in[at].at[k], 0, own[at].shape[1]))
                parts += ring_parts(at, 0, offset) if offset != far else []
                if offset == 0:
                    add(outs[at], parts)
                else:
                    add(here, parts)
                    ring_send(at, 0, offset)

    def both(offset):
        for at in range(count):
            if not half_first[at]:
                for turned in (1, 0):
                    here, parts = base(at, turned, offset)
                    parts += ring_parts(at, turned, offset) if offset != far else []
                    if offset == 0 and turned == 0:
                        landed(half_in[at].at[0], half_sem.at[at, 0])
                        parts.append((half_in[at].at[0], 0, own[at].shape[1]))
                        add(outs[at], parts)
                        continue
                    if len(parts) > 1:
                        add(here, parts)
                    if offset == 0:
                        send(here, half_in[at].at[0], spot.to_half, 4 * far, at, half_sem.at[at, 0])
                    else:
                        ring_send(at, turned, offset)

    groups = [[far]] + [[at, -at] for at in range(far - 1, 0, -1)] + [[0]]
    for number, group in enumerate(groups):
        for offset in group:
            turned_half(offset)
        for offset in group:
            both(offset)
        if number > 0:
            for offset in groups[number - 1]:
                straight(offset)
    for offset in groups[-1]:
        straight(offset)
    for copy in sent:
        copy.wait_send()


def scatter_call(size, arrays, half_first, across, out_type, number):
    count = len(arrays)
    far = size // 2
    pieces = [a.shape[1:] for a in arrays]
    own = [pltpu.VMEM((2 * size,) + p, a.dtype) for p, a in zip(pieces, arrays)]
    core_in = [
        pltpu.VMEM((2 * size if across else 1,) + p, a.dtype) for p, a in zip(pieces, arrays)
    ]
    half_in = [
        pltpu.VMEM((size if first else 1,) + p, a.dtype)
        for p, a, first in zip(pieces, arrays, half_first)
    ]
    ring_in = [
        pltpu.VMEM((2 * far if first else 4 * far,) + p, a.dtype)
        for p, a, first in zip(pieces, arrays, half_first)
    ]
    return pl.pallas_call(
        functools.partial(scatter_body, size, half_first, across),
        out_shape=[jax.ShapeDtypeStruct(p, out_type) for p in pieces],
        in_specs=[pl.BlockSpec(memory_space=pl.ANY)] * count,
        out_specs=[pl.BlockSpec(memory_space=pltpu.VMEM)] * count,
        scratch_shapes=own
        + core_in
        + half_in
        + ring_in
        + [
            pltpu.SemaphoreType.DMA((count, 2 * size)),
            pltpu.SemaphoreType.DMA((count, 2 * size)),
            pltpu.SemaphoreType.DMA((count, size)),
            pltpu.SemaphoreType.DMA((count, 4 * far)),
            pltpu.SemaphoreType.DMA((count, 4 * far + 3 * size)),
        ],
        compiler_params=pltpu.CompilerParams(
            collective_id=number, has_side_effects=True, vmem_limit_bytes=60 * 1024 * 1024
        ),
    )(*arrays)


def layer_norm(values, gain, shift):
    center = values - jnp.mean(values, axis=-1, keepdims=True)
    spread = jnp.mean(center * center, axis=-1, keepdims=True)
    return center * lax.rsqrt(spread + 1e-05) * gain + shift


def gelu_tanh(values):
    return jax.nn.gelu(values, approximate=True)


def attention_mask(seq_length):
    positions = jnp.arange(LEN)
    return (positions[None, :] <= positions[:, None]) & (positions[None, :] < seq_length)


def attention_scores(query_rows, key_rows, allowed):
    scores = (
        jnp.einsum("qhd,khd->hqk", query_rows, key_rows, preferred_element_type=jnp.float32) * 0.125
    )
    return jnp.where(allowed[None], scores, -1e30)


def layer_forward(stream, weights, vector, allowed):
    w_qkv, w_out, w_fc, w_proj = weights
    normed_low = layer_norm(stream, vector[0:D], vector[D : 2 * D]).astype(jnp.bfloat16)
    qkv_bias = jnp.concatenate(
        [vector[4 * D : 5 * D], jnp.zeros((D,), jnp.float32), vector[5 * D : 6 * D]]
    )
    projected = (jnp.dot(normed_low, w_qkv, preferred_element_type=jnp.float32) + qkv_bias).astype(
        jnp.bfloat16
    )
    heads_view = projected.reshape(LEN, 3, HEADS, HD)
    scores = attention_scores(heads_view[:, 0], heads_view[:, 1], allowed)
    row_max = jnp.max(scores, axis=-1, keepdims=True)
    log_total = row_max + jnp.log(jnp.sum(jnp.exp(scores - row_max), axis=-1, keepdims=True))
    attn_probs = jnp.exp(scores - log_total).astype(jnp.bfloat16)
    mixed_low = jnp.einsum(
        "hqk,khd->qhd", attn_probs, heads_view[:, 2], preferred_element_type=jnp.float32
    )
    mixed_low = mixed_low.reshape(LEN, D).astype(jnp.bfloat16)
    stream_mid = (
        stream
        + jnp.dot(mixed_low, w_out, preferred_element_type=jnp.float32)
        + vector[6 * D : 7 * D]
    )
    normed_two = layer_norm(stream_mid, vector[2 * D : 3 * D], vector[3 * D : 4 * D]).astype(
        jnp.bfloat16
    )
    hidden_pre = (
        jnp.dot(normed_two, w_fc, preferred_element_type=jnp.float32) + vector[8 * D : 8 * D + FF]
    )
    hidden_low = gelu_tanh(hidden_pre).astype(jnp.bfloat16)
    stream_out = (
        stream_mid
        + jnp.dot(hidden_low, w_proj, preferred_element_type=jnp.float32)
        + vector[7 * D : 8 * D]
    )
    return (
        stream_out,
        (
            stream,
            normed_low,
            projected,
            log_total,
            mixed_low,
            stream_mid,
            normed_two,
            hidden_pre,
            hidden_low,
        ),
    )


def layer_backward(grad_out, saved_acts, weights, vector, allowed):
    (
        stream,
        normed_low,
        projected,
        log_total,
        mixed_low,
        stream_mid,
        normed_two,
        hidden_pre,
        hidden_low,
    ) = saved_acts
    w_qkv, w_out, w_fc, w_proj = weights
    branch_low = grad_out.astype(jnp.bfloat16)
    grad_wproj = jnp.dot(hidden_low.T, branch_low, preferred_element_type=jnp.bfloat16)
    grad_hidden = jnp.dot(branch_low, w_proj.T, preferred_element_type=jnp.float32)
    pre_low = jax.vjp(gelu_tanh, hidden_pre)[1](grad_hidden)[0].astype(jnp.bfloat16)
    grad_wfc = jnp.dot(normed_two.T, pre_low, preferred_element_type=jnp.bfloat16)
    grad_normed_two = jnp.dot(pre_low, w_fc.T, preferred_element_type=jnp.float32)
    grad_mid, grad_gain_two, grad_shift_two = jax.vjp(
        layer_norm, stream_mid, vector[2 * D : 3 * D], vector[3 * D : 4 * D]
    )[1](grad_normed_two)
    grad_mid = grad_mid + grad_out
    attn_low = grad_mid.astype(jnp.bfloat16)
    grad_wout = jnp.dot(mixed_low.T, attn_low, preferred_element_type=jnp.bfloat16)
    grad_mixed = (
        jnp.dot(attn_low, w_out.T, preferred_element_type=jnp.float32)
        .astype(jnp.bfloat16)
        .reshape(LEN, HEADS, HD)
    )
    heads_view = projected.reshape(LEN, 3, HEADS, HD)
    query_rows = heads_view[:, 0]
    key_rows = heads_view[:, 1]
    value_rows = heads_view[:, 2]
    attn_probs = jnp.exp(attention_scores(query_rows, key_rows, allowed) - log_total)
    grad_probs = jnp.einsum(
        "qhd,khd->hqk", grad_mixed, value_rows, preferred_element_type=jnp.float32
    )
    grad_values = jnp.einsum(
        "hqk,qhd->khd",
        attn_probs.astype(jnp.bfloat16),
        grad_mixed,
        preferred_element_type=jnp.float32,
    )
    row_dot = jnp.sum(grad_probs * attn_probs, axis=-1, keepdims=True)
    scores_low = (attn_probs * (grad_probs - row_dot)).astype(jnp.bfloat16)
    grad_queries = (
        jnp.einsum("hqk,khd->qhd", scores_low, key_rows, preferred_element_type=jnp.float32) * 0.125
    )
    grad_keys = (
        jnp.einsum("hqk,qhd->khd", scores_low, query_rows, preferred_element_type=jnp.float32)
        * 0.125
    )
    qkv_low = (
        jnp.stack([grad_queries, grad_keys, grad_values], axis=1)
        .reshape(LEN, 3 * D)
        .astype(jnp.bfloat16)
    )
    grad_wqkv = jnp.dot(normed_low.T, qkv_low, preferred_element_type=jnp.bfloat16)
    grad_normed = jnp.dot(qkv_low, w_qkv.T, preferred_element_type=jnp.float32)
    grad_input, grad_gain_one, grad_shift_one = jax.vjp(
        layer_norm, stream, vector[0:D], vector[D : 2 * D]
    )[1](grad_normed)
    bias_qkv = jnp.sum(qkv_low.astype(jnp.float32), axis=0)
    grad_vector = jnp.concatenate(
        [
            grad_gain_one,
            grad_shift_one,
            grad_gain_two,
            grad_shift_two,
            bias_qkv[0:D],
            bias_qkv[2 * D : 3 * D],
            jnp.sum(attn_low.astype(jnp.float32), axis=0),
            jnp.sum(branch_low.astype(jnp.float32), axis=0),
            jnp.sum(pre_low.astype(jnp.float32), axis=0),
        ]
    )
    return (grad_input + grad_mid, (grad_wqkv, grad_wout, grad_wfc, grad_wproj), grad_vector)


def combine_stats(earlier, later):
    max_one, total_one, target_one = earlier
    max_two, total_two, target_two = later
    joint_max = jnp.maximum(max_one, max_two)
    joint_total = total_one * jnp.exp(max_one - joint_max) + total_two * jnp.exp(
        max_two - joint_max
    )
    return (joint_max, joint_total, target_one + target_two)


def adamw(weight, moment_one, moment_two, gradient, step_rate, decay_rate, step_float):
    one_new = 0.5 * moment_one + 0.5 * gradient
    two_new = 0.5 * moment_two + 0.5 * gradient * gradient
    fix_scale = 1.0 - jnp.power(0.5, step_float)
    update = one_new / fix_scale / (jnp.sqrt(two_new / fix_scale) + 1e-08)
    return (weight - step_rate * (update + decay_rate * weight), one_new, two_new)


def on_device(
    token_ids,
    seq_lengths,
    loss_slots,
    target_ids,
    step_count,
    w_qkv,
    w_out,
    w_fc,
    w_proj,
    vectors,
    pos_table,
    embed_table,
    mom_qkv,
    mom_out,
    mom_fc,
    mom_proj,
    mom_vectors,
    mom_pos,
    mom_embed,
    sec_qkv,
    sec_out,
    sec_fc,
    sec_proj,
    sec_vectors,
    sec_pos,
    sec_embed,
):
    per_layer = 8 * D + FF
    net = Net()
    size, halves = net.size, net.halves
    same_core = halves * size
    devices = 2 * same_core
    low = jnp.bfloat16
    near = LEN * 9 // 16
    rest = LEN - near
    slots = loss_slots.shape[0]

    numbers = jnp.concatenate([token_ids, loss_slots, target_ids, seq_lengths])
    numbers = net.ring_gather(jnp.stack([numbers, net.swap_half(numbers)], axis=1))
    numbers = jnp.stack(numbers).transpose(2, 0, 1)
    group_tokens = numbers[:, :, :LEN]
    group_slots = numbers[:, :, LEN : LEN + slots].reshape(same_core * slots)
    group_targets = numbers[:, :, LEN + slots : LEN + 2 * slots].reshape(same_core * slots)
    core_total = jnp.sum(numbers[:, :, LEN + 2 * slots :].astype(jnp.float32))
    token_total = core_total + net.swap_core(core_total[None])[0]

    own_rows = embed_table.shape[0]
    table_own = embed_table.astype(low)
    table_low = jnp.concatenate([table_own, net.swap_core(table_own)])
    chip_rows = 2 * own_rows
    own_start = net.device * own_rows
    other_start = (net.device + (1 - 2 * net.core) * size) * own_rows

    def locate(ids):
        mine = ids - own_start
        other = ids - other_start
        return jnp.where(
            (mine >= 0) & (mine < own_rows),
            mine,
            jnp.where((other >= 0) & (other < own_rows), other + own_rows, -1),
        )

    def one_hot(ids):
        return (ids[:, None] == jnp.arange(chip_rows)[None, :]).astype(low)

    local_tokens = locate(group_tokens)

    def look_up(ids):
        return jnp.dot(
            one_hot(ids.reshape(-1)), table_low, preferred_element_type=jnp.float32
        ).astype(low)

    shared = pos_table.shape[0]
    vector_rows = -(-vectors.shape[0] // D)
    padded = jnp.pad(vectors, (0, vector_rows * D - vectors.shape[0])).reshape(vector_rows, D)
    spare = -(shared + vector_rows) % 16
    small_own = jnp.concatenate([pos_table, padded, jnp.zeros((spare, D), jnp.float32)])
    shards_low = []
    for layer_at in range(LAYERS):
        shards_low += [part[layer_at].astype(low) for part in (w_qkv, w_fc, w_proj, w_out)]
    gathered = gather_call(
        size,
        shards_low + [small_own.astype(low)],
        (True, True, False, False) * LAYERS + (False,),
        True,
        1,
    )
    small_low = gathered[-1]
    pos_low = small_low[:, :shared].reshape(devices * shared, D)
    vector_all = (
        small_low[:, shared : shared + vector_rows]
        .reshape(devices, vector_rows * D)[:, : vectors.shape[0]]
        .reshape(-1)
        .astype(jnp.float32)
    )

    near_all = look_up(local_tokens[:, :, :near]).reshape(same_core, near, D)
    rest_all = look_up(local_tokens[:, :, near:]).reshape(same_core, rest, D)
    bands = max(1, same_core // 16)
    band = D // bands
    stream = jnp.concatenate(
        [
            jnp.concatenate(
                scatter_call(
                    size,
                    [part[:, :, at * band : (at + 1) * band] for part in (near_all, rest_all)],
                    (True, False),
                    False,
                    low,
                    2,
                )
            )
            for at in range(bands)
        ],
        axis=1,
    )
    stream = stream.astype(jnp.float32) + pos_low[:LEN].astype(jnp.float32)

    allowed = attention_mask(seq_lengths[0])
    kept_weights = []
    saved_list = []
    for layer_at in range(LAYERS):
        w_a, w_c, w_d, w_b = (
            part.reshape(-1, part.shape[2]) for part in gathered[layer_at * 4 : layer_at * 4 + 4]
        )
        weights = (w_a, w_b, w_c, w_d)
        kept_weights.append(weights)
        stream, saved_acts = layer_forward(
            stream, weights, vector_all[layer_at * per_layer : (layer_at + 1) * per_layer], allowed
        )
        saved_list.append(saved_acts)
    tail_start = LAYERS * per_layer
    final_norm, final_pull = jax.vjp(
        layer_norm,
        stream,
        vector_all[tail_start : tail_start + D],
        vector_all[tail_start + D : tail_start + 2 * D],
    )
    slot_rows = jnp.maximum(loss_slots, 0)
    own_picked = final_norm[slot_rows].astype(low)
    group_rows = net.ring_gather(jnp.stack([own_picked, net.swap_half(own_picked)]))
    group_rows = jnp.stack(group_rows, axis=1).reshape(same_core * slots, D)
    logits = jnp.dot(group_rows, table_low.T, preferred_element_type=jnp.float32)
    target_onehot = locate(group_targets)[:, None] == jnp.arange(chip_rows)[None, :]
    row_max = jnp.max(logits, axis=-1)
    row_total = jnp.sum(jnp.exp(logits - row_max[:, None]), axis=-1)
    target_logit = jnp.sum(jnp.where(target_onehot, logits, 0.0), axis=-1)
    half_of = jnp.arange(halves)[:, None]
    wide_index = jnp.arange(size)[None, :]
    place_of = jnp.where(wide_index % 2 == 0, wide_index // 2, size - 1 - (wide_index - 1) // 2)
    to_device = ((half_of ^ net.half) * size + (place_of - net.place) % size).reshape(-1)
    offsets = (net.place + wide_index) % size
    wide_there = jnp.where(offsets < size // 2, 2 * offsets, 2 * (size - 1 - offsets) + 1)
    from_device = ((half_of ^ net.half) * size + wide_there).reshape(-1)
    stats = jnp.stack([row_max, row_total, target_logit], axis=-1)
    stats = jnp.take(stats.reshape(same_core, slots * 3), to_device, axis=0)
    stats = stats.reshape(same_core * slots, 3).T

    def merged(stats, there):
        return jnp.stack(combine_stats((stats[0], stats[1], stats[2]), (there[0], there[1], there[2])))

    stats = merged(stats, net.swap_half(stats))
    bit = 1
    while bit < size:
        stats = merged(stats, net.flip(stats, bit))
        bit *= 2
    stats = jnp.stack([stats[0] + jnp.log(stats[1]), stats[2]]).reshape(2, same_core, slots)
    stats = jnp.take(stats, from_device, axis=1).reshape(2, same_core * slots)
    log_total, merged_target = stats[0], stats[1]
    group_used = (group_slots >= 0).astype(jnp.float32)
    own_loss = jnp.sum(((log_total - merged_target) * group_used)[:slots])
    grad_logits = (
        (jnp.exp(logits - log_total[:, None]) - target_onehot.astype(jnp.float32))
        * (group_used / token_total)[:, None]
    ).astype(low)
    grad_rows = jnp.dot(grad_logits, table_low, preferred_element_type=jnp.float32)
    grad_rows = grad_rows.reshape(halves, size, slots, D)
    cut = D // 2
    pair = grad_rows[0, :, :, :cut] + net.swap_half(grad_rows[1, :, :, :cut])
    grad_one = net.ring_scatter(lambda at: pair[at], jnp.float32)
    both = net.ring_scatter(lambda at: grad_rows[:, at, :, cut:], jnp.float32)
    grad_two = both[0] + net.swap_half(both[1])
    grad_rows = jnp.concatenate([grad_one, grad_two], axis=1)
    grad_final = jnp.zeros((LEN, D), jnp.float32).at[slot_rows].add(grad_rows)
    grad_stream, grad_gain_final, grad_shift_final = final_pull(grad_final)
    layer_shards = []
    vector_grads = []
    for layer_at in reversed(range(LAYERS)):
        grad_stream, full_grads, grad_vector = layer_backward(
            grad_stream,
            saved_list[layer_at],
            kept_weights[layer_at],
            vector_all[layer_at * per_layer : (layer_at + 1) * per_layer],
            allowed,
        )
        grad_a, grad_b, grad_c, grad_d = full_grads
        shard_a, shard_c, shard_d, shard_b = scatter_call(
            size,
            [part.reshape(devices, -1, part.shape[1]) for part in (grad_a, grad_c, grad_d, grad_b)],
            (True, True, False, False),
            True,
            jnp.float32,
            3,
        )
        layer_shards.insert(0, (shard_a, shard_b, shard_c, shard_d))
        vector_grads.insert(0, grad_vector)
    grad_low = grad_stream.astype(low)
    grad_near, grad_rest = grad_low[:near], grad_low[near:]
    near_all, rest_all = gather_call(size, [grad_near, grad_rest], (True, False), False, 4)

    def spread(ids, rows):
        return jnp.dot(one_hot(ids.reshape(-1)).T, rows, preferred_element_type=jnp.float32)

    grad_table = jnp.dot(grad_logits.T, group_rows, preferred_element_type=jnp.float32)
    grad_table = grad_table + spread(local_tokens[:, :, :near], near_all.reshape(-1, D))
    grad_table = grad_table + spread(local_tokens[:, :, near:], rest_all.reshape(-1, D))
    table_shard = grad_table[:own_rows] + net.swap_core(grad_table[own_rows:])
    grad_pos = jnp.concatenate(
        [
            jnp.sum(near_all.astype(jnp.float32), axis=0),
            jnp.sum(rest_all.astype(jnp.float32), axis=0),
        ]
    )
    grad_pos = jnp.pad(grad_pos, ((0, POS - LEN), (0, 0)))
    other_device = net.device + (1 - 2 * net.core) * size
    pos_shard = lax.dynamic_slice_in_dim(grad_pos, net.device * shared, shared) + net.swap_core(
        lax.dynamic_slice_in_dim(grad_pos, other_device * shared, shared)
    )
    grad_small = jnp.concatenate(vector_grads + [grad_gain_final, grad_shift_final])
    small_shard = net.reduce_rows(
        grad_small.reshape(devices * 2, -1), False, jnp.float32
    ).reshape(-1)
    qkv_shard = jnp.stack([member[0] for member in layer_shards])
    out_shard = jnp.stack([member[1] for member in layer_shards])
    fc_shard = jnp.stack([member[2] for member in layer_shards])
    proj_shard = jnp.stack([member[3] for member in layer_shards])
    shards = (qkv_shard, out_shard, fc_shard, proj_shard, small_shard, pos_shard, table_shard)
    squares = jnp.sum(jnp.stack([jnp.sum(member * member) for member in shards]))
    loss_total, square_total = net.total(jnp.stack([own_loss, squares]))
    loss_value = loss_total / token_total
    grad_norm = jnp.sqrt(square_total)
    factor = CLIP_LIMIT / jnp.maximum(grad_norm, CLIP_LIMIT)
    step_float = step_count.astype(jnp.float32)
    params = (w_qkv, w_out, w_fc, w_proj, vectors, pos_table, embed_table)
    moments_one = (mom_qkv, mom_out, mom_fc, mom_proj, mom_vectors, mom_pos, mom_embed)
    moments_two = (sec_qkv, sec_out, sec_fc, sec_proj, sec_vectors, sec_pos, sec_embed)
    step_rates = (
        RATE_MATRIX,
        RATE_MATRIX,
        RATE_MATRIX,
        RATE_MATRIX,
        RATE_VECTOR,
        RATE_MATRIX,
        RATE_MATRIX,
    )
    decay_rates = (
        DECAY_MATRIX,
        DECAY_MATRIX,
        DECAY_MATRIX,
        DECAY_MATRIX,
        0.0,
        DECAY_MATRIX,
        DECAY_MATRIX,
    )
    results = [
        adamw(
            params[where_at],
            moments_one[where_at],
            moments_two[where_at],
            shards[where_at] * factor,
            step_rates[where_at],
            decay_rates[where_at],
            step_float,
        )
        for where_at in range(7)
    ]
    return (
        loss_value,
        grad_norm,
        results[0][0],
        results[1][0],
        results[2][0],
        results[3][0],
        results[4][0],
        results[5][0],
        results[6][0],
        results[0][1],
        results[1][1],
        results[2][1],
        results[3][1],
        results[4][1],
        results[5][1],
        results[6][1],
        results[0][2],
        results[1][2],
        results[2][2],
        results[3][2],
        results[4][2],
        results[5][2],
        results[6][2],
    )


def solution(mesh):
    return jax.shard_map(
        on_device,
        mesh=mesh,
        in_specs=(
            P(("narrow", "wide")),
            P(("narrow", "wide")),
            P(("narrow", "wide")),
            P(("narrow", "wide")),
            P(),
            P(None, ("narrow", "wide"), None),
            P(None, ("narrow", "wide"), None),
            P(None, ("narrow", "wide"), None),
            P(None, ("narrow", "wide"), None),
            P(("narrow", "wide")),
            P(("narrow", "wide"), None),
            P(("narrow", "wide"), None),
            P(None, ("narrow", "wide"), None),
            P(None, ("narrow", "wide"), None),
            P(None, ("narrow", "wide"), None),
            P(None, ("narrow", "wide"), None),
            P(("narrow", "wide")),
            P(("narrow", "wide"), None),
            P(("narrow", "wide"), None),
            P(None, ("narrow", "wide"), None),
            P(None, ("narrow", "wide"), None),
            P(None, ("narrow", "wide"), None),
            P(None, ("narrow", "wide"), None),
            P(("narrow", "wide")),
            P(("narrow", "wide"), None),
            P(("narrow", "wide"), None),
        ),
        out_specs=(
            P(),
            P(),
            P(None, ("narrow", "wide"), None),
            P(None, ("narrow", "wide"), None),
            P(None, ("narrow", "wide"), None),
            P(None, ("narrow", "wide"), None),
            P(("narrow", "wide")),
            P(("narrow", "wide"), None),
            P(("narrow", "wide"), None),
            P(None, ("narrow", "wide"), None),
            P(None, ("narrow", "wide"), None),
            P(None, ("narrow", "wide"), None),
            P(None, ("narrow", "wide"), None),
            P(("narrow", "wide")),
            P(("narrow", "wide"), None),
            P(("narrow", "wide"), None),
            P(None, ("narrow", "wide"), None),
            P(None, ("narrow", "wide"), None),
            P(None, ("narrow", "wide"), None),
            P(None, ("narrow", "wide"), None),
            P(("narrow", "wide")),
            P(("narrow", "wide"), None),
            P(("narrow", "wide"), None),
        ),
        check_vma=False,
    )
```

```python
import functools

import jax
import jax.numpy as jnp
from jax import lax
from jax.experimental import pallas as pl
from jax.experimental.pallas import tpu as pltpu
from jax.sharding import PartitionSpec as P

D = 1024
HEADS = 16
HD = 64
FF = 4096
POS = 1024
LAYERS = 2
LEN = 512
LOSS_DEV = 32


CLIP_LIMIT = 0.002
RATE_MATRIX = 0.03
RATE_VECTOR = 0.3
DECAY_MATRIX = 0.1


class Net:
    def __init__(self):
        self.narrow_at = lax.axis_index("narrow")
        self.wide_at = lax.axis_index("wide")
        self.narrow_size = lax.axis_size("narrow")
        self.size = lax.axis_size("wide")
        size = self.size
        self.core = self.narrow_at % 2
        self.half = self.narrow_at // 2
        self.halves = self.narrow_size // 2
        self.place = jnp.where(
            self.wide_at % 2 == 0, self.wide_at // 2, size - 1 - (self.wide_at - 1) // 2
        )
        self.device = self.narrow_at * size + self.wide_at
        order = list(range(0, size, 2)) + list(range(size - 1, 0, -2))
        pairs = [(n, w) for n in range(self.narrow_size) for w in range(size)]
        self.core_pairs = [(n * size + w, (n ^ 1) * size + w) for n, w in pairs]
        self.half_pairs = [(n * size + w, (n ^ 2) * size + w) for n, w in pairs]
        self.right = [
            (n * size + order[i], n * size + order[(i + 1) % size])
            for n in range(self.narrow_size)
            for i in range(size)
        ]
        self.left = [(later, earlier) for earlier, later in self.right]

    def step(self, array, pairs):
        return lax.ppermute(array, ("narrow", "wide"), pairs)

    def swap_core(self, array):
        return self.step(array, self.core_pairs)

    def swap_half(self, array):
        return self.step(array, self.half_pairs)

    def wide_of(self, offset):
        size = self.size
        at = lax.rem(self.place + offset, size)
        return jnp.where(at < size // 2, 2 * at, 2 * (size - 1 - at) + 1)

    def ring_scatter(self, take, low):
        size = self.size
        far = size // 2
        block = take(far)
        cut = block.shape[0] // 2
        from_left = self.step(block[:cut].astype(low), self.right)
        from_right = self.step(block[cut:].astype(low), self.left)
        for at in range(far - 1, 0, -1):
            to_right = take(at).astype(jnp.float32)
            to_left = take(size - at).astype(jnp.float32)
            if at == far - 1:
                to_right = jnp.concatenate(
                    [to_right[:cut] + from_left.astype(jnp.float32), to_right[cut:]]
                )
                to_left = jnp.concatenate(
                    [to_left[:cut], to_left[cut:] + from_right.astype(jnp.float32)]
                )
            else:
                to_right = to_right + from_left.astype(jnp.float32)
                to_left = to_left + from_right.astype(jnp.float32)
            from_left = self.step(to_right.astype(low), self.right)
            from_right = self.step(to_left.astype(low), self.left)
        return (
            take(0).astype(jnp.float32)
            + from_left.astype(jnp.float32)
            + from_right.astype(jnp.float32)
        )

    def reduce_rows(self, array, half_first, low):
        size, halves = self.size, self.halves
        rows = array.shape[0] // (halves * 2 * size)
        columns = array.shape[1]
        split = array.reshape(halves, 2, size, rows, columns)

        def pick(value, at, axis):
            return lax.dynamic_index_in_dim(value, at, axis, keepdims=False)

        def plus(one, two):
            return one.astype(jnp.float32) + two.astype(jnp.float32)

        chip = plus(
            pick(split, self.core, 1), self.swap_core(pick(split, 1 - self.core, 1).astype(low))
        ).astype(low)
        if half_first:
            pair = plus(
                pick(chip, self.half, 0), self.swap_half(pick(chip, 1 - self.half, 0))
            ).astype(low)
            return self.ring_scatter(lambda at: pick(pair, self.wide_of(at), 0), low)
        both = self.ring_scatter(lambda at: pick(chip, self.wide_of(at), 1), low)
        return plus(
            pick(both, self.half, 0), self.swap_half(pick(both, 1 - self.half, 0).astype(low))
        )


MESH = pl.DeviceIdType.MESH


class Spot:
    def __init__(self, size):
        self.size = size
        narrow, wide = lax.axis_index("narrow"), lax.axis_index("wide")
        odd = lax.rem(wide, 2)
        self.core, self.half = lax.rem(narrow, 2), lax.div(narrow, 2)
        self.wide = wide
        self.place = (1 - odd) * lax.div(wide, 2) + odd * (size - 1 - lax.div(wide, 2))
        self.to_core = (narrow + 1 - 2 * self.core, wide)
        self.to_half = (narrow + 2 - 4 * self.half, wide)
        self.right = (narrow, self.wide_of(1))
        self.left = (narrow, self.wide_of(size - 1))

    def wide_of(self, offset):
        at = lax.rem(self.place + offset, self.size)
        late = lax.div(at, self.size // 2)
        return (1 - late) * 2 * at + late * (2 * (self.size - 1 - at) + 1)

    def index(self, turned, other_core, offset):
        half = self.half + turned * (1 - 2 * self.half)
        core = self.core + other_core * (1 - 2 * self.core)
        return (2 * half + core) * self.size + self.wide_of(offset)

    def meet(self, with_core):
        barrier = pltpu.get_barrier_semaphore()
        peers = [self.to_half, self.right, self.left] + ([self.to_core] if with_core else [])
        for peer in peers:
            pl.semaphore_signal(barrier, inc=1, device_id=peer, device_id_type=MESH)
        pl.semaphore_wait(barrier, len(peers))


def cut_of(rows):
    return rows // 2 if rows % 32 == 0 else rows


def gather_steps(size, ring_first, across, shards, wholes, sems, spot, tick, ready):
    count = len(ring_first)
    ring_sem, half_sem, core_sem, send_sem, local_sem = sems
    far = size // 2

    def index(turned, offset, toward=None):
        if across:
            return spot.index(turned, 0, offset % size)
        if toward == "half":
            turned = 1 - turned
        offset = offset + {"right": -1, "left": 1}.get(toward, 0)
        return turned * size + offset % size

    def send(at, source, turned, offset, toward, sem, rows=None):
        target = wholes[at].at[index(turned, offset, toward)]
        if rows is not None:
            source, target = source.at[rows], target.at[rows]
        device = {
            "half": spot.to_half,
            "right": spot.right,
            "left": spot.left,
            "core": spot.to_core,
        }[toward]
        pltpu.make_async_remote_copy(
            src_ref=source,
            dst_ref=target,
            send_sem=send_sem.at[at],
            recv_sem=sem,
            device_id=device,
            device_id_type=MESH,
        ).start()

    def landed(region, sem):
        pltpu.make_async_copy(region, region, sem).wait()

    def piece(at, turned, offset):
        return wholes[at].at[index(turned, offset)]

    def on_core(at, source, turned, offset):
        if across:
            send(at, source, turned, offset, "core", core_sem.at[at])

    def on_ring(at, turned, source, offset, way, step, rows=None):
        toward = ("right", "left")[way]
        send(at, source, turned, offset, toward, ring_sem.at[at, turned, way, step], rows)

    locals_ = []
    for at in range(count):
        copy = pltpu.make_async_copy(shards[at], piece(at, 0, 0), local_sem.at[at])
        copy.start()
        locals_.append(copy)
    for at in range(count):
        if not ring_first[at]:
            send(at, shards[at], 0, 0, "half", half_sem.at[at, 0])
    for at in range(count):
        if ring_first[at]:
            on_ring(at, 0, shards[at], 0, 0, 1)
            on_ring(at, 0, shards[at], 0, 1, 1)
            send(at, shards[at], 0, 0, "half", half_sem.at[at, 0])
    for at in range(count):
        on_core(at, shards[at], 0, 0)
    for at in range(count):
        if not ring_first[at]:
            landed(piece(at, 1, 0), half_sem.at[at, 0])
            for way in (0, 1):
                on_ring(at, 0, shards[at], 0, way, 1)
                on_ring(at, 1, piece(at, 1, 0), 0, way, 1)
            on_core(at, piece(at, 1, 0), 1, 0)
    for at in range(count):
        locals_[at].wait()
        ready(at, 0, 0)
        if not ring_first[at]:
            ready(at, 1, 0)
        tick()

    def turned_arrivals(at, step):
        offsets = (0,) if step == 0 else (far,) if step == far else (-step, step)
        for offset in offsets:
            landed(piece(at, 1, offset), half_sem.at[at, offset % size])
            on_core(at, piece(at, 1, offset), 1, offset)
            came.append((at, 1, offset))

    came = []

    def flush():
        for one in came:
            ready(*one)
        came.clear()
        tick()

    for step in range(1, far + 1):
        for at in range(count):
            rows = shards[at].shape[0]
            cut = cut_of(rows)
            if ring_first[at]:
                if step < far:
                    for way in (0, 1):
                        offset = (-step, step)[way]
                        here = piece(at, 0, offset)
                        landed(here, ring_sem.at[at, 0, way, step])
                        if step < far - 1:
                            on_ring(at, 0, here, offset, way, step + 1)
                        elif way == 0:
                            on_ring(at, 0, here, offset, way, step + 1, pl.ds(0, cut))
                        elif cut < rows:
                            on_ring(at, 0, here, offset, way, step + 1, pl.ds(cut, rows - cut))
                        send(at, here, 0, offset, "half", half_sem.at[at, offset % size])
                        on_core(at, here, 0, offset)
                        came.append((at, 0, offset))
                else:
                    here = piece(at, 0, far)
                    landed(here.at[pl.ds(0, cut)], ring_sem.at[at, 0, 0, step])
                    if cut < rows:
                        landed(here.at[pl.ds(cut, rows - cut)], ring_sem.at[at, 0, 1, step])
                    send(at, here, 0, far, "half", half_sem.at[at, far])
                    on_core(at, here, 0, far)
                    came.append((at, 0, far))
                turned_arrivals(at, step - 1)
            else:
                for way in (0, 1):
                    for turned in (0, 1):
                        if step == far and turned != way:
                            continue
                        offset = (-step, step)[way]
                        here = piece(at, turned, offset)
                        landed(here, ring_sem.at[at, turned, way, step])
                        if step < far - 1 or (step == far - 1 and turned == way):
                            on_ring(at, turned, here, offset, way, step + 1)
                        on_core(at, here, turned, offset)
                        came.append((at, turned, offset))
            flush()
    for at in range(count):
        if ring_first[at]:
            turned_arrivals(at, far)
            flush()
    for at in range(count):
        if across:
            landed(wholes[at].at[pl.ds(0, 2 * size)], core_sem.at[at])
        sent = 4 * size - 1 if across else 2 * size - 1
        landed(wholes[at].at[pl.ds(0, sent)], send_sem.at[at])


def gather_sems(count, size):
    return [
        pltpu.SemaphoreType.DMA((count, 2, 2, size // 2 + 1)),
        pltpu.SemaphoreType.DMA((count, size)),
        pltpu.SemaphoreType.DMA((count,)),
        pltpu.SemaphoreType.DMA((count,)),
        pltpu.SemaphoreType.DMA((count,)),
    ]


def look_up_body(size, ring_first, *refs):
    count = len(ring_first)
    shards, (table_own, ids) = refs[:count], refs[count : count + 2]
    refs = refs[count + 2 :]
    wholes, (table_out, found) = refs[:count], refs[count : count + 2]
    table, hot, stage, table_sem, stage_sem, *sems = refs[count + 2 :]
    spot = Spot(size)
    spot.meet(True)
    height = table_own.shape[0]
    mine = pltpu.make_async_copy(table_own, table.at[pl.ds(0, height)], table_sem.at[0])
    mine.start()
    swap = pltpu.make_async_remote_copy(
        src_ref=table_own,
        dst_ref=table.at[pl.ds(height, height)],
        send_sem=table_sem.at[1],
        recv_sem=table_sem.at[2],
        device_id=spot.to_core,
        device_id_type=MESH,
    )
    swap.start()
    out = pltpu.make_async_copy(table, table_out, table_sem.at[3])
    pieces, rows = found.shape[:2]
    width = 256
    state = {"ticks": 0, "done": 0}

    def copy_out(number):
        slot = lax.rem(number, 2)
        return pltpu.make_async_copy(stage.at[slot], found.at[number], stage_sem.at[slot])

    def work(first, last):
        def one(number, nothing):
            columns = lax.broadcasted_iota(jnp.int32, (rows, 2 * height), 1)
            hot[...] = jnp.where(columns == ids[number], 1.0, 0.0).astype(jnp.bfloat16)

            @pl.when(number >= 2)
            def _():
                copy_out(number - 2).wait()

            def part(at, nothing):
                window = pl.ds(pl.multiple_of(at * width, width), width)
                stage[lax.rem(number, 2), :, window] = jnp.dot(
                    hot[...], table[:, window], preferred_element_type=jnp.float32
                ).astype(jnp.bfloat16)
                return nothing

            lax.fori_loop(0, D // width, part, 0)
            copy_out(number).start()
            return nothing

        lax.fori_loop(first, last, one, 0)

    def tick(share=1):
        if state["done"] == pieces:
            return
        if state["done"] == 0:
            mine.wait()
            swap.wait_recv()
            out.start()
        last = min(pieces, state["done"] + share)
        work(state["done"], last)
        state["done"] = last

    gather_steps(
        size, ring_first, True, shards, wholes, sems, spot, tick, lambda at, turned, offset: None
    )
    tick(pieces)
    copy_out(pieces - 2).wait()
    copy_out(pieces - 1).wait()
    out.wait()
    swap.wait_send()


def look_up_call(size, shards, ring_first, table_own, ids, number):
    count = len(shards)
    height = table_own.shape[0]
    found = ids.shape[:2] + (D,)
    outs = [jax.ShapeDtypeStruct((4 * size,) + a.shape, a.dtype) for a in shards]
    outs.append(jax.ShapeDtypeStruct((2 * height, D), table_own.dtype))
    outs.append(jax.ShapeDtypeStruct(found, table_own.dtype))
    return pl.pallas_call(
        functools.partial(look_up_body, size, ring_first),
        out_shape=outs,
        in_specs=[pl.BlockSpec(memory_space=pl.ANY)] * (count + 1)
        + [pl.BlockSpec(memory_space=pltpu.VMEM)],
        out_specs=[pl.BlockSpec(memory_space=pl.ANY)] * (count + 2),
        scratch_shapes=[
            pltpu.VMEM((2 * height, D), table_own.dtype),
            pltpu.VMEM((ids.shape[1], 2 * height), table_own.dtype),
            pltpu.VMEM((2,) + found[1:], table_own.dtype),
            pltpu.SemaphoreType.DMA((4,)),
            pltpu.SemaphoreType.DMA((2,)),
        ]
        + gather_sems(count, size),
        compiler_params=pltpu.CompilerParams(
            collective_id=number, has_side_effects=True, vmem_limit_bytes=48 * 1024 * 1024
        ),
    )(*shards, table_own, ids)


def spread_body(size, *refs):
    near, rest, ids_near, ids_rest, start = refs[:5]
    table_out, place_out = refs[5:7]
    near_all, rest_all, total, core_in, table_sem, *sems = refs[7:]
    ids = (ids_near, ids_rest)
    wholes = (near_all, rest_all)
    spot = Spot(size)
    spot.meet(True)
    height = table_out.shape[0]
    block = 2 * height // 8
    first = pltpu.make_async_copy(start, total, table_sem.at[0])
    first.start()
    place_out[...] = jnp.zeros_like(place_out)
    waiting = []

    def spread(pieces, blocks):
        def one(number, nothing):
            window = pl.ds(pl.multiple_of(number * block, 16), block)
            row = number * block + lax.broadcasted_iota(jnp.int32, (block, near.shape[0]), 0)
            value = total[window, :]
            for at, piece in pieces:
                hot = jnp.where(row == ids[at][piece], 1.0, 0.0).astype(jnp.bfloat16)
                value = value + jnp.dot(
                    hot, wholes[at][piece], preferred_element_type=jnp.float32
                )
            total[window, :] = value
            return nothing

        lax.fori_loop(blocks[0], blocks[1], one, 0)

    def place(pieces):
        for at, piece in pieces:
            rows = pl.ds(at * near.shape[0], near.shape[0])
            place_out[rows, :] += wholes[at][piece].astype(jnp.float32)

    def ready(at, turned, offset):
        waiting.append((at, turned * size + offset % size))

    def tick():
        if tick.first:
            first.wait()
            tick.first = False
        if len(waiting) >= 4:
            spread(waiting, (0, 8))
            place(waiting)
            waiting.clear()

    tick.first = True
    gather_steps(size, (True, False), False, (near, rest), wholes, sems, spot, tick, ready)
    if waiting:
        spread(waiting, (4, 8))
    swap = pltpu.make_async_remote_copy(
        src_ref=total.at[pl.ds(height, height)],
        dst_ref=core_in,
        send_sem=table_sem.at[1],
        recv_sem=table_sem.at[2],
        device_id=spot.to_core,
        device_id_type=MESH,
    )
    swap.start()
    if waiting:
        spread(waiting, (0, 4))
        place(waiting)
    swap.wait_recv()
    step = height // 4

    def add(number, nothing):
        window = pl.ds(pl.multiple_of(number * step, 16), step)
        total[window, :] += core_in[window, :]
        return nothing

    lax.fori_loop(0, 4, add, 0)
    out = pltpu.make_async_copy(total.at[pl.ds(0, height)], table_out, table_sem.at[0])
    out.start()
    swap.wait_send()
    out.wait()


def spread_call(size, near, rest, ids, start, number):
    height = start.shape[0] // 2
    pieces = (2 * size,) + near.shape
    return pl.pallas_call(
        functools.partial(spread_body, size),
        out_shape=[
            jax.ShapeDtypeStruct((height, D), jnp.float32),
            jax.ShapeDtypeStruct((LEN, D), jnp.float32),
        ],
        in_specs=[pl.BlockSpec(memory_space=pl.ANY)] * 2
        + [pl.BlockSpec(memory_space=pltpu.VMEM)] * 2
        + [pl.BlockSpec(memory_space=pl.ANY)],
        out_specs=[
            pl.BlockSpec(memory_space=pl.ANY),
            pl.BlockSpec(memory_space=pltpu.VMEM),
        ],
        scratch_shapes=[
            pltpu.VMEM(pieces, near.dtype),
            pltpu.VMEM(pieces, near.dtype),
            pltpu.VMEM((2 * height, D), jnp.float32),
            pltpu.VMEM((height, D), jnp.float32),
            pltpu.SemaphoreType.DMA((3,)),
        ]
        + gather_sems(2, size),
        compiler_params=pltpu.CompilerParams(
            collective_id=number, has_side_effects=True, vmem_limit_bytes=60 * 1024 * 1024
        ),
    )(near, rest, *ids, start)


def plain_gather_body(size, ring_first, across, *refs):
    count = len(ring_first)
    spot = Spot(size)
    spot.meet(across)
    gather_steps(
        size,
        ring_first,
        across,
        refs[:count],
        refs[count : 2 * count],
        refs[2 * count :],
        spot,
        lambda: None,
        lambda at, turned, offset: None,
    )


def gather_call(size, shards, ring_first, across, number):
    count = len(shards)
    total = (4 if across else 2) * size
    return pl.pallas_call(
        functools.partial(plain_gather_body, size, ring_first, across),
        out_shape=[jax.ShapeDtypeStruct((total,) + a.shape, a.dtype) for a in shards],
        in_specs=[pl.BlockSpec(memory_space=pl.ANY)] * count,
        out_specs=[pl.BlockSpec(memory_space=pl.ANY)] * count,
        scratch_shapes=gather_sems(count, size),
        compiler_params=pltpu.CompilerParams(collective_id=number, has_side_effects=True),
    )(*shards)


def cast_body(size, everyone, own_ref, out_ref, come_sem, send_sem, local_sem):
    spot = Spot(size)
    group = (4 if everyone else 2) * size
    narrow = lax.axis_index("narrow")
    mine = (narrow if everyone else spot.half) * size + spot.wide

    def device(step):
        at = lax.rem(mine + step, group)
        block = lax.div(at, size)
        return (block if everyone else 2 * block + spot.core, lax.rem(at, size))

    barrier = pltpu.get_barrier_semaphore()

    def greet(step, nothing):
        pl.semaphore_signal(barrier, inc=1, device_id=device(step), device_id_type=MESH)
        return nothing

    def tell(step, nothing):
        pltpu.make_async_remote_copy(
            src_ref=own_ref,
            dst_ref=out_ref.at[mine],
            send_sem=send_sem,
            recv_sem=come_sem,
            device_id=device(step),
            device_id_type=MESH,
        ).start()
        return nothing

    lax.fori_loop(1, group, greet, 0)
    keep = pltpu.make_async_copy(own_ref, out_ref.at[mine], local_sem)
    keep.start()
    pl.semaphore_wait(barrier, group - 1)
    lax.fori_loop(1, group, tell, 0)
    others = out_ref.at[pl.ds(0, group - 1)]
    pltpu.make_async_copy(others, others, come_sem).wait()
    pltpu.make_async_copy(others, others, send_sem).wait()
    keep.wait()


def cast_call(size, block, everyone, number):
    group = (4 if everyone else 2) * size
    return pl.pallas_call(
        functools.partial(cast_body, size, everyone),
        out_shape=jax.ShapeDtypeStruct((group,) + block.shape, block.dtype),
        in_specs=[pl.BlockSpec(memory_space=pltpu.VMEM)],
        out_specs=pl.BlockSpec(memory_space=pltpu.VMEM),
        scratch_shapes=[pltpu.SemaphoreType.DMA] * 3,
        compiler_params=pltpu.CompilerParams(collective_id=number, has_side_effects=True),
    )(block)


def scatter_body(size, half_first, across, bases, *refs):
    count = len(half_first)
    arrays, outs = refs[:count], refs[count : 2 * count]
    own, core_in, half_in, ring_in = (
        refs[(2 + part) * count : (3 + part) * count] for part in range(4)
    )
    local_sem, core_sem, half_sem, ring_sem, send_sem = refs[6 * count :]
    spot = Spot(size)
    far = size // 2
    slots = [far] + [o for at in range(far - 1, 0, -1) for o in (at, -at)] + [0]
    sent = []

    def landed(region, sem):
        pltpu.make_async_copy(region, region, sem).wait()

    def send(source, target, device, number, at, sem):
        copy = pltpu.make_async_remote_copy(
            src_ref=source,
            dst_ref=target,
            send_sem=send_sem.at[at, number],
            recv_sem=sem,
            device_id=device,
            device_id_type=MESH,
        )
        copy.start()
        sent.append(copy)

    def source_of(at, turned, other_core, offset):
        if across:
            return arrays[at].at[spot.index(turned, other_core, offset % size)]
        base, stride = bases[at]
        return arrays[at].at[base + stride * (turned * size + offset % size)]

    def add(target, parts):
        rows, columns = target.shape
        width = 512 if columns % 512 == 0 else 256 if columns % 256 == 0 else 128

        def one(step, nothing):
            window = pl.ds(pl.multiple_of(step * width, width), width)
            total = parts[0][0][:, window].astype(jnp.float32)
            for part, first, last in parts[1:]:
                if first == 0 and last == rows:
                    total = total + part[:, window].astype(jnp.float32)
            target[:, window] = total.astype(target.dtype)
            for part, first, last in parts[1:]:
                if first != 0 or last != rows:
                    span = pl.ds(first, last - first)
                    target[span, window] = (
                        total[first:last] + part[span, window].astype(jnp.float32)
                    ).astype(target.dtype)
            return nothing

        lax.fori_loop(0, columns // width, one, 0)

    def ring_slot(way, step):
        return way * far + step - 1

    def base(at, turned, offset):
        k = offset % size
        rows = own[at].shape[1]
        here = own[at].at[turned * size + k]
        landed(here, local_sem.at[at, turned * size + k])
        parts = [(here, 0, rows)]
        if across:
            there = core_in[at].at[turned * size + k]
            landed(there, core_sem.at[at, turned * size + k])
            parts.append((there, 0, rows))
        return here, parts

    def ring_parts(at, turned, offset):
        parts = []
        rows = own[at].shape[1]
        cut = cut_of(rows)
        ways = (0, 1) if offset == 0 else (0,) if offset > 0 else (1,)
        for way in ways:
            step = far - abs(offset)
            slot = ring_slot(way, step)
            if half_first[at]:
                if step == 1:
                    first, last = (0, cut) if way == 0 else (cut, rows)
                else:
                    first, last = 0, rows
                if first == last:
                    continue
                region = ring_in[at].at[slot]
                span = region if (first, last) == (0, rows) else region.at[pl.ds(first, last - first)]
                landed(span, ring_sem.at[at, slot])
                parts.append((region, first, last))
            else:
                if step == 1 and turned != way:
                    continue
                region = ring_in[at].at[turned * 2 * far + slot]
                landed(region, ring_sem.at[at, turned * 2 * far + slot])
                parts.append((region, 0, rows))
        return parts

    def ring_send(at, turned, offset):
        here = own[at].at[turned * size + offset % size]
        rows = own[at].shape[1]
        cut = cut_of(rows)
        step = far - abs(offset) + 1
        if offset == far:
            if half_first[at]:
                spans = [(0, pl.ds(0, cut))] + ([(1, pl.ds(cut, rows - cut))] if cut < rows else [])
                for way, span in spans:
                    slot = ring_slot(way, 1)
                    send(
                        here.at[span],
                        ring_in[at].at[slot].at[span],
                        (spot.right, spot.left)[way],
                        slot,
                        at,
                        ring_sem.at[at, slot],
                    )
                return
            ways = (turned,)
        else:
            ways = (0,) if offset > 0 else (1,)
        for way in ways:
            slot = ring_slot(way, step) + (0 if half_first[at] else turned * 2 * far)
            send(
                here,
                ring_in[at].at[slot],
                (spot.right, spot.left)[way],
                slot,
                at,
                ring_sem.at[at, slot],
            )

    spot.meet(across)
    core_base = 4 * far + size
    for offset in slots:
        k = offset % size
        for turned in (1, 0):
            for at in range(count):
                if across:
                    send(
                        source_of(at, turned, 1, offset),
                        core_in[at].at[turned * size + k],
                        spot.to_core,
                        core_base + turned * size + k,
                        at,
                        core_sem.at[at, turned * size + k],
                    )
                pltpu.make_async_copy(
                    source_of(at, turned, 0, offset),
                    own[at].at[turned * size + k],
                    local_sem.at[at, turned * size + k],
                ).start()

    def turned_half(offset):
        for at in range(count):
            if half_first[at]:
                here, parts = base(at, 1, offset)
                k = offset % size
                if across:
                    add(here, parts)
                send(here, half_in[at].at[k], spot.to_half, 4 * far + k, at, half_sem.at[at, k])

    def straight(offset):
        for at in range(count):
            if half_first[at]:
                here, parts = base(at, 0, offset)
                k = offset % size
                landed(half_in[at].at[k], half_sem.at[at, k])
                parts.append((half_in[at].at[k], 0, own[at].shape[1]))
                parts += ring_parts(at, 0, offset) if offset != far else []
                if offset == 0:
                    add(outs[at], parts)
                else:
                    add(here, parts)
                    ring_send(at, 0, offset)

    def both(offset):
        for at in range(count):
            if not half_first[at]:
                for turned in (1, 0):
                    here, parts = base(at, turned, offset)
                    parts += ring_parts(at, turned, offset) if offset != far else []
                    if offset == 0 and turned == 0:
                        landed(half_in[at].at[0], half_sem.at[at, 0])
                        parts.append((half_in[at].at[0], 0, own[at].shape[1]))
                        add(outs[at], parts)
                        continue
                    if len(parts) > 1:
                        add(here, parts)
                    if offset == 0:
                        send(here, half_in[at].at[0], spot.to_half, 4 * far, at, half_sem.at[at, 0])
                    else:
                        ring_send(at, turned, offset)

    groups = [[far]] + [[at, -at] for at in range(far - 1, 0, -1)] + [[0]]
    for number, group in enumerate(groups):
        for offset in group:
            turned_half(offset)
        for offset in group:
            both(offset)
        if number > 0:
            for offset in groups[number - 1]:
                straight(offset)
    for offset in groups[-1]:
        straight(offset)
    for copy in sent:
        copy.wait_send()


def scatter_call(size, arrays, half_first, across, out_type, number, bases=None):
    count = len(arrays)
    far = size // 2
    pieces = [a.shape[1:] for a in arrays]
    own = [pltpu.VMEM((2 * size,) + p, a.dtype) for p, a in zip(pieces, arrays)]
    core_in = [
        pltpu.VMEM((2 * size if across else 1,) + p, a.dtype) for p, a in zip(pieces, arrays)
    ]
    half_in = [
        pltpu.VMEM((size if first else 1,) + p, a.dtype)
        for p, a, first in zip(pieces, arrays, half_first)
    ]
    ring_in = [
        pltpu.VMEM((2 * far if first else 4 * far,) + p, a.dtype)
        for p, a, first in zip(pieces, arrays, half_first)
    ]
    return pl.pallas_call(
        functools.partial(scatter_body, size, half_first, across, bases or ((0, 1),) * count),
        out_shape=[jax.ShapeDtypeStruct(p, out_type) for p in pieces],
        in_specs=[pl.BlockSpec(memory_space=pl.ANY)] * count,
        out_specs=[pl.BlockSpec(memory_space=pltpu.VMEM)] * count,
        scratch_shapes=own
        + core_in
        + half_in
        + ring_in
        + [
            pltpu.SemaphoreType.DMA((count, 2 * size)),
            pltpu.SemaphoreType.DMA((count, 2 * size)),
            pltpu.SemaphoreType.DMA((count, size)),
            pltpu.SemaphoreType.DMA((count, 4 * far)),
            pltpu.SemaphoreType.DMA((count, 4 * far + 3 * size)),
        ],
        compiler_params=pltpu.CompilerParams(
            collective_id=number, has_side_effects=True, vmem_limit_bytes=60 * 1024 * 1024
        ),
    )(*arrays)


def layer_norm(values, gain, shift):
    center = values - jnp.mean(values, axis=-1, keepdims=True)
    spread = jnp.mean(center * center, axis=-1, keepdims=True)
    return center * lax.rsqrt(spread + 1e-05) * gain + shift


def gelu_tanh(values):
    return jax.nn.gelu(values, approximate=True)


def fill_mask(mask_ref, length):
    row = lax.broadcasted_iota(jnp.int32, mask_ref.shape, 0)
    column = lax.broadcasted_iota(jnp.int32, mask_ref.shape, 1)
    mask_ref[...] = jnp.where((column <= row) & (column < length), 0.0, -1e30)


def masked_scores(query, key, mask):
    scores = lax.dot_general(
        query * 0.125, key, (((1,), (1,)), ((), ())), preferred_element_type=jnp.float32
    )
    return scores + mask


def softmax_rows(scores):
    top = jnp.max(scores, axis=-1, keepdims=True)
    raised = jnp.exp(scores - top)
    return raised * (1.0 / jnp.sum(raised, axis=-1, keepdims=True))


def attend_body(length_ref, query_ref, key_ref, value_ref, mixed_ref, mask_ref):
    @pl.when(pl.program_id(0) == 0)
    def _():
        fill_mask(mask_ref, length_ref[0])

    rows = query_ref.shape[0]
    block = rows // 2
    for head in range(2):
        lanes = slice(head * HD, (head + 1) * HD)
        for at in range(2):
            here, seen = slice(at * block, (at + 1) * block), slice(0, (at + 1) * block)
            scores = masked_scores(
                query_ref[here, lanes], key_ref[seen, lanes], mask_ref[here, seen]
            )
            probs = softmax_rows(scores).astype(jnp.bfloat16)
            mixed_ref[here, lanes] = jnp.dot(
                probs, value_ref[seen, lanes], preferred_element_type=jnp.float32
            ).astype(jnp.bfloat16)


def attend(projected, seq_lengths):
    rows = projected.shape[0]
    pairs = HEADS // 2
    return pl.pallas_call(
        attend_body,
        grid=(pairs,),
        out_shape=jax.ShapeDtypeStruct((rows, D), jnp.bfloat16),
        in_specs=[
            pl.BlockSpec(memory_space=pltpu.SMEM),
            pl.BlockSpec((rows, 2 * HD), lambda p: (0, p)),
            pl.BlockSpec((rows, 2 * HD), lambda p: (0, pairs + p)),
            pl.BlockSpec((rows, 2 * HD), lambda p: (0, 2 * pairs + p)),
        ],
        out_specs=pl.BlockSpec((rows, 2 * HD), lambda p: (0, p)),
        scratch_shapes=[pltpu.VMEM((rows, rows), jnp.float32)],
        compiler_params=pltpu.CompilerParams(vmem_limit_bytes=32 * 1024 * 1024),
        cost_estimate=pl.CostEstimate(
            flops=4 * HEADS * rows * rows * HD, bytes_accessed=8 * rows * D, transcendentals=0
        ),
    )(seq_lengths, projected, projected, projected)


def attend_back_body(length_ref, query_ref, key_ref, value_ref, grad_ref, out_ref, mask_ref):
    @pl.when(pl.program_id(0) == 0)
    def _():
        fill_mask(mask_ref, length_ref[0])

    rows = query_ref.shape[0]
    block = rows // 2
    pair = pl.program_id(0)
    low = jnp.bfloat16
    columns = (((0,), (0,)), ((), ()))
    across = (((1,), (1,)), ((), ()))
    grads = []
    for head in range(2):
        lanes = slice(head * HD, (head + 1) * HD)
        grad_query, grad_key, grad_value = [], [], []
        for at in range(2):
            here, seen = slice(at * block, (at + 1) * block), slice(0, (at + 1) * block)
            query, key = query_ref[here, lanes], key_ref[seen, lanes]
            grad = grad_ref[here, lanes]
            probs = softmax_rows(masked_scores(query, key, mask_ref[here, seen]))
            grad_probs = lax.dot_general(
                grad, value_ref[seen, lanes], across, preferred_element_type=jnp.float32
            )
            grad_value.append(
                lax.dot_general(
                    probs.astype(low), grad, columns, preferred_element_type=jnp.float32
                )
            )
            row_dot = jnp.sum(grad_probs * probs, axis=-1, keepdims=True)
            scores_low = (probs * (grad_probs - row_dot)).astype(low)
            grad_query.append(jnp.dot(scores_low, key, preferred_element_type=jnp.float32) * 0.125)
            grad_key.append(
                lax.dot_general(scores_low, query, columns, preferred_element_type=jnp.float32)
                * 0.125
            )
        joined = []
        for parts in (grad_key, grad_value):
            joined.append(jnp.concatenate([parts[0] + parts[1][:block], parts[1][block:]]))
        grads.append((jnp.concatenate(grad_query), joined[0], joined[1]))
    for part in range(3):
        window = pl.ds(pl.multiple_of(part * D + pair * 2 * HD, 2 * HD), 2 * HD)
        out_ref[:, window] = jnp.concatenate(
            [grads[0][part].astype(low), grads[1][part].astype(low)], axis=1
        )


def attend_back(projected, grad_mixed, seq_lengths):
    rows = projected.shape[0]
    pairs = HEADS // 2
    return pl.pallas_call(
        attend_back_body,
        grid=(pairs,),
        out_shape=jax.ShapeDtypeStruct((rows, 3 * D), jnp.bfloat16),
        in_specs=[
            pl.BlockSpec(memory_space=pltpu.SMEM),
            pl.BlockSpec((rows, 2 * HD), lambda p: (0, p)),
            pl.BlockSpec((rows, 2 * HD), lambda p: (0, pairs + p)),
            pl.BlockSpec((rows, 2 * HD), lambda p: (0, 2 * pairs + p)),
            pl.BlockSpec((rows, 2 * HD), lambda p: (0, p)),
        ],
        out_specs=pl.BlockSpec((rows, 3 * D), lambda p: (0, 0)),
        scratch_shapes=[pltpu.VMEM((rows, rows), jnp.float32)],
        compiler_params=pltpu.CompilerParams(vmem_limit_bytes=48 * 1024 * 1024),
        cost_estimate=pl.CostEstimate(
            flops=10 * HEADS * rows * rows * HD, bytes_accessed=16 * rows * D, transcendentals=0
        ),
    )(seq_lengths, projected, projected, projected, grad_mixed)


def layer_forward(stream, weights, vector, seq_lengths):
    w_qkv, w_out, w_fc, w_proj = weights
    normed_low = layer_norm(stream, vector[0:D], vector[D : 2 * D]).astype(jnp.bfloat16)
    qkv_bias = jnp.concatenate(
        [vector[4 * D : 5 * D], jnp.zeros((D,), jnp.float32), vector[5 * D : 6 * D]]
    )
    projected = (jnp.dot(normed_low, w_qkv, preferred_element_type=jnp.float32) + qkv_bias).astype(
        jnp.bfloat16
    )
    mixed_low = attend(projected, seq_lengths)
    stream_mid = (
        stream
        + jnp.dot(mixed_low, w_out, preferred_element_type=jnp.float32)
        + vector[6 * D : 7 * D]
    )
    normed_two = layer_norm(stream_mid, vector[2 * D : 3 * D], vector[3 * D : 4 * D]).astype(
        jnp.bfloat16
    )
    hidden_pre = (
        jnp.dot(normed_two, w_fc, preferred_element_type=jnp.float32) + vector[8 * D : 8 * D + FF]
    )
    hidden_low = gelu_tanh(hidden_pre).astype(jnp.bfloat16)
    stream_out = (
        stream_mid
        + jnp.dot(hidden_low, w_proj, preferred_element_type=jnp.float32)
        + vector[7 * D : 8 * D]
    )
    return (
        stream_out,
        (
            stream,
            normed_low,
            projected,
            mixed_low,
            stream_mid,
            normed_two,
            hidden_pre,
            hidden_low,
        ),
    )


def layer_backward(grad_out, saved_acts, weights, vector, seq_lengths):
    (
        stream,
        normed_low,
        projected,
        mixed_low,
        stream_mid,
        normed_two,
        hidden_pre,
        hidden_low,
    ) = saved_acts
    w_qkv, w_out, w_fc, w_proj = weights
    branch_low = grad_out.astype(jnp.bfloat16)
    grad_wproj = jnp.dot(hidden_low.T, branch_low, preferred_element_type=jnp.bfloat16)
    grad_hidden = jnp.dot(branch_low, w_proj.T, preferred_element_type=jnp.float32)
    pre_low = jax.vjp(gelu_tanh, hidden_pre)[1](grad_hidden)[0].astype(jnp.bfloat16)
    grad_wfc = jnp.dot(normed_two.T, pre_low, preferred_element_type=jnp.bfloat16)
    grad_normed_two = jnp.dot(pre_low, w_fc.T, preferred_element_type=jnp.float32)
    grad_mid, grad_gain_two, grad_shift_two = jax.vjp(
        layer_norm, stream_mid, vector[2 * D : 3 * D], vector[3 * D : 4 * D]
    )[1](grad_normed_two)
    grad_mid = grad_mid + grad_out
    attn_low = grad_mid.astype(jnp.bfloat16)
    grad_wout = jnp.dot(mixed_low.T, attn_low, preferred_element_type=jnp.bfloat16)
    grad_mixed = jnp.dot(attn_low, w_out.T, preferred_element_type=jnp.float32).astype(
        jnp.bfloat16
    )
    qkv_low = attend_back(projected, grad_mixed, seq_lengths)
    grad_wqkv = jnp.dot(normed_low.T, qkv_low, preferred_element_type=jnp.bfloat16)
    grad_normed = jnp.dot(qkv_low, w_qkv.T, preferred_element_type=jnp.float32)
    grad_input, grad_gain_one, grad_shift_one = jax.vjp(
        layer_norm, stream, vector[0:D], vector[D : 2 * D]
    )[1](grad_normed)
    bias_qkv = jnp.sum(qkv_low.astype(jnp.float32), axis=0)
    grad_vector = jnp.concatenate(
        [
            grad_gain_one,
            grad_shift_one,
            grad_gain_two,
            grad_shift_two,
            bias_qkv[0:D],
            bias_qkv[2 * D : 3 * D],
            jnp.sum(attn_low.astype(jnp.float32), axis=0),
            jnp.sum(branch_low.astype(jnp.float32), axis=0),
            jnp.sum(pre_low.astype(jnp.float32), axis=0),
        ]
    )
    return (grad_input + grad_mid, (grad_wqkv, grad_wout, grad_wfc, grad_wproj), grad_vector)


def adamw(weight, moment_one, moment_two, gradient, step_rate, decay_rate, step_float):
    one_new = 0.5 * moment_one + 0.5 * gradient
    two_new = 0.5 * moment_two + 0.5 * gradient * gradient
    fix_scale = 1.0 - jnp.power(0.5, step_float)
    update = one_new / fix_scale / (jnp.sqrt(two_new / fix_scale) + 1e-08)
    return (weight - step_rate * (update + decay_rate * weight), one_new, two_new)


def on_device(
    token_ids,
    seq_lengths,
    loss_slots,
    target_ids,
    step_count,
    w_qkv,
    w_out,
    w_fc,
    w_proj,
    vectors,
    pos_table,
    embed_table,
    mom_qkv,
    mom_out,
    mom_fc,
    mom_proj,
    mom_vectors,
    mom_pos,
    mom_embed,
    sec_qkv,
    sec_out,
    sec_fc,
    sec_proj,
    sec_vectors,
    sec_pos,
    sec_embed,
):
    per_layer = 8 * D + FF
    net = Net()
    size, halves = net.size, net.halves
    same_core = halves * size
    devices = 2 * same_core
    low = jnp.bfloat16
    near = LEN // 2
    fused = size <= 8
    rest = LEN - near
    slots = loss_slots.shape[0]

    half_of = jnp.arange(halves)[:, None]
    wide_index = jnp.arange(size)[None, :]
    place_of = jnp.where(wide_index % 2 == 0, wide_index // 2, size - 1 - (wide_index - 1) // 2)
    to_device = ((half_of ^ net.half) * size + (place_of - net.place) % size).reshape(-1)
    offsets = (net.place + wide_index) % size
    wide_there = jnp.where(offsets < size // 2, 2 * offsets, 2 * (size - 1 - offsets) + 1)
    from_device = ((half_of ^ net.half) * size + wide_there).reshape(-1)

    numbers = jnp.concatenate([token_ids, loss_slots, target_ids, seq_lengths])
    numbers = jnp.pad(numbers, (0, -numbers.shape[0] % 1024)).reshape(-1, 128)
    numbers = cast_call(size, numbers, False, 5).reshape(same_core, -1)
    numbers = jnp.take(numbers, from_device, axis=0).reshape(halves, size, -1)
    group_tokens = numbers[:, :, :LEN]
    group_slots = numbers[:, :, LEN : LEN + slots].reshape(same_core * slots)
    group_targets = numbers[:, :, LEN + slots : LEN + 2 * slots].reshape(same_core * slots)
    core_total = jnp.sum(numbers[:, :, LEN + 2 * slots].astype(jnp.float32))
    token_total = core_total + net.swap_core(core_total[None])[0]

    own_rows = embed_table.shape[0]
    height = own_rows + -own_rows % 64
    chip_rows = 2 * height
    table_own = jnp.pad(embed_table.astype(low), ((0, height - own_rows), (0, 0)))
    own_start = net.device * own_rows
    other_start = (net.device + (1 - 2 * net.core) * size) * own_rows

    def locate(ids):
        mine = ids - own_start
        other = ids - other_start
        return jnp.where(
            (mine >= 0) & (mine < own_rows),
            mine,
            jnp.where((other >= 0) & (other < own_rows), other + height, -1),
        )

    def one_hot(ids):
        return (ids[:, None] == jnp.arange(chip_rows)[None, :]).astype(low)

    local_tokens = locate(group_tokens).reshape(same_core, LEN)
    ids_near, ids_rest = local_tokens[:, :near], local_tokens[:, near:]

    shared = pos_table.shape[0]
    vector_rows = -(-vectors.shape[0] // D)
    padded = jnp.pad(vectors, (0, vector_rows * D - vectors.shape[0])).reshape(vector_rows, D)
    spare = -(shared + vector_rows) % 16
    small_own = jnp.concatenate([pos_table, padded, jnp.zeros((spare, D), jnp.float32)])
    shards_low = []
    for layer_at in range(LAYERS):
        shards_low += [part[layer_at].astype(low) for part in (w_qkv, w_fc, w_proj, w_out)]
    shards_low.append(small_own.astype(low))
    ring_first = (True, True, False, False) * LAYERS + (False,)
    if fused:
        *gathered, table_low, found = look_up_call(
            size, shards_low, ring_first, table_own, jnp.concatenate([ids_near, ids_rest])[..., None], 1
        )
        stream = scatter_call(
            size, [found, found], (True, False), False, low, 2, ((0, 1), (same_core, 1))
        )
        stream = jnp.concatenate(stream)
    else:
        gathered = gather_call(size, shards_low, ring_first, True, 1)
        table_low = jnp.concatenate([table_own, net.swap_core(table_own)])
        found = [
            jnp.dot(
                one_hot(ids.reshape(-1)), table_low, preferred_element_type=jnp.float32
            ).astype(low).reshape(same_core, -1, D)
            for ids in (ids_near, ids_rest)
        ]
        bands = max(1, same_core // 16)
        band = D // bands
        parts = []
        for at in range(bands):
            window = [part[:, :, at * band : (at + 1) * band] for part in found]
            parts.append(jnp.concatenate(scatter_call(size, window, (True, False), False, low, 2)))
        stream = jnp.concatenate(parts, axis=1)
    small_low = gathered[-1]
    pos_low = small_low[:, :shared].reshape(devices * shared, D)
    vector_all = (
        small_low[:, shared : shared + vector_rows]
        .reshape(devices, vector_rows * D)[:, : vectors.shape[0]]
        .reshape(-1)
        .astype(jnp.float32)
    )

    stream = stream.astype(jnp.float32) + pos_low[:LEN].astype(jnp.float32)

    kept_weights = []
    saved_list = []
    for layer_at in range(LAYERS):
        w_a, w_c, w_d, w_b = (
            part.reshape(-1, part.shape[2]) for part in gathered[layer_at * 4 : layer_at * 4 + 4]
        )
        weights = (w_a, w_b, w_c, w_d)
        kept_weights.append(weights)
        stream, saved_acts = layer_forward(
            stream, weights, vector_all[layer_at * per_layer : (layer_at + 1) * per_layer], seq_lengths
        )
        saved_list.append(saved_acts)
    tail_start = LAYERS * per_layer
    final_norm, final_pull = jax.vjp(
        layer_norm,
        stream,
        vector_all[tail_start : tail_start + D],
        vector_all[tail_start + D : tail_start + 2 * D],
    )
    slot_rows = jnp.maximum(loss_slots, 0)
    own_picked = final_norm[slot_rows].astype(low)
    some = slots // 2
    group_rows = jnp.concatenate(
        gather_call(size, [own_picked[:some], own_picked[some:]], (True, False), False, 6), axis=1
    ).reshape(same_core * slots, D)
    real = jnp.arange(chip_rows) % height < own_rows
    logits = jnp.where(
        real, jnp.dot(group_rows, table_low.T, preferred_element_type=jnp.float32), -1e30
    )
    target_onehot = locate(group_targets)[:, None] == jnp.arange(chip_rows)[None, :]
    row_max = jnp.max(logits, axis=-1)
    row_total = jnp.sum(jnp.exp(logits - row_max[:, None]), axis=-1)
    target_logit = jnp.sum(jnp.where(target_onehot, logits, 0.0), axis=-1)
    stats = jnp.stack([row_max, row_total, target_logit], axis=-1)
    stats = jnp.take(stats.reshape(same_core, slots * 3), to_device, axis=0)
    stats = stats.reshape(same_core * slots, 3).T.reshape(-1)
    entries = stats.shape[0]
    stats = jnp.pad(stats, (0, -entries % 1024)).reshape(-1, 128)
    stats = cast_call(size, stats, False, 7).reshape(same_core, -1)[:, :entries]
    stats = stats.reshape(same_core, 3, same_core * slots)
    joint_max = jnp.max(stats[:, 0], axis=0)
    joint_total = jnp.sum(stats[:, 1] * jnp.exp(stats[:, 0] - joint_max), axis=0)
    stats = jnp.stack([joint_max + jnp.log(joint_total), jnp.sum(stats[:, 2], axis=0)])
    stats = stats.reshape(2, same_core, slots)
    stats = jnp.take(stats, from_device, axis=1).reshape(2, same_core * slots)
    log_total, merged_target = stats[0], stats[1]
    group_used = (group_slots >= 0).astype(jnp.float32)
    own_loss = jnp.sum(((log_total - merged_target) * group_used)[:slots])
    grad_logits = (
        (jnp.exp(logits - log_total[:, None]) - target_onehot.astype(jnp.float32))
        * (group_used / token_total)[:, None]
    ).astype(low)
    grad_rows = jnp.dot(grad_logits, table_low, preferred_element_type=jnp.float32)
    grad_rows = grad_rows.reshape(2 * same_core, some, D)
    grad_rows = jnp.concatenate(
        scatter_call(
            size,
            [grad_rows, grad_rows],
            (True, False),
            False,
            jnp.float32,
            8,
            ((0, 2), (1, 2)),
        )
    )
    grad_final = jnp.zeros((LEN, D), jnp.float32).at[slot_rows].add(grad_rows)
    grad_stream, grad_gain_final, grad_shift_final = final_pull(grad_final)
    layer_shards = []
    vector_grads = []
    for layer_at in reversed(range(LAYERS)):
        grad_stream, full_grads, grad_vector = layer_backward(
            grad_stream,
            saved_list[layer_at],
            kept_weights[layer_at],
            vector_all[layer_at * per_layer : (layer_at + 1) * per_layer],
            seq_lengths,
        )
        grad_a, grad_b, grad_c, grad_d = full_grads
        shard_a, shard_c, shard_d, shard_b = scatter_call(
            size,
            [part.reshape(devices, -1, part.shape[1]) for part in (grad_a, grad_c, grad_d, grad_b)],
            (True, True, False, False),
            True,
            jnp.float32,
            3,
        )
        layer_shards.insert(0, (shard_a, shard_b, shard_c, shard_d))
        vector_grads.insert(0, grad_vector)
    grad_low = grad_stream.astype(low)
    grad_near, grad_rest = grad_low[:near], grad_low[near:]
    grad_table = jnp.dot(grad_logits.T, group_rows, preferred_element_type=jnp.float32)
    if fused:
        ids = [part[:, None] for part in (ids_near, ids_rest)]
        grad_table, grad_pos = spread_call(size, grad_near, grad_rest, ids, grad_table, 4)
    else:
        wholes = gather_call(size, [grad_near, grad_rest], (True, False), False, 4)
        for ids, whole in zip((ids_near, ids_rest), wholes):
            grad_table = grad_table + jnp.dot(
                one_hot(ids.reshape(-1)).T, whole.reshape(-1, D), preferred_element_type=jnp.float32
            )
        grad_table = grad_table[:height] + net.swap_core(grad_table[height:])
        grad_pos = jnp.concatenate(
            [jnp.sum(whole.astype(jnp.float32), axis=0) for whole in wholes]
        )
    table_shard = grad_table[:own_rows]
    grad_pos = jnp.pad(grad_pos, ((0, POS - LEN), (0, 0)))
    other_device = net.device + (1 - 2 * net.core) * size
    pos_shard = lax.dynamic_slice_in_dim(grad_pos, net.device * shared, shared) + net.swap_core(
        lax.dynamic_slice_in_dim(grad_pos, other_device * shared, shared)
    )
    grad_small = jnp.concatenate(vector_grads + [grad_gain_final, grad_shift_final])
    small_shard = net.reduce_rows(
        grad_small.reshape(devices * 2, -1), False, jnp.float32
    ).reshape(-1)
    qkv_shard = jnp.stack([member[0] for member in layer_shards])
    out_shard = jnp.stack([member[1] for member in layer_shards])
    fc_shard = jnp.stack([member[2] for member in layer_shards])
    proj_shard = jnp.stack([member[3] for member in layer_shards])
    shards = (qkv_shard, out_shard, fc_shard, proj_shard, small_shard, pos_shard, table_shard)
    squares = jnp.sum(jnp.stack([jnp.sum(member * member) for member in shards]))
    sums = jnp.pad(jnp.stack([own_loss, squares]), (0, 1022)).reshape(8, 128)
    sums = jnp.sum(cast_call(size, sums, True, 9), axis=0)
    loss_total, square_total = sums[0, 0], sums[0, 1]
    loss_value = loss_total / token_total
    grad_norm = jnp.sqrt(square_total)
    factor = CLIP_LIMIT / jnp.maximum(grad_norm, CLIP_LIMIT)
    step_float = step_count.astype(jnp.float32)
    params = (w_qkv, w_out, w_fc, w_proj, vectors, pos_table, embed_table)
    moments_one = (mom_qkv, mom_out, mom_fc, mom_proj, mom_vectors, mom_pos, mom_embed)
    moments_two = (sec_qkv, sec_out, sec_fc, sec_proj, sec_vectors, sec_pos, sec_embed)
    step_rates = (
        RATE_MATRIX,
        RATE_MATRIX,
        RATE_MATRIX,
        RATE_MATRIX,
        RATE_VECTOR,
        RATE_MATRIX,
        RATE_MATRIX,
    )
    decay_rates = (
        DECAY_MATRIX,
        DECAY_MATRIX,
        DECAY_MATRIX,
        DECAY_MATRIX,
        0.0,
        DECAY_MATRIX,
        DECAY_MATRIX,
    )
    results = [
        adamw(
            params[where_at],
            moments_one[where_at],
            moments_two[where_at],
            shards[where_at] * factor,
            step_rates[where_at],
            decay_rates[where_at],
            step_float,
        )
        for where_at in range(7)
    ]
    return (
        loss_value,
        grad_norm,
        results[0][0],
        results[1][0],
        results[2][0],
        results[3][0],
        results[4][0],
        results[5][0],
        results[6][0],
        results[0][1],
        results[1][1],
        results[2][1],
        results[3][1],
        results[4][1],
        results[5][1],
        results[6][1],
        results[0][2],
        results[1][2],
        results[2][2],
        results[3][2],
        results[4][2],
        results[5][2],
        results[6][2],
    )


def solution(mesh):
    return jax.shard_map(
        on_device,
        mesh=mesh,
        in_specs=(
            P(("narrow", "wide")),
            P(("narrow", "wide")),
            P(("narrow", "wide")),
            P(("narrow", "wide")),
            P(),
            P(None, ("narrow", "wide"), None),
            P(None, ("narrow", "wide"), None),
            P(None, ("narrow", "wide"), None),
            P(None, ("narrow", "wide"), None),
            P(("narrow", "wide")),
            P(("narrow", "wide"), None),
            P(("narrow", "wide"), None),
            P(None, ("narrow", "wide"), None),
            P(None, ("narrow", "wide"), None),
            P(None, ("narrow", "wide"), None),
            P(None, ("narrow", "wide"), None),
            P(("narrow", "wide")),
            P(("narrow", "wide"), None),
            P(("narrow", "wide"), None),
            P(None, ("narrow", "wide"), None),
            P(None, ("narrow", "wide"), None),
            P(None, ("narrow", "wide"), None),
            P(None, ("narrow", "wide"), None),
            P(("narrow", "wide")),
            P(("narrow", "wide"), None),
            P(("narrow", "wide"), None),
        ),
        out_specs=(
            P(),
            P(),
            P(None, ("narrow", "wide"), None),
            P(None, ("narrow", "wide"), None),
            P(None, ("narrow", "wide"), None),
            P(None, ("narrow", "wide"), None),
            P(("narrow", "wide")),
            P(("narrow", "wide"), None),
            P(("narrow", "wide"), None),
            P(None, ("narrow", "wide"), None),
            P(None, ("narrow", "wide"), None),
            P(None, ("narrow", "wide"), None),
            P(None, ("narrow", "wide"), None),
            P(("narrow", "wide")),
            P(("narrow", "wide"), None),
            P(("narrow", "wide"), None),
            P(None, ("narrow", "wide"), None),
            P(None, ("narrow", "wide"), None),
            P(None, ("narrow", "wide"), None),
            P(None, ("narrow", "wide"), None),
            P(("narrow", "wide")),
            P(("narrow", "wide"), None),
            P(("narrow", "wide"), None),
        ),
        check_vma=False,
    )
```

```python
import functools

import jax
import jax.numpy as jnp
from jax import lax
from jax.experimental import pallas as pl
from jax.experimental.pallas import tpu as pltpu
from jax.sharding import PartitionSpec as P

D = 1024
HEADS = 16
HD = 64
FF = 4096
POS = 1024
LAYERS = 2
LEN = 512
LOSS_DEV = 32


CLIP_LIMIT = 0.002
RATE_MATRIX = 0.03
RATE_VECTOR = 0.3
DECAY_MATRIX = 0.1


class Net:
    def __init__(self):
        self.narrow_at = lax.axis_index("narrow")
        self.wide_at = lax.axis_index("wide")
        self.narrow_size = lax.axis_size("narrow")
        self.size = lax.axis_size("wide")
        size = self.size
        self.core = self.narrow_at % 2
        self.half = self.narrow_at // 2
        self.halves = self.narrow_size // 2
        self.place = jnp.where(
            self.wide_at % 2 == 0, self.wide_at // 2, size - 1 - (self.wide_at - 1) // 2
        )
        self.device = self.narrow_at * size + self.wide_at
        order = list(range(0, size, 2)) + list(range(size - 1, 0, -2))
        pairs = [(n, w) for n in range(self.narrow_size) for w in range(size)]
        self.core_pairs = [(n * size + w, (n ^ 1) * size + w) for n, w in pairs]
        self.half_pairs = [(n * size + w, (n ^ 2) * size + w) for n, w in pairs]
        self.right = [
            (n * size + order[i], n * size + order[(i + 1) % size])
            for n in range(self.narrow_size)
            for i in range(size)
        ]
        self.left = [(later, earlier) for earlier, later in self.right]

    def step(self, array, pairs):
        return lax.ppermute(array, ("narrow", "wide"), pairs)

    def swap_core(self, array):
        return self.step(array, self.core_pairs)

    def swap_half(self, array):
        return self.step(array, self.half_pairs)

    def wide_of(self, offset):
        size = self.size
        at = lax.rem(self.place + offset, size)
        return jnp.where(at < size // 2, 2 * at, 2 * (size - 1 - at) + 1)


MESH = pl.DeviceIdType.MESH


class Spot:
    def __init__(self, size):
        self.size = size
        narrow, wide = lax.axis_index("narrow"), lax.axis_index("wide")
        odd = lax.rem(wide, 2)
        self.core, self.half = lax.rem(narrow, 2), lax.div(narrow, 2)
        self.wide = wide
        self.place = (1 - odd) * lax.div(wide, 2) + odd * (size - 1 - lax.div(wide, 2))
        self.to_core = (narrow + 1 - 2 * self.core, wide)
        self.to_half = (narrow + 2 - 4 * self.half, wide)
        self.right = (narrow, self.wide_of(1))
        self.left = (narrow, self.wide_of(size - 1))

    def wide_of(self, offset):
        at = lax.rem(self.place + offset, self.size)
        late = lax.div(at, self.size // 2)
        return (1 - late) * 2 * at + late * (2 * (self.size - 1 - at) + 1)

    def index(self, turned, other_core, offset):
        half = self.half + turned * (1 - 2 * self.half)
        core = self.core + other_core * (1 - 2 * self.core)
        return (2 * half + core) * self.size + self.wide_of(offset)

    def meet(self, with_core):
        barrier = pltpu.get_barrier_semaphore()
        peers = [self.to_half, self.right, self.left] + ([self.to_core] if with_core else [])
        for peer in peers:
            pl.semaphore_signal(barrier, inc=1, device_id=peer, device_id_type=MESH)
        pl.semaphore_wait(barrier, len(peers))


def cut_of(rows):
    return rows // 2 if rows % 32 == 0 else rows


def gather_steps(size, ring_first, across, shards, wholes, sems, spot, tick, ready):
    count = len(ring_first)
    ring_sem, half_sem, core_sem, send_sem, local_sem = sems
    far = size // 2

    def index(turned, offset, toward=None):
        if across:
            return spot.index(turned, 0, offset % size)
        if toward == "half":
            turned = 1 - turned
        offset = offset + {"right": -1, "left": 1}.get(toward, 0)
        return turned * size + offset % size

    def send(at, source, turned, offset, toward, sem, rows=None):
        target = wholes[at].at[index(turned, offset, toward)]
        if rows is not None:
            source, target = source.at[rows], target.at[rows]
        device = {
            "half": spot.to_half,
            "right": spot.right,
            "left": spot.left,
            "core": spot.to_core,
        }[toward]
        pltpu.make_async_remote_copy(
            src_ref=source,
            dst_ref=target,
            send_sem=send_sem.at[at],
            recv_sem=sem,
            device_id=device,
            device_id_type=MESH,
        ).start()

    def landed(region, sem):
        pltpu.make_async_copy(region, region, sem).wait()

    def piece(at, turned, offset):
        return wholes[at].at[index(turned, offset)]

    def on_core(at, source, turned, offset):
        if across:
            send(at, source, turned, offset, "core", core_sem.at[at])

    def on_ring(at, turned, source, offset, way, step, rows=None):
        toward = ("right", "left")[way]
        send(at, source, turned, offset, toward, ring_sem.at[at, turned, way, step], rows)

    locals_ = []
    for at in range(count):
        copy = pltpu.make_async_copy(shards[at], piece(at, 0, 0), local_sem.at[at])
        copy.start()
        locals_.append(copy)
    for at in range(count):
        if not ring_first[at]:
            send(at, shards[at], 0, 0, "half", half_sem.at[at, 0])
    for at in range(count):
        if ring_first[at]:
            on_ring(at, 0, shards[at], 0, 0, 1)
            on_ring(at, 0, shards[at], 0, 1, 1)
            send(at, shards[at], 0, 0, "half", half_sem.at[at, 0])
    for at in range(count):
        on_core(at, shards[at], 0, 0)
    for at in range(count):
        if not ring_first[at]:
            landed(piece(at, 1, 0), half_sem.at[at, 0])
            for way in (0, 1):
                on_ring(at, 0, shards[at], 0, way, 1)
                on_ring(at, 1, piece(at, 1, 0), 0, way, 1)
            on_core(at, piece(at, 1, 0), 1, 0)
    for at in range(count):
        locals_[at].wait()
        ready(at, 0, 0)
        if not ring_first[at]:
            ready(at, 1, 0)
        tick()

    def turned_arrivals(at, step):
        offsets = (0,) if step == 0 else (far,) if step == far else (-step, step)
        for offset in offsets:
            landed(piece(at, 1, offset), half_sem.at[at, offset % size])
            on_core(at, piece(at, 1, offset), 1, offset)
            came.append((at, 1, offset))

    came = []

    def flush():
        for one in came:
            ready(*one)
        came.clear()
        tick()

    for step in range(1, far + 1):
        for at in range(count):
            rows = shards[at].shape[0]
            cut = cut_of(rows)
            if ring_first[at]:
                if step < far:
                    for way in (0, 1):
                        offset = (-step, step)[way]
                        here = piece(at, 0, offset)
                        landed(here, ring_sem.at[at, 0, way, step])
                        if step < far - 1:
                            on_ring(at, 0, here, offset, way, step + 1)
                        elif way == 0:
                            on_ring(at, 0, here, offset, way, step + 1, pl.ds(0, cut))
                        elif cut < rows:
                            on_ring(at, 0, here, offset, way, step + 1, pl.ds(cut, rows - cut))
                        send(at, here, 0, offset, "half", half_sem.at[at, offset % size])
                        on_core(at, here, 0, offset)
                        came.append((at, 0, offset))
                else:
                    here = piece(at, 0, far)
                    landed(here.at[pl.ds(0, cut)], ring_sem.at[at, 0, 0, step])
                    if cut < rows:
                        landed(here.at[pl.ds(cut, rows - cut)], ring_sem.at[at, 0, 1, step])
                    send(at, here, 0, far, "half", half_sem.at[at, far])
                    on_core(at, here, 0, far)
                    came.append((at, 0, far))
                turned_arrivals(at, step - 1)
            else:
                for way in (0, 1):
                    for turned in (0, 1):
                        if step == far and turned != way:
                            continue
                        offset = (-step, step)[way]
                        here = piece(at, turned, offset)
                        landed(here, ring_sem.at[at, turned, way, step])
                        if step < far - 1 or (step == far - 1 and turned == way):
                            on_ring(at, turned, here, offset, way, step + 1)
                        on_core(at, here, turned, offset)
                        came.append((at, turned, offset))
            flush()
    for at in range(count):
        if ring_first[at]:
            turned_arrivals(at, far)
            flush()
    for at in range(count):
        if across:
            landed(wholes[at].at[pl.ds(0, 2 * size)], core_sem.at[at])
        sent = 4 * size - 1 if across else 2 * size - 1
        landed(wholes[at].at[pl.ds(0, sent)], send_sem.at[at])


def gather_sems(count, size):
    return [
        pltpu.SemaphoreType.DMA((count, 2, 2, size // 2 + 1)),
        pltpu.SemaphoreType.DMA((count, size)),
        pltpu.SemaphoreType.DMA((count,)),
        pltpu.SemaphoreType.DMA((count,)),
        pltpu.SemaphoreType.DMA((count,)),
    ]


def look_up_body(size, ring_first, *refs):
    count = len(ring_first)
    shards, (table_own, ids) = refs[:count], refs[count : count + 2]
    refs = refs[count + 2 :]
    wholes, (table_out, found) = refs[:count], refs[count : count + 2]
    table, hot, stage, table_sem, stage_sem, *sems = refs[count + 2 :]
    spot = Spot(size)
    spot.meet(True)
    height = table_own.shape[0]
    mine = pltpu.make_async_copy(table_own, table.at[pl.ds(0, height)], table_sem.at[0])
    mine.start()
    swap = pltpu.make_async_remote_copy(
        src_ref=table_own,
        dst_ref=table.at[pl.ds(height, height)],
        send_sem=table_sem.at[1],
        recv_sem=table_sem.at[2],
        device_id=spot.to_core,
        device_id_type=MESH,
    )
    swap.start()
    out = pltpu.make_async_copy(table, table_out, table_sem.at[3])
    pieces, rows = found.shape[:2]
    width = 256
    state = {"ticks": 0, "done": 0}

    def copy_out(number):
        slot = lax.rem(number, 2)
        return pltpu.make_async_copy(stage.at[slot], found.at[number], stage_sem.at[slot])

    def work(first, last):
        def one(number, nothing):
            columns = lax.broadcasted_iota(jnp.int32, (rows, 2 * height), 1)
            hot[...] = jnp.where(columns == ids[number], 1.0, 0.0).astype(jnp.bfloat16)

            @pl.when(number >= 2)
            def _():
                copy_out(number - 2).wait()

            def part(at, nothing):
                window = pl.ds(pl.multiple_of(at * width, width), width)
                stage[lax.rem(number, 2), :, window] = jnp.dot(
                    hot[...], table[:, window], preferred_element_type=jnp.float32
                ).astype(jnp.bfloat16)
                return nothing

            lax.fori_loop(0, D // width, part, 0)
            copy_out(number).start()
            return nothing

        lax.fori_loop(first, last, one, 0)

    def tick(share=1):
        if state["done"] == pieces:
            return
        if state["done"] == 0:
            mine.wait()
            swap.wait_recv()
            out.start()
        last = min(pieces, state["done"] + share)
        work(state["done"], last)
        state["done"] = last

    gather_steps(
        size, ring_first, True, shards, wholes, sems, spot, tick, lambda at, turned, offset: None
    )
    tick(pieces)
    copy_out(pieces - 2).wait()
    copy_out(pieces - 1).wait()
    out.wait()
    swap.wait_send()


def look_up_call(size, shards, ring_first, table_own, ids, number):
    count = len(shards)
    height = table_own.shape[0]
    found = ids.shape[:2] + (D,)
    outs = [jax.ShapeDtypeStruct((4 * size,) + a.shape, a.dtype) for a in shards]
    outs.append(jax.ShapeDtypeStruct((2 * height, D), table_own.dtype))
    outs.append(jax.ShapeDtypeStruct(found, table_own.dtype))
    return pl.pallas_call(
        functools.partial(look_up_body, size, ring_first),
        out_shape=outs,
        in_specs=[pl.BlockSpec(memory_space=pl.ANY)] * (count + 1)
        + [pl.BlockSpec(memory_space=pltpu.VMEM)],
        out_specs=[pl.BlockSpec(memory_space=pl.ANY)] * (count + 2),
        scratch_shapes=[
            pltpu.VMEM((2 * height, D), table_own.dtype),
            pltpu.VMEM((ids.shape[1], 2 * height), table_own.dtype),
            pltpu.VMEM((2,) + found[1:], table_own.dtype),
            pltpu.SemaphoreType.DMA((4,)),
            pltpu.SemaphoreType.DMA((2,)),
        ]
        + gather_sems(count, size),
        compiler_params=pltpu.CompilerParams(
            collective_id=number, has_side_effects=True, vmem_limit_bytes=48 * 1024 * 1024
        ),
    )(*shards, table_own, ids)


def spread_body(size, *refs):
    near, rest, ids_near, ids_rest, start = refs[:5]
    table_out, place_out, squares_ref = refs[5:8]
    near_all, rest_all, total, core_in, table_sem, *sems = refs[8:]
    ids = (ids_near, ids_rest)
    wholes = (near_all, rest_all)
    spot = Spot(size)
    spot.meet(True)
    height = table_out.shape[0]
    block = 2 * height // 8
    first = pltpu.make_async_copy(start, total, table_sem.at[0])
    first.start()
    place_out[...] = jnp.zeros_like(place_out)
    waiting = []

    def spread(pieces, blocks):
        def one(number, nothing):
            window = pl.ds(pl.multiple_of(number * block, 16), block)
            row = number * block + lax.broadcasted_iota(jnp.int32, (block, near.shape[0]), 0)
            value = total[window, :]
            for at, piece in pieces:
                hot = jnp.where(row == ids[at][piece], 1.0, 0.0).astype(jnp.bfloat16)
                value = value + jnp.dot(
                    hot, wholes[at][piece], preferred_element_type=jnp.float32
                )
            total[window, :] = value
            return nothing

        lax.fori_loop(blocks[0], blocks[1], one, 0)

    def place(pieces):
        for at, piece in pieces:
            rows = pl.ds(at * near.shape[0], near.shape[0])
            place_out[rows, :] += wholes[at][piece].astype(jnp.float32)

    def ready(at, turned, offset):
        waiting.append((at, turned * size + offset % size))

    def tick():
        if tick.first:
            first.wait()
            tick.first = False
        if len(waiting) >= 4:
            spread(waiting, (0, 8))
            place(waiting)
            waiting.clear()

    tick.first = True
    gather_steps(size, (True, False), False, (near, rest), wholes, sems, spot, tick, ready)
    if waiting:
        spread(waiting, (4, 8))
    swap = pltpu.make_async_remote_copy(
        src_ref=total.at[pl.ds(height, height)],
        dst_ref=core_in,
        send_sem=table_sem.at[1],
        recv_sem=table_sem.at[2],
        device_id=spot.to_core,
        device_id_type=MESH,
    )
    swap.start()
    if waiting:
        spread(waiting, (0, 4))
        place(waiting)
    swap.wait_recv()
    step = height // 4

    def add(number, squares):
        window = pl.ds(pl.multiple_of(number * step, 16), step)
        value = total[window, :] + core_in[window, :]
        total[window, :] = value
        return squares + jnp.sum(value * value, axis=0, keepdims=True)

    squares = lax.fori_loop(0, 4, add, jnp.zeros((1, D), jnp.float32))
    squares_ref[...] = jnp.broadcast_to(squares, squares_ref.shape)
    out = pltpu.make_async_copy(total.at[pl.ds(0, height)], table_out, table_sem.at[0])
    out.start()
    swap.wait_send()
    out.wait()


def spread_call(size, near, rest, ids, start, number):
    height = start.shape[0] // 2
    pieces = (2 * size,) + near.shape
    return pl.pallas_call(
        functools.partial(spread_body, size),
        out_shape=[
            jax.ShapeDtypeStruct((height, D), jnp.float32),
            jax.ShapeDtypeStruct((LEN, D), jnp.float32),
            jax.ShapeDtypeStruct((8, D), jnp.float32),
        ],
        in_specs=[pl.BlockSpec(memory_space=pl.ANY)] * 2
        + [pl.BlockSpec(memory_space=pltpu.VMEM)] * 2
        + [pl.BlockSpec(memory_space=pl.ANY)],
        out_specs=[
            pl.BlockSpec(memory_space=pl.ANY),
            pl.BlockSpec(memory_space=pltpu.VMEM),
            pl.BlockSpec(memory_space=pltpu.VMEM),
        ],
        scratch_shapes=[
            pltpu.VMEM(pieces, near.dtype),
            pltpu.VMEM(pieces, near.dtype),
            pltpu.VMEM((2 * height, D), jnp.float32),
            pltpu.VMEM((height, D), jnp.float32),
            pltpu.SemaphoreType.DMA((3,)),
        ]
        + gather_sems(2, size),
        compiler_params=pltpu.CompilerParams(
            collective_id=number, has_side_effects=True, vmem_limit_bytes=60 * 1024 * 1024
        ),
    )(near, rest, *ids, start)


def plain_gather_body(size, ring_first, across, *refs):
    count = len(ring_first)
    spot = Spot(size)
    spot.meet(across)
    gather_steps(
        size,
        ring_first,
        across,
        refs[:count],
        refs[count : 2 * count],
        refs[2 * count :],
        spot,
        lambda: None,
        lambda at, turned, offset: None,
    )


def gather_call(size, shards, ring_first, across, number):
    count = len(shards)
    total = (4 if across else 2) * size
    return pl.pallas_call(
        functools.partial(plain_gather_body, size, ring_first, across),
        out_shape=[jax.ShapeDtypeStruct((total,) + a.shape, a.dtype) for a in shards],
        in_specs=[pl.BlockSpec(memory_space=pl.ANY)] * count,
        out_specs=[pl.BlockSpec(memory_space=pl.ANY)] * count,
        scratch_shapes=gather_sems(count, size),
        compiler_params=pltpu.CompilerParams(collective_id=number, has_side_effects=True),
    )(*shards)


def cast_body(size, everyone, own_ref, out_ref, come_sem, send_sem, local_sem):
    spot = Spot(size)
    group = (4 if everyone else 2) * size
    narrow = lax.axis_index("narrow")
    mine = (narrow if everyone else spot.half) * size + spot.wide

    def device(step):
        at = lax.rem(mine + step, group)
        block = lax.div(at, size)
        return (block if everyone else 2 * block + spot.core, lax.rem(at, size))

    barrier = pltpu.get_barrier_semaphore()

    def greet(step, nothing):
        pl.semaphore_signal(barrier, inc=1, device_id=device(step), device_id_type=MESH)
        return nothing

    def tell(step, nothing):
        pltpu.make_async_remote_copy(
            src_ref=own_ref,
            dst_ref=out_ref.at[mine],
            send_sem=send_sem,
            recv_sem=come_sem,
            device_id=device(step),
            device_id_type=MESH,
        ).start()
        return nothing

    lax.fori_loop(1, group, greet, 0)
    keep = pltpu.make_async_copy(own_ref, out_ref.at[mine], local_sem)
    keep.start()
    pl.semaphore_wait(barrier, group - 1)
    lax.fori_loop(1, group, tell, 0)
    others = out_ref.at[pl.ds(0, group - 1)]
    pltpu.make_async_copy(others, others, come_sem).wait()
    pltpu.make_async_copy(others, others, send_sem).wait()
    keep.wait()


def cast_call(size, block, everyone, number):
    group = (4 if everyone else 2) * size
    return pl.pallas_call(
        functools.partial(cast_body, size, everyone),
        out_shape=jax.ShapeDtypeStruct((group,) + block.shape, block.dtype),
        in_specs=[pl.BlockSpec(memory_space=pltpu.VMEM)],
        out_specs=pl.BlockSpec(memory_space=pltpu.VMEM),
        scratch_shapes=[pltpu.SemaphoreType.DMA] * 3,
        compiler_params=pltpu.CompilerParams(collective_id=number, has_side_effects=True),
    )(block)


def scatter_body(size, half_first, across, bases, working, *refs):
    count = len(half_first)
    extra_in = FeedBack.INPUTS if working else 0
    extra_out = FeedBack.OUTPUTS if working else 0
    arrays, refs = refs[:count], refs[count:]
    work_in, refs = refs[:extra_in], refs[extra_in:]
    outs, squares_ref, refs = refs[:count], refs[count], refs[count + 1 :]
    work_out, refs = refs[:extra_out], refs[extra_out:]
    own, core_in, half_in, ring_in = (
        refs[part * count : (1 + part) * count] for part in range(4)
    )
    local_sem, core_sem, half_sem, ring_sem, send_sem = refs[4 * count : 4 * count + 5]
    work = FeedBack(work_in, work_out, refs[4 * count + 5 :]) if working else None
    squares = []
    spot = Spot(size)
    far = size // 2
    slots = [far] + [o for at in range(far - 1, 0, -1) for o in (at, -at)] + [0]
    sent = []

    def landed(region, sem):
        pltpu.make_async_copy(region, region, sem).wait()

    def send(source, target, device, number, at, sem):
        copy = pltpu.make_async_remote_copy(
            src_ref=source,
            dst_ref=target,
            send_sem=send_sem.at[at, number],
            recv_sem=sem,
            device_id=device,
            device_id_type=MESH,
        )
        copy.start()
        sent.append(copy)

    def source_of(at, turned, other_core, offset):
        if across:
            return arrays[at].at[spot.index(turned, other_core, offset % size)]
        base, stride = bases[at]
        return arrays[at].at[base + stride * (turned * size + offset % size)]

    def add(target, parts):
        rows, columns = target.shape
        width = 512 if columns % 512 == 0 else 256 if columns % 256 == 0 else 128

        def one(step, nothing):
            window = pl.ds(pl.multiple_of(step * width, width), width)
            if len(parts) == 2 and parts[1][1:] == (0, rows):
                one, two = parts[0][0][:, window], parts[1][0][:, window]
                if one.dtype == target.dtype:
                    target[:, window] = one + two
                    return nothing
            total = parts[0][0][:, window].astype(jnp.float32)
            for part, first, last in parts[1:]:
                if first == 0 and last == rows:
                    total = total + part[:, window].astype(jnp.float32)
            target[:, window] = total.astype(target.dtype)
            for part, first, last in parts[1:]:
                if first != 0 or last != rows:
                    span = pl.ds(first, last - first)
                    target[span, window] = (
                        total[first:last] + part[span, window].astype(jnp.float32)
                    ).astype(target.dtype)
            return nothing

        lax.fori_loop(0, columns // width, one, 0)

    def square_sum(ref):
        width = 128

        def one(step, total):
            part = ref[:, pl.ds(pl.multiple_of(step * width, width), width)].astype(jnp.float32)
            return total + jnp.sum(part * part, axis=0, keepdims=True)

        return lax.fori_loop(
            0, ref.shape[1] // width, one, jnp.zeros((1, width), jnp.float32)
        )

    def ring_slot(way, step):
        return way * far + step - 1

    def base(at, turned, offset):
        k = offset % size
        rows = own[at].shape[1]
        here = own[at].at[turned * size + k]
        landed(here, local_sem.at[at, turned * size + k])
        parts = [(here, 0, rows)]
        if across:
            there = core_in[at].at[turned * size + k]
            landed(there, core_sem.at[at, turned * size + k])
            parts.append((there, 0, rows))
        return here, parts

    def ring_parts(at, turned, offset):
        parts = []
        rows = own[at].shape[1]
        cut = cut_of(rows)
        ways = (0, 1) if offset == 0 else (0,) if offset > 0 else (1,)
        for way in ways:
            step = far - abs(offset)
            slot = ring_slot(way, step)
            if half_first[at]:
                if step == 1:
                    first, last = (0, cut) if way == 0 else (cut, rows)
                else:
                    first, last = 0, rows
                if first == last:
                    continue
                region = ring_in[at].at[slot]
                span = region if (first, last) == (0, rows) else region.at[pl.ds(first, last - first)]
                landed(span, ring_sem.at[at, slot])
                parts.append((region, first, last))
            else:
                if step == 1 and turned != way:
                    continue
                region = ring_in[at].at[turned * 2 * far + slot]
                landed(region, ring_sem.at[at, turned * 2 * far + slot])
                parts.append((region, 0, rows))
        return parts

    def ring_send(at, turned, offset):
        here = own[at].at[turned * size + offset % size]
        rows = own[at].shape[1]
        cut = cut_of(rows)
        step = far - abs(offset) + 1
        if offset == far:
            if half_first[at]:
                spans = [(0, pl.ds(0, cut))] + ([(1, pl.ds(cut, rows - cut))] if cut < rows else [])
                for way, span in spans:
                    slot = ring_slot(way, 1)
                    send(
                        here.at[span],
                        ring_in[at].at[slot].at[span],
                        (spot.right, spot.left)[way],
                        slot,
                        at,
                        ring_sem.at[at, slot],
                    )
                return
            ways = (turned,)
        else:
            ways = (0,) if offset > 0 else (1,)
        for way in ways:
            slot = ring_slot(way, step) + (0 if half_first[at] else turned * 2 * far)
            send(
                here,
                ring_in[at].at[slot],
                (spot.right, spot.left)[way],
                slot,
                at,
                ring_sem.at[at, slot],
            )

    spot.meet(across)
    core_base = 4 * far + size
    for offset in slots:
        k = offset % size
        for turned in (1, 0):
            for at in range(count):
                if across:
                    send(
                        source_of(at, turned, 1, offset),
                        core_in[at].at[turned * size + k],
                        spot.to_core,
                        core_base + turned * size + k,
                        at,
                        core_sem.at[at, turned * size + k],
                    )
                pltpu.make_async_copy(
                    source_of(at, turned, 0, offset),
                    own[at].at[turned * size + k],
                    local_sem.at[at, turned * size + k],
                ).start()

    if working:
        work.start()

    def turned_half(offset):
        for at in range(count):
            if half_first[at]:
                here, parts = base(at, 1, offset)
                k = offset % size
                if across:
                    add(here, parts)
                send(here, half_in[at].at[k], spot.to_half, 4 * far + k, at, half_sem.at[at, k])

    def straight(offset):
        for at in range(count):
            if half_first[at]:
                here, parts = base(at, 0, offset)
                k = offset % size
                landed(half_in[at].at[k], half_sem.at[at, k])
                parts.append((half_in[at].at[k], 0, own[at].shape[1]))
                parts += ring_parts(at, 0, offset) if offset != far else []
                if offset == 0:
                    add(outs[at], parts)
                    squares.append(square_sum(outs[at]))
                else:
                    add(here, parts)
                    ring_send(at, 0, offset)

    def both(offset):
        for at in range(count):
            if not half_first[at]:
                for turned in (1, 0):
                    here, parts = base(at, turned, offset)
                    parts += ring_parts(at, turned, offset) if offset != far else []
                    if offset == 0 and turned == 0:
                        landed(half_in[at].at[0], half_sem.at[at, 0])
                        parts.append((half_in[at].at[0], 0, own[at].shape[1]))
                        add(outs[at], parts)
                        squares.append(square_sum(outs[at]))
                        continue
                    if len(parts) > 1:
                        add(here, parts)
                    if offset == 0:
                        send(here, half_in[at].at[0], spot.to_half, 4 * far, at, half_sem.at[at, 0])
                    else:
                        ring_send(at, turned, offset)

    groups = [[far]] + [[at, -at] for at in range(far - 1, 0, -1)] + [[0]]
    def tick():
        if working:
            work.tick()

    tick()
    for number, group in enumerate(groups):
        for offset in group:
            turned_half(offset)
        tick()
        for offset in group:
            both(offset)
        tick()
        if number > 0:
            for offset in groups[number - 1]:
                straight(offset)
            tick()
    for offset in groups[-1]:
        straight(offset)
    total = squares[0]
    for one in squares[1:]:
        total = total + one
    squares_ref[...] = jnp.broadcast_to(total, squares_ref.shape)
    if working:
        work.finish()
    for copy in sent:
        copy.wait_send()


def scatter_call(size, arrays, half_first, across, out_type, number, bases=None, work=None):
    count = len(arrays)
    far = size // 2
    pieces = [a.shape[1:] for a in arrays]
    own = [pltpu.VMEM((2 * size,) + p, a.dtype) for p, a in zip(pieces, arrays)]
    core_in = [
        pltpu.VMEM((2 * size if across else 1,) + p, a.dtype) for p, a in zip(pieces, arrays)
    ]
    half_in = [
        pltpu.VMEM((size if first else 1,) + p, a.dtype)
        for p, a, first in zip(pieces, arrays, half_first)
    ]
    ring_in = [
        pltpu.VMEM((2 * far if first else 4 * far,) + p, a.dtype)
        for p, a, first in zip(pieces, arrays, half_first)
    ]
    outs = [jax.ShapeDtypeStruct(p, out_type) for p in pieces]
    outs.append(jax.ShapeDtypeStruct((8, 128), jnp.float32))
    in_specs = [pl.BlockSpec(memory_space=pl.ANY)] * count
    out_specs = [pl.BlockSpec(memory_space=pltpu.VMEM)] * (count + 1)
    scratch = (
        own
        + core_in
        + half_in
        + ring_in
        + [
            pltpu.SemaphoreType.DMA((count, 2 * size)),
            pltpu.SemaphoreType.DMA((count, 2 * size)),
            pltpu.SemaphoreType.DMA((count, size)),
            pltpu.SemaphoreType.DMA((count, 4 * far)),
            pltpu.SemaphoreType.DMA((count, 4 * far + 3 * size)),
        ]
    )
    if work is not None:
        in_specs += FeedBack.in_specs()
        outs += FeedBack.out_shape(work[0], work[4])
        out_specs += FeedBack.out_specs()
        scratch += FeedBack.scratch(work[0].shape[0])
    return pl.pallas_call(
        functools.partial(
            scatter_body, size, half_first, across, bases or ((0, 1),) * count, work is not None
        ),
        out_shape=outs,
        in_specs=in_specs,
        out_specs=out_specs,
        scratch_shapes=scratch,
        compiler_params=pltpu.CompilerParams(
            collective_id=number, has_side_effects=True, vmem_limit_bytes=60 * 1024 * 1024
        ),
    )(*arrays, *(work or ()))


def layer_norm(values, gain, shift):
    center = values - jnp.mean(values, axis=-1, keepdims=True)
    spread = jnp.mean(center * center, axis=-1, keepdims=True)
    return center * lax.rsqrt(spread + 1e-05) * gain + shift


def gelu_tanh(values):
    return jax.nn.gelu(values, approximate=True)


INNER = (((1,), (1,)), ((), ()))
OUTER = (((0,), (0,)), ((), ()))


def dot_inner(one, two):
    return lax.dot_general(one, two, INNER, preferred_element_type=jnp.float32)


def dot_outer(one, two):
    return lax.dot_general(one, two, OUTER, preferred_element_type=jnp.float32)


def fill_mask(mask_ref, length):
    key = lax.broadcasted_iota(jnp.int32, mask_ref.shape, 0)
    query = lax.broadcasted_iota(jnp.int32, mask_ref.shape, 1)
    mask_ref[...] = jnp.where((key <= query) & (key < length), 0.0, -1e30)


def probs_by_key(query, key, mask):
    scores = dot_inner(key, query * 0.125) + mask
    raised = jnp.exp(scores - jnp.max(scores, axis=0, keepdims=True))
    return raised * (1.0 / jnp.sum(raised, axis=0, keepdims=True))


def attend_body(length_ref, query_ref, key_ref, value_ref, mixed_ref, mask_ref):
    @pl.when(pl.program_id(0) == 0)
    def _():
        fill_mask(mask_ref, length_ref[0])

    rows = query_ref.shape[0]
    block = rows // 2
    for at in range(2):
        here, seen = slice(at * block, (at + 1) * block), slice(0, (at + 1) * block)
        mixed = []
        for head in range(2):
            lanes = slice(head * HD, (head + 1) * HD)
            probs = probs_by_key(query_ref[here, lanes], key_ref[seen, lanes], mask_ref[seen, here])
            mixed.append(dot_outer(value_ref[seen, lanes], probs.astype(jnp.bfloat16)))
        mixed_ref[here, :] = jnp.concatenate(mixed).T.astype(jnp.bfloat16)


def attend(projected, seq_lengths):
    rows = projected.shape[0]
    pairs = HEADS // 2
    return pl.pallas_call(
        attend_body,
        grid=(pairs,),
        out_shape=jax.ShapeDtypeStruct((rows, D), jnp.bfloat16),
        in_specs=[
            pl.BlockSpec(memory_space=pltpu.SMEM),
            pl.BlockSpec((rows, 2 * HD), lambda p: (0, p)),
            pl.BlockSpec((rows, 2 * HD), lambda p: (0, pairs + p)),
            pl.BlockSpec((rows, 2 * HD), lambda p: (0, 2 * pairs + p)),
        ],
        out_specs=pl.BlockSpec((rows, 2 * HD), lambda p: (0, p)),
        scratch_shapes=[pltpu.VMEM((rows, rows), jnp.float32)],
        compiler_params=pltpu.CompilerParams(vmem_limit_bytes=32 * 1024 * 1024),
        cost_estimate=pl.CostEstimate(
            flops=4 * HEADS * rows * rows * HD, bytes_accessed=8 * rows * D, transcendentals=0
        ),
    )(seq_lengths, projected, projected, projected)


def attend_back_body(length_ref, query_ref, key_ref, value_ref, grad_ref, out_ref, mask_ref):
    @pl.when(pl.program_id(0) == 0)
    def _():
        fill_mask(mask_ref, length_ref[0])

    rows = query_ref.shape[0]
    block = rows // 2
    pair = pl.program_id(0)
    low = jnp.bfloat16
    grad_query, grad_key, grad_value = [], [], []
    for at in range(2):
        here, seen = slice(at * block, (at + 1) * block), slice(0, (at + 1) * block)
        heads = []
        for head in range(2):
            lanes = slice(head * HD, (head + 1) * HD)
            query, key = query_ref[here, lanes], key_ref[seen, lanes]
            grad = grad_ref[here, lanes]
            probs = probs_by_key(query, key, mask_ref[seen, here])
            grad_probs = dot_inner(value_ref[seen, lanes], grad)
            value_part = jnp.dot(probs.astype(low), grad, preferred_element_type=jnp.float32)
            key_dot = jnp.sum(grad_probs * probs, axis=0, keepdims=True)
            scores_low = (probs * (grad_probs - key_dot)).astype(low)
            key_part = jnp.dot(scores_low, query, preferred_element_type=jnp.float32) * 0.125
            heads.append((dot_outer(key, scores_low) * 0.125, key_part, value_part))
        grad_query.append(jnp.concatenate([part[0] for part in heads]).T)
        grad_key.append(jnp.concatenate([part[1] for part in heads], axis=1))
        grad_value.append(jnp.concatenate([part[2] for part in heads], axis=1))
    for part, parts in enumerate((grad_query, grad_key, grad_value)):
        window = pl.ds(pl.multiple_of(part * D + pair * 2 * HD, 2 * HD), 2 * HD)
        first = parts[0] if part == 0 else parts[0] + parts[1][:block]
        out_ref[:block, window] = first.astype(low)
        second = parts[1] if part == 0 else parts[1][block:]
        out_ref[block:, window] = second.astype(low)


def attend_back(projected, grad_mixed, seq_lengths):
    rows = projected.shape[0]
    pairs = HEADS // 2
    return pl.pallas_call(
        attend_back_body,
        grid=(pairs,),
        out_shape=jax.ShapeDtypeStruct((rows, 3 * D), jnp.bfloat16),
        in_specs=[
            pl.BlockSpec(memory_space=pltpu.SMEM),
            pl.BlockSpec((rows, 2 * HD), lambda p: (0, p)),
            pl.BlockSpec((rows, 2 * HD), lambda p: (0, pairs + p)),
            pl.BlockSpec((rows, 2 * HD), lambda p: (0, 2 * pairs + p)),
            pl.BlockSpec((rows, 2 * HD), lambda p: (0, p)),
        ],
        out_specs=pl.BlockSpec((rows, 3 * D), lambda p: (0, 0)),
        scratch_shapes=[pltpu.VMEM((rows, rows), jnp.float32)],
        compiler_params=pltpu.CompilerParams(vmem_limit_bytes=48 * 1024 * 1024),
        cost_estimate=pl.CostEstimate(
            flops=10 * HEADS * rows * rows * HD, bytes_accessed=16 * rows * D, transcendentals=0
        ),
    )(seq_lengths, projected, projected, projected, grad_mixed)


class FeedBack:
    CHUNK = 256
    INPUTS = 6
    OUTPUTS = 4

    def __init__(self, ins, outs, scratch):
        self.branch, self.turned, pre, hidden, w_fc, w_proj = ins
        self.grad_normed, self.bias, self.grad_fc, self.grad_proj = outs
        pre_in, hidden_in, fc_in, proj_in, self.fc_out, self.proj_out, self.in_sem, self.out_sem = scratch
        self.chunks = w_proj.shape[0] // self.CHUNK
        self.sources = (pre, hidden, w_fc, w_proj)
        self.slots = (pre_in, hidden_in, fc_in, proj_in)
        self.done = 0

    def span(self, number):
        return pl.ds(pl.multiple_of(number * self.CHUNK, self.CHUNK), self.CHUNK)

    def loads(self, number):
        slot = lax.rem(number, 2)
        for at, (source, place) in enumerate(zip(self.sources, self.slots)):
            here = source.at[self.span(number)] if at == 3 else source.at[:, self.span(number)]
            yield pltpu.make_async_copy(here, place.at[slot], self.in_sem.at[at, slot])

    def stores(self, number):
        slot = lax.rem(number, 2)
        yield pltpu.make_async_copy(
            self.fc_out.at[slot], self.grad_fc.at[:, self.span(number)], self.out_sem.at[0, slot]
        )
        yield pltpu.make_async_copy(
            self.proj_out.at[slot], self.grad_proj.at[self.span(number)], self.out_sem.at[1, slot]
        )

    def start(self):
        self.grad_normed[...] = jnp.zeros_like(self.grad_normed)
        for copy in self.loads(0):
            copy.start()

    def run(self, first, last):
        def one(number, nothing):
            slot = lax.rem(number, 2)
            for copy in self.loads(number):
                copy.wait()

            @pl.when(number + 1 < self.chunks)
            def _():
                for copy in self.loads(number + 1):
                    copy.start()

            @pl.when(number >= 2)
            def _():
                for copy in self.stores(number - 2):
                    copy.wait()

            low = jnp.bfloat16
            pre_in, hidden_in, fc_in, proj_in = self.slots
            grad_hidden = dot_inner(self.branch[...], proj_in[slot])
            value = pre_in[slot]
            square = value * value
            bent = jnp.tanh(0.7978845608 * value * (1.0 + 0.044715 * square))
            slope = 0.5 * (1.0 + bent) + 0.5 * value * (1.0 - bent * bent) * (
                0.7978845608 * (1.0 + 3.0 * 0.044715 * square)
            )
            pre_low = (grad_hidden * slope).astype(low)
            self.bias[:, self.span(number)] = jnp.sum(
                pre_low.astype(jnp.float32), axis=0, keepdims=True
            )
            self.grad_normed[...] += dot_inner(pre_low, fc_in[slot])
            self.fc_out[slot] = jnp.dot(
                self.turned[...], pre_low, preferred_element_type=jnp.float32
            ).astype(low)
            self.proj_out[slot] = dot_outer(hidden_in[slot], self.branch[...]).astype(low)
            for copy in self.stores(number):
                copy.start()
            return nothing

        lax.fori_loop(first, last, one, 0)

    def tick(self):
        if self.done < self.chunks:
            self.run(self.done, self.done + 1)
            self.done += 1

    def finish(self):
        if self.done < self.chunks:
            self.run(self.done, self.chunks)
        for number in (self.chunks - 2, self.chunks - 1):
            for copy in self.stores(jnp.int32(number)):
                copy.wait()

    @classmethod
    def in_specs(cls):
        return [pl.BlockSpec(memory_space=pltpu.VMEM)] * 2 + [pl.BlockSpec(memory_space=pl.ANY)] * 4

    @classmethod
    def out_specs(cls):
        return [pl.BlockSpec(memory_space=pltpu.VMEM)] * 2 + [pl.BlockSpec(memory_space=pl.ANY)] * 2

    @classmethod
    def out_shape(cls, branch, w_fc):
        hidden = w_fc.shape[1]
        return [
            jax.ShapeDtypeStruct(branch.shape, jnp.float32),
            jax.ShapeDtypeStruct((1, hidden), jnp.float32),
            jax.ShapeDtypeStruct((D, hidden), jnp.bfloat16),
            jax.ShapeDtypeStruct((hidden, D), jnp.bfloat16),
        ]

    @classmethod
    def scratch(cls, rows):
        low, chunk = jnp.bfloat16, cls.CHUNK
        return [
            pltpu.VMEM((2, rows, chunk), jnp.float32),
            pltpu.VMEM((2, rows, chunk), low),
            pltpu.VMEM((2, D, chunk), low),
            pltpu.VMEM((2, chunk, D), low),
            pltpu.VMEM((2, D, chunk), low),
            pltpu.VMEM((2, chunk, D), low),
            pltpu.SemaphoreType.DMA((4, 2)),
            pltpu.SemaphoreType.DMA((2, 2)),
        ]


def feed_back_body(*refs):
    ins, outs = FeedBack.INPUTS, FeedBack.OUTPUTS
    work = FeedBack(refs[:ins], refs[ins : ins + outs], refs[ins + outs :])
    work.start()
    work.finish()


def feed_back(operands):
    branch, w_fc = operands[0], operands[4]
    return pl.pallas_call(
        feed_back_body,
        out_shape=FeedBack.out_shape(branch, w_fc),
        in_specs=FeedBack.in_specs(),
        out_specs=FeedBack.out_specs(),
        scratch_shapes=FeedBack.scratch(branch.shape[0]),
        compiler_params=pltpu.CompilerParams(vmem_limit_bytes=40 * 1024 * 1024),
    )(*operands)


def layer_forward(stream, weights, vector, seq_lengths):
    w_qkv, w_out, w_fc, w_proj = weights
    normed_low = layer_norm(stream, vector[0:D], vector[D : 2 * D]).astype(jnp.bfloat16)
    qkv_bias = jnp.concatenate(
        [vector[4 * D : 5 * D], jnp.zeros((D,), jnp.float32), vector[5 * D : 6 * D]]
    )
    projected = (jnp.dot(normed_low, w_qkv, preferred_element_type=jnp.float32) + qkv_bias).astype(
        jnp.bfloat16
    )
    mixed_low = attend(projected, seq_lengths)
    stream_mid = (
        stream
        + jnp.dot(mixed_low, w_out, preferred_element_type=jnp.float32)
        + vector[6 * D : 7 * D]
    )
    normed_two = layer_norm(stream_mid, vector[2 * D : 3 * D], vector[3 * D : 4 * D]).astype(
        jnp.bfloat16
    )
    hidden_pre = (
        jnp.dot(normed_two, w_fc, preferred_element_type=jnp.float32) + vector[8 * D : 8 * D + FF]
    )
    hidden_low = gelu_tanh(hidden_pre).astype(jnp.bfloat16)
    stream_out = (
        stream_mid
        + jnp.dot(hidden_low, w_proj, preferred_element_type=jnp.float32)
        + vector[7 * D : 8 * D]
    )
    return (
        stream_out,
        (
            stream,
            normed_low,
            projected,
            mixed_low,
            stream_mid,
            normed_two,
            hidden_pre,
            hidden_low,
        ),
    )


def feed_plain(operands):
    branch_low, normed_turned, hidden_pre, hidden_low, w_fc, w_proj = operands
    grad_wproj = jnp.dot(hidden_low.T, branch_low, preferred_element_type=jnp.bfloat16)
    grad_hidden = jnp.dot(branch_low, w_proj.T, preferred_element_type=jnp.float32)
    pre_low = jax.vjp(gelu_tanh, hidden_pre)[1](grad_hidden)[0].astype(jnp.bfloat16)
    grad_wfc = jnp.dot(normed_turned, pre_low, preferred_element_type=jnp.bfloat16)
    grad_normed_two = jnp.dot(pre_low, w_fc.T, preferred_element_type=jnp.float32)
    bias = jnp.sum(pre_low.astype(jnp.float32), axis=0)
    return grad_normed_two, bias, grad_wfc, grad_wproj


def layer_backward(grad_out, saved_acts, weights, vector, seq_lengths, feed):
    (
        stream,
        normed_low,
        projected,
        mixed_low,
        stream_mid,
        normed_two,
        hidden_pre,
        hidden_low,
    ) = saved_acts
    w_qkv, w_out, w_fc, w_proj = weights
    branch_low = grad_out.astype(jnp.bfloat16)
    grad_normed_two, grad_bias, grad_wfc, grad_wproj = feed(
        (branch_low, normed_two.T, hidden_pre, hidden_low, w_fc, w_proj)
    )
    grad_mid, grad_gain_two, grad_shift_two = jax.vjp(
        layer_norm, stream_mid, vector[2 * D : 3 * D], vector[3 * D : 4 * D]
    )[1](grad_normed_two)
    grad_mid = grad_mid + grad_out
    attn_low = grad_mid.astype(jnp.bfloat16)
    grad_wout = jnp.dot(mixed_low.T, attn_low, preferred_element_type=jnp.bfloat16)
    grad_mixed = jnp.dot(attn_low, w_out.T, preferred_element_type=jnp.float32).astype(
        jnp.bfloat16
    )
    qkv_low = attend_back(projected, grad_mixed, seq_lengths)
    grad_wqkv = jnp.dot(normed_low.T, qkv_low, preferred_element_type=jnp.bfloat16)
    grad_normed = jnp.dot(qkv_low, w_qkv.T, preferred_element_type=jnp.float32)
    grad_input, grad_gain_one, grad_shift_one = jax.vjp(
        layer_norm, stream, vector[0:D], vector[D : 2 * D]
    )[1](grad_normed)
    bias_qkv = jnp.sum(qkv_low.astype(jnp.float32), axis=0)
    grad_vector = jnp.concatenate(
        [
            grad_gain_one,
            grad_shift_one,
            grad_gain_two,
            grad_shift_two,
            bias_qkv[0:D],
            bias_qkv[2 * D : 3 * D],
            jnp.sum(attn_low.astype(jnp.float32), axis=0),
            jnp.sum(branch_low.astype(jnp.float32), axis=0),
            grad_bias.reshape(-1),
        ]
    )
    return (grad_input + grad_mid, (grad_wqkv, grad_wout, grad_wfc, grad_wproj), grad_vector)


def adamw(weight, moment_one, moment_two, gradient, step_rate, decay_rate, step_float):
    one_new = 0.5 * moment_one + 0.5 * gradient
    two_new = 0.5 * moment_two + 0.5 * gradient * gradient
    fix_scale = 1.0 - jnp.power(0.5, step_float)
    update = one_new / fix_scale / (jnp.sqrt(two_new / fix_scale) + 1e-08)
    return (weight - step_rate * (update + decay_rate * weight), one_new, two_new)


def on_device(
    token_ids,
    seq_lengths,
    loss_slots,
    target_ids,
    step_count,
    w_qkv,
    w_out,
    w_fc,
    w_proj,
    vectors,
    pos_table,
    embed_table,
    mom_qkv,
    mom_out,
    mom_fc,
    mom_proj,
    mom_vectors,
    mom_pos,
    mom_embed,
    sec_qkv,
    sec_out,
    sec_fc,
    sec_proj,
    sec_vectors,
    sec_pos,
    sec_embed,
):
    per_layer = 8 * D + FF
    net = Net()
    size, halves = net.size, net.halves
    same_core = halves * size
    devices = 2 * same_core
    low = jnp.bfloat16
    near = LEN // 2
    fused = size <= 8
    rest = LEN - near
    slots = loss_slots.shape[0]

    half_of = jnp.arange(halves)[:, None]
    wide_index = jnp.arange(size)[None, :]
    place_of = jnp.where(wide_index % 2 == 0, wide_index // 2, size - 1 - (wide_index - 1) // 2)
    to_device = ((half_of ^ net.half) * size + (place_of - net.place) % size).reshape(-1)
    offsets = (net.place + wide_index) % size
    wide_there = jnp.where(offsets < size // 2, 2 * offsets, 2 * (size - 1 - offsets) + 1)
    from_device = ((half_of ^ net.half) * size + wide_there).reshape(-1)

    numbers = jnp.concatenate([token_ids, loss_slots, target_ids, seq_lengths])
    numbers = jnp.pad(numbers, (0, -numbers.shape[0] % 1024)).reshape(-1, 128)
    numbers = cast_call(size, numbers, False, 5).reshape(same_core, -1)
    numbers = jnp.take(numbers, from_device, axis=0).reshape(halves, size, -1)
    group_tokens = numbers[:, :, :LEN]
    group_slots = numbers[:, :, LEN : LEN + slots].reshape(same_core * slots)
    group_targets = numbers[:, :, LEN + slots : LEN + 2 * slots].reshape(same_core * slots)
    core_total = jnp.sum(numbers[:, :, LEN + 2 * slots].astype(jnp.float32))
    token_total = core_total + net.swap_core(core_total[None])[0]

    own_rows = embed_table.shape[0]
    height = own_rows + -own_rows % 64
    chip_rows = 2 * height
    table_own = jnp.pad(embed_table.astype(low), ((0, height - own_rows), (0, 0)))
    own_start = net.device * own_rows
    other_start = (net.device + (1 - 2 * net.core) * size) * own_rows

    def locate(ids):
        mine = ids - own_start
        other = ids - other_start
        return jnp.where(
            (mine >= 0) & (mine < own_rows),
            mine,
            jnp.where((other >= 0) & (other < own_rows), other + height, -1),
        )

    def one_hot(ids):
        return (ids[:, None] == jnp.arange(chip_rows)[None, :]).astype(low)

    local_tokens = locate(group_tokens).reshape(same_core, LEN)
    ids_near, ids_rest = local_tokens[:, :near], local_tokens[:, near:]

    shared = pos_table.shape[0]
    vector_rows = -(-vectors.shape[0] // D)
    padded = jnp.pad(vectors, (0, vector_rows * D - vectors.shape[0])).reshape(vector_rows, D)
    spare = -(shared + vector_rows) % 16
    small_own = jnp.concatenate([pos_table, padded, jnp.zeros((spare, D), jnp.float32)])
    shards_low = []
    for layer_at in range(LAYERS):
        shards_low += [part[layer_at].astype(low) for part in (w_qkv, w_fc, w_proj, w_out)]
    shards_low.append(small_own.astype(low))
    ring_first = (True, True, False, False) * LAYERS + (False,)
    if fused:
        *gathered, table_low, found = look_up_call(
            size, shards_low, ring_first, table_own, jnp.concatenate([ids_near, ids_rest])[..., None], 1
        )
        stream = scatter_call(
            size, [found, found], (True, False), False, low, 2, ((0, 1), (same_core, 1))
        )
        stream = jnp.concatenate(stream[:2])
    else:
        gathered = gather_call(size, shards_low, ring_first, True, 1)
        table_low = jnp.concatenate([table_own, net.swap_core(table_own)])
        found = [
            jnp.dot(
                one_hot(ids.reshape(-1)), table_low, preferred_element_type=jnp.float32
            ).astype(low).reshape(same_core, -1, D)
            for ids in (ids_near, ids_rest)
        ]
        bands = max(1, same_core // 16)
        band = D // bands
        parts = []
        for at in range(bands):
            window = [part[:, :, at * band : (at + 1) * band] for part in found]
            parts.append(
                jnp.concatenate(scatter_call(size, window, (True, False), False, low, 2)[:2])
            )
        stream = jnp.concatenate(parts, axis=1)
    small_low = gathered[-1]
    pos_low = small_low[:, :shared].reshape(devices * shared, D)
    vector_all = (
        small_low[:, shared : shared + vector_rows]
        .reshape(devices, vector_rows * D)[:, : vectors.shape[0]]
        .reshape(-1)
        .astype(jnp.float32)
    )

    stream = stream.astype(jnp.float32) + pos_low[:LEN].astype(jnp.float32)

    kept_weights = []
    saved_list = []
    for layer_at in range(LAYERS):
        w_a, w_c, w_d, w_b = (
            part.reshape(-1, part.shape[2]) for part in gathered[layer_at * 4 : layer_at * 4 + 4]
        )
        weights = (w_a, w_b, w_c, w_d)
        kept_weights.append(weights)
        stream, saved_acts = layer_forward(
            stream, weights, vector_all[layer_at * per_layer : (layer_at + 1) * per_layer], seq_lengths
        )
        saved_list.append(saved_acts)
    tail_start = LAYERS * per_layer
    final_norm, final_pull = jax.vjp(
        layer_norm,
        stream,
        vector_all[tail_start : tail_start + D],
        vector_all[tail_start + D : tail_start + 2 * D],
    )
    slot_rows = jnp.maximum(loss_slots, 0)
    own_picked = final_norm[slot_rows].astype(low)
    some = slots // 2
    group_rows = jnp.concatenate(
        gather_call(size, [own_picked[:some], own_picked[some:]], (True, False), False, 6), axis=1
    ).reshape(same_core * slots, D)
    real = jnp.arange(chip_rows) % height < own_rows
    logits = jnp.where(
        real, jnp.dot(group_rows, table_low.T, preferred_element_type=jnp.float32), -1e30
    )
    target_onehot = locate(group_targets)[:, None] == jnp.arange(chip_rows)[None, :]
    row_max = jnp.max(logits, axis=-1)
    row_total = jnp.sum(jnp.exp(logits - row_max[:, None]), axis=-1)
    target_logit = jnp.sum(jnp.where(target_onehot, logits, 0.0), axis=-1)
    stats = jnp.stack([row_max, row_total, target_logit], axis=-1)
    stats = jnp.take(stats.reshape(same_core, slots * 3), to_device, axis=0)
    stats = stats.reshape(same_core * slots, 3).T.reshape(-1)
    entries = stats.shape[0]
    stats = jnp.pad(stats, (0, -entries % 1024)).reshape(-1, 128)
    stats = cast_call(size, stats, False, 7).reshape(same_core, -1)[:, :entries]
    stats = stats.reshape(same_core, 3, same_core * slots)
    joint_max = jnp.max(stats[:, 0], axis=0)
    joint_total = jnp.sum(stats[:, 1] * jnp.exp(stats[:, 0] - joint_max), axis=0)
    stats = jnp.stack([joint_max + jnp.log(joint_total), jnp.sum(stats[:, 2], axis=0)])
    stats = stats.reshape(2, same_core, slots)
    stats = jnp.take(stats, from_device, axis=1).reshape(2, same_core * slots)
    log_total, merged_target = stats[0], stats[1]
    group_used = (group_slots >= 0).astype(jnp.float32)
    own_loss = jnp.sum(((log_total - merged_target) * group_used)[:slots])
    grad_logits = (
        (jnp.exp(logits - log_total[:, None]) - target_onehot.astype(jnp.float32))
        * (group_used / token_total)[:, None]
    ).astype(low)
    grad_rows = jnp.dot(grad_logits, table_low, preferred_element_type=jnp.float32)
    grad_rows = grad_rows.reshape(2 * same_core, some, D)
    grad_rows = jnp.concatenate(
        scatter_call(
            size,
            [grad_rows, grad_rows],
            (True, False),
            False,
            jnp.float32,
            8,
            ((0, 2), (1, 2)),
        )[:2]
    )
    grad_final = jnp.zeros((LEN, D), jnp.float32).at[slot_rows].add(grad_rows)
    grad_stream, grad_gain_final, grad_shift_final = final_pull(grad_final)
    layer_shards = []
    vector_grads = []
    squares = jnp.float32(0)
    pending = None

    def reduce_layers(full_grads, number, more=(), work=None):
        grad_a, grad_b, grad_c, grad_d = full_grads
        arrays = [part.reshape(devices, -1, part.shape[1]) for part in (grad_a, grad_c, grad_d, grad_b)]
        arrays += more
        outs = scatter_call(
            size,
            arrays,
            (True, True, False, False) + (False,) * len(more),
            True,
            jnp.float32,
            number,
            work=work,
        )
        shard_a, shard_c, shard_d, shard_b, *rest = outs
        layer_shards.insert(0, (shard_a, shard_b, shard_c, shard_d))
        return rest

    for layer_at in reversed(range(LAYERS)):
        feed = feed_plain
        if pending is not None:
            held = []

            def feed(operands):
                sums, *results = reduce_layers(pending, 3, work=operands)
                held.append(jnp.sum(sums[0]))
                return results

        grad_stream, full_grads, grad_vector = layer_backward(
            grad_stream,
            saved_list[layer_at],
            kept_weights[layer_at],
            vector_all[layer_at * per_layer : (layer_at + 1) * per_layer],
            seq_lengths,
            feed,
        )
        if pending is not None:
            squares = squares + held[0]
        pending = full_grads
        vector_grads.insert(0, grad_vector)
    grad_low = grad_stream.astype(low)
    grad_near, grad_rest = grad_low[:near], grad_low[near:]
    grad_table = jnp.dot(grad_logits.T, group_rows, preferred_element_type=jnp.float32)
    if fused:
        ids = [part[:, None] for part in (ids_near, ids_rest)]
        grad_table, grad_pos, sums = spread_call(size, grad_near, grad_rest, ids, grad_table, 4)
        squares = squares + jnp.sum(sums[0])
    else:
        wholes = gather_call(size, [grad_near, grad_rest], (True, False), False, 4)
        for ids, whole in zip((ids_near, ids_rest), wholes):
            grad_table = grad_table + jnp.dot(
                one_hot(ids.reshape(-1)).T, whole.reshape(-1, D), preferred_element_type=jnp.float32
            )
        grad_table = grad_table[:height] + net.swap_core(grad_table[height:])
        squares = squares + jnp.sum(grad_table * grad_table)
        grad_pos = jnp.concatenate(
            [jnp.sum(whole.astype(jnp.float32), axis=0) for whole in wholes]
        )
    table_shard = grad_table[:own_rows]
    grad_pos = jnp.pad(grad_pos, ((0, POS - LEN), (0, 0)))
    other_device = net.device + (1 - 2 * net.core) * size
    pos_shard = lax.dynamic_slice_in_dim(grad_pos, net.device * shared, shared) + net.swap_core(
        lax.dynamic_slice_in_dim(grad_pos, other_device * shared, shared)
    )
    grad_small = jnp.concatenate(vector_grads + [grad_gain_final, grad_shift_final])
    own_small = vectors.shape[0]
    grad_small = jnp.pad(grad_small.reshape(devices, own_small), ((0, 0), (0, -own_small % 1024)))
    small_shard, sums = reduce_layers(pending, 10, [grad_small.reshape(devices, -1, 128)])
    small_shard = small_shard.reshape(-1)[:own_small]
    squares = squares + jnp.sum(sums[0]) + jnp.sum(pos_shard * pos_shard)
    qkv_shard = jnp.stack([member[0] for member in layer_shards])
    out_shard = jnp.stack([member[1] for member in layer_shards])
    fc_shard = jnp.stack([member[2] for member in layer_shards])
    proj_shard = jnp.stack([member[3] for member in layer_shards])
    shards = (qkv_shard, out_shard, fc_shard, proj_shard, small_shard, pos_shard, table_shard)
    sums = jnp.pad(jnp.stack([own_loss, squares]), (0, 1022)).reshape(8, 128)
    sums = jnp.sum(cast_call(size, sums, True, 9), axis=0)
    loss_total, square_total = sums[0, 0], sums[0, 1]
    loss_value = loss_total / token_total
    grad_norm = jnp.sqrt(square_total)
    factor = CLIP_LIMIT / jnp.maximum(grad_norm, CLIP_LIMIT)
    step_float = step_count.astype(jnp.float32)
    params = (w_qkv, w_out, w_fc, w_proj, vectors, pos_table, embed_table)
    moments_one = (mom_qkv, mom_out, mom_fc, mom_proj, mom_vectors, mom_pos, mom_embed)
    moments_two = (sec_qkv, sec_out, sec_fc, sec_proj, sec_vectors, sec_pos, sec_embed)
    step_rates = (
        RATE_MATRIX,
        RATE_MATRIX,
        RATE_MATRIX,
        RATE_MATRIX,
        RATE_VECTOR,
        RATE_MATRIX,
        RATE_MATRIX,
    )
    decay_rates = (
        DECAY_MATRIX,
        DECAY_MATRIX,
        DECAY_MATRIX,
        DECAY_MATRIX,
        0.0,
        DECAY_MATRIX,
        DECAY_MATRIX,
    )
    results = [
        adamw(
            params[where_at],
            moments_one[where_at],
            moments_two[where_at],
            shards[where_at] * factor,
            step_rates[where_at],
            decay_rates[where_at],
            step_float,
        )
        for where_at in range(7)
    ]
    return (
        loss_value,
        grad_norm,
        results[0][0],
        results[1][0],
        results[2][0],
        results[3][0],
        results[4][0],
        results[5][0],
        results[6][0],
        results[0][1],
        results[1][1],
        results[2][1],
        results[3][1],
        results[4][1],
        results[5][1],
        results[6][1],
        results[0][2],
        results[1][2],
        results[2][2],
        results[3][2],
        results[4][2],
        results[5][2],
        results[6][2],
    )


def solution(mesh):
    return jax.shard_map(
        on_device,
        mesh=mesh,
        in_specs=(
            P(("narrow", "wide")),
            P(("narrow", "wide")),
            P(("narrow", "wide")),
            P(("narrow", "wide")),
            P(),
            P(None, ("narrow", "wide"), None),
            P(None, ("narrow", "wide"), None),
            P(None, ("narrow", "wide"), None),
            P(None, ("narrow", "wide"), None),
            P(("narrow", "wide")),
            P(("narrow", "wide"), None),
            P(("narrow", "wide"), None),
            P(None, ("narrow", "wide"), None),
            P(None, ("narrow", "wide"), None),
            P(None, ("narrow", "wide"), None),
            P(None, ("narrow", "wide"), None),
            P(("narrow", "wide")),
            P(("narrow", "wide"), None),
            P(("narrow", "wide"), None),
            P(None, ("narrow", "wide"), None),
            P(None, ("narrow", "wide"), None),
            P(None, ("narrow", "wide"), None),
            P(None, ("narrow", "wide"), None),
            P(("narrow", "wide")),
            P(("narrow", "wide"), None),
            P(("narrow", "wide"), None),
        ),
        out_specs=(
            P(),
            P(),
            P(None, ("narrow", "wide"), None),
            P(None, ("narrow", "wide"), None),
            P(None, ("narrow", "wide"), None),
            P(None, ("narrow", "wide"), None),
            P(("narrow", "wide")),
            P(("narrow", "wide"), None),
            P(("narrow", "wide"), None),
            P(None, ("narrow", "wide"), None),
            P(None, ("narrow", "wide"), None),
            P(None, ("narrow", "wide"), None),
            P(None, ("narrow", "wide"), None),
            P(("narrow", "wide")),
            P(("narrow", "wide"), None),
            P(("narrow", "wide"), None),
            P(None, ("narrow", "wide"), None),
            P(None, ("narrow", "wide"), None),
            P(None, ("narrow", "wide"), None),
            P(None, ("narrow", "wide"), None),
            P(("narrow", "wide")),
            P(("narrow", "wide"), None),
            P(("narrow", "wide"), None),
        ),
        check_vma=False,
    )
```

```python
import functools

import jax
import jax.numpy as jnp
from jax import lax
from jax.experimental import pallas as pl
from jax.experimental.pallas import tpu as pltpu
from jax.sharding import PartitionSpec as P

D = 1024
HEADS = 16
HD = 64
FF = 4096
POS = 1024
LAYERS = 2
LEN = 512
LOSS_DEV = 32


CLIP_LIMIT = 0.002
RATE_MATRIX = 0.03
RATE_VECTOR = 0.3
DECAY_MATRIX = 0.1


class Net:
    def __init__(self):
        self.narrow_at = lax.axis_index("narrow")
        self.wide_at = lax.axis_index("wide")
        self.narrow_size = lax.axis_size("narrow")
        self.size = lax.axis_size("wide")
        size = self.size
        self.core = self.narrow_at % 2
        self.half = self.narrow_at // 2
        self.halves = self.narrow_size // 2
        self.place = jnp.where(
            self.wide_at % 2 == 0, self.wide_at // 2, size - 1 - (self.wide_at - 1) // 2
        )
        self.device = self.narrow_at * size + self.wide_at
        order = list(range(0, size, 2)) + list(range(size - 1, 0, -2))
        pairs = [(n, w) for n in range(self.narrow_size) for w in range(size)]
        self.core_pairs = [(n * size + w, (n ^ 1) * size + w) for n, w in pairs]
        self.half_pairs = [(n * size + w, (n ^ 2) * size + w) for n, w in pairs]
        self.right = [
            (n * size + order[i], n * size + order[(i + 1) % size])
            for n in range(self.narrow_size)
            for i in range(size)
        ]
        self.left = [(later, earlier) for earlier, later in self.right]

    def step(self, array, pairs):
        return lax.ppermute(array, ("narrow", "wide"), pairs)

    def swap_core(self, array):
        return self.step(array, self.core_pairs)

    def swap_half(self, array):
        return self.step(array, self.half_pairs)

    def wide_of(self, offset):
        size = self.size
        at = lax.rem(self.place + offset, size)
        return jnp.where(at < size // 2, 2 * at, 2 * (size - 1 - at) + 1)


MESH = pl.DeviceIdType.MESH


class Spot:
    def __init__(self, size):
        self.size = size
        narrow, wide = lax.axis_index("narrow"), lax.axis_index("wide")
        odd = lax.rem(wide, 2)
        self.core, self.half = lax.rem(narrow, 2), lax.div(narrow, 2)
        self.wide = wide
        self.place = (1 - odd) * lax.div(wide, 2) + odd * (size - 1 - lax.div(wide, 2))
        self.to_core = (narrow + 1 - 2 * self.core, wide)
        self.to_half = (narrow + 2 - 4 * self.half, wide)
        self.right = (narrow, self.wide_of(1))
        self.left = (narrow, self.wide_of(size - 1))

    def wide_of(self, offset):
        at = lax.rem(self.place + offset, self.size)
        late = lax.div(at, self.size // 2)
        return (1 - late) * 2 * at + late * (2 * (self.size - 1 - at) + 1)

    def index(self, turned, other_core, offset):
        half = self.half + turned * (1 - 2 * self.half)
        core = self.core + other_core * (1 - 2 * self.core)
        return (2 * half + core) * self.size + self.wide_of(offset)

    def meet(self, with_core):
        barrier = pltpu.get_barrier_semaphore()
        peers = [self.to_half, self.right, self.left] + ([self.to_core] if with_core else [])
        for peer in peers:
            pl.semaphore_signal(barrier, inc=1, device_id=peer, device_id_type=MESH)
        pl.semaphore_wait(barrier, len(peers))


def cut_of(rows):
    return rows // 2 if rows % 32 == 0 else rows


def gather_steps(size, ring_first, across, shards, wholes, sems, spot, tick, ready):
    count = len(ring_first)
    ring_sem, half_sem, core_sem, send_sem, local_sem = sems
    far = size // 2

    def index(turned, offset, toward=None):
        if across:
            return spot.index(turned, 0, offset % size)
        if toward == "half":
            turned = 1 - turned
        offset = offset + {"right": -1, "left": 1}.get(toward, 0)
        return turned * size + offset % size

    def send(at, source, turned, offset, toward, sem, rows=None):
        target = wholes[at].at[index(turned, offset, toward)]
        if rows is not None:
            source, target = source.at[rows], target.at[rows]
        device = {
            "half": spot.to_half,
            "right": spot.right,
            "left": spot.left,
            "core": spot.to_core,
        }[toward]
        pltpu.make_async_remote_copy(
            src_ref=source,
            dst_ref=target,
            send_sem=send_sem.at[at],
            recv_sem=sem,
            device_id=device,
            device_id_type=MESH,
        ).start()

    def landed(region, sem):
        pltpu.make_async_copy(region, region, sem).wait()

    def piece(at, turned, offset):
        return wholes[at].at[index(turned, offset)]

    expected, due = [], []

    def on_core(at, source, turned, offset):
        if across:
            number = turned * size + offset % size
            send(at, source, turned, offset, "core", core_sem.at[at, number])
            expected.append((at, turned, offset))

    def core_arrivals():
        for at, turned, offset in due:
            region = wholes[at].at[spot.index(turned, 1, offset % size)]
            landed(region, core_sem.at[at, turned * size + offset % size])
            ready(at, turned, offset, 1)
        due[:] = expected
        expected.clear()

    def on_ring(at, turned, source, offset, way, step, rows=None):
        toward = ("right", "left")[way]
        send(at, source, turned, offset, toward, ring_sem.at[at, turned, way, step], rows)

    locals_ = []
    for at in range(count):
        copy = pltpu.make_async_copy(shards[at], piece(at, 0, 0), local_sem.at[at])
        copy.start()
        locals_.append(copy)
    for at in range(count):
        if not ring_first[at]:
            send(at, shards[at], 0, 0, "half", half_sem.at[at, 0])
    for at in range(count):
        if ring_first[at]:
            on_ring(at, 0, shards[at], 0, 0, 1)
            on_ring(at, 0, shards[at], 0, 1, 1)
            send(at, shards[at], 0, 0, "half", half_sem.at[at, 0])
    for at in range(count):
        on_core(at, shards[at], 0, 0)
    for at in range(count):
        if not ring_first[at]:
            landed(piece(at, 1, 0), half_sem.at[at, 0])
            for way in (0, 1):
                on_ring(at, 0, shards[at], 0, way, 1)
                on_ring(at, 1, piece(at, 1, 0), 0, way, 1)
            on_core(at, piece(at, 1, 0), 1, 0)
    for at in range(count):
        locals_[at].wait()
        ready(at, 0, 0, 0)
        if not ring_first[at]:
            ready(at, 1, 0, 0)
        tick()

    def turned_arrivals(at, step):
        offsets = (0,) if step == 0 else (far,) if step == far else (-step, step)
        for offset in offsets:
            landed(piece(at, 1, offset), half_sem.at[at, offset % size])
            on_core(at, piece(at, 1, offset), 1, offset)
            came.append((at, 1, offset))

    came = []

    def flush():
        for one in came:
            ready(*one, 0)
        came.clear()
        core_arrivals()
        tick()

    for step in range(1, far + 1):
        for at in range(count):
            rows = shards[at].shape[0]
            cut = cut_of(rows)
            if ring_first[at]:
                if step < far:
                    for way in (0, 1):
                        offset = (-step, step)[way]
                        here = piece(at, 0, offset)
                        landed(here, ring_sem.at[at, 0, way, step])
                        if step < far - 1:
                            on_ring(at, 0, here, offset, way, step + 1)
                        elif way == 0:
                            on_ring(at, 0, here, offset, way, step + 1, pl.ds(0, cut))
                        elif cut < rows:
                            on_ring(at, 0, here, offset, way, step + 1, pl.ds(cut, rows - cut))
                        send(at, here, 0, offset, "half", half_sem.at[at, offset % size])
                        on_core(at, here, 0, offset)
                        came.append((at, 0, offset))
                else:
                    here = piece(at, 0, far)
                    landed(here.at[pl.ds(0, cut)], ring_sem.at[at, 0, 0, step])
                    if cut < rows:
                        landed(here.at[pl.ds(cut, rows - cut)], ring_sem.at[at, 0, 1, step])
                    send(at, here, 0, far, "half", half_sem.at[at, far])
                    on_core(at, here, 0, far)
                    came.append((at, 0, far))
                turned_arrivals(at, step - 1)
            else:
                for way in (0, 1):
                    for turned in (0, 1):
                        if step == far and turned != way:
                            continue
                        offset = (-step, step)[way]
                        here = piece(at, turned, offset)
                        landed(here, ring_sem.at[at, turned, way, step])
                        if step < far - 1 or (step == far - 1 and turned == way):
                            on_ring(at, turned, here, offset, way, step + 1)
                        on_core(at, here, turned, offset)
                        came.append((at, turned, offset))
            flush()
    for at in range(count):
        if ring_first[at]:
            turned_arrivals(at, far)
            flush()
    core_arrivals()
    core_arrivals()
    for at in range(count):
        sent = 4 * size - 1 if across else 2 * size - 1
        landed(wholes[at].at[pl.ds(0, sent)], send_sem.at[at])


def gather_sems(count, size):
    return [
        pltpu.SemaphoreType.DMA((count, 2, 2, size // 2 + 1)),
        pltpu.SemaphoreType.DMA((count, size)),
        pltpu.SemaphoreType.DMA((count, 2 * size)),
        pltpu.SemaphoreType.DMA((count,)),
        pltpu.SemaphoreType.DMA((count,)),
    ]


def look_up_body(size, ring_first, *refs):
    count = len(ring_first)
    shards, (table_own, ids) = refs[:count], refs[count : count + 2]
    refs = refs[count + 2 :]
    wholes, (table_out, found) = refs[:count], refs[count : count + 2]
    table, hot, stage, table_sem, stage_sem, *sems = refs[count + 2 :]
    spot = Spot(size)
    spot.meet(True)
    height = table_own.shape[0]
    mine = pltpu.make_async_copy(table_own, table.at[pl.ds(0, height)], table_sem.at[0])
    mine.start()
    swap = pltpu.make_async_remote_copy(
        src_ref=table_own,
        dst_ref=table.at[pl.ds(height, height)],
        send_sem=table_sem.at[1],
        recv_sem=table_sem.at[2],
        device_id=spot.to_core,
        device_id_type=MESH,
    )
    swap.start()
    out = pltpu.make_async_copy(table, table_out, table_sem.at[3])
    pieces, rows = found.shape[:2]
    width = 256
    state = {"ticks": 0, "done": 0}

    def copy_out(number):
        slot = lax.rem(number, 2)
        return pltpu.make_async_copy(stage.at[slot], found.at[number], stage_sem.at[slot])

    def work(first, last):
        def one(number, nothing):
            columns = lax.broadcasted_iota(jnp.int32, (rows, 2 * height), 1)
            hot[...] = jnp.where(columns == ids[number], 1.0, 0.0).astype(jnp.bfloat16)

            @pl.when(number >= 2)
            def _():
                copy_out(number - 2).wait()

            def part(at, nothing):
                window = pl.ds(pl.multiple_of(at * width, width), width)
                stage[lax.rem(number, 2), :, window] = jnp.dot(
                    hot[...], table[:, window], preferred_element_type=jnp.float32
                ).astype(jnp.bfloat16)
                return nothing

            lax.fori_loop(0, D // width, part, 0)
            copy_out(number).start()
            return nothing

        lax.fori_loop(first, last, one, 0)

    def tick(share=1):
        if state["done"] == pieces:
            return
        if state["done"] == 0:
            mine.wait()
            swap.wait_recv()
            out.start()
        last = min(pieces, state["done"] + share)
        work(state["done"], last)
        state["done"] = last

    gather_steps(
        size, ring_first, True, shards, wholes, sems, spot, tick, lambda at, turned, offset, other: None
    )
    tick(pieces)
    copy_out(pieces - 2).wait()
    copy_out(pieces - 1).wait()
    out.wait()
    swap.wait_send()


def look_up_call(size, shards, ring_first, table_own, ids, number):
    count = len(shards)
    height = table_own.shape[0]
    found = ids.shape[:2] + (D,)
    outs = [jax.ShapeDtypeStruct((4 * size,) + a.shape, a.dtype) for a in shards]
    outs.append(jax.ShapeDtypeStruct((2 * height, D), table_own.dtype))
    outs.append(jax.ShapeDtypeStruct(found, table_own.dtype))
    return pl.pallas_call(
        functools.partial(look_up_body, size, ring_first),
        out_shape=outs,
        in_specs=[pl.BlockSpec(memory_space=pl.ANY)] * (count + 1)
        + [pl.BlockSpec(memory_space=pltpu.VMEM)],
        out_specs=[pl.BlockSpec(memory_space=pl.ANY)] * (count + 2),
        scratch_shapes=[
            pltpu.VMEM((2 * height, D), table_own.dtype),
            pltpu.VMEM((ids.shape[1], 2 * height), table_own.dtype),
            pltpu.VMEM((2,) + found[1:], table_own.dtype),
            pltpu.SemaphoreType.DMA((4,)),
            pltpu.SemaphoreType.DMA((2,)),
        ]
        + gather_sems(count, size),
        compiler_params=pltpu.CompilerParams(
            collective_id=number, has_side_effects=True, vmem_limit_bytes=48 * 1024 * 1024
        ),
    )(*shards, table_own, ids)


def spread_body(size, shared, *refs):
    near, rest, ids_near, ids_rest, start = refs[:5]
    table_out, place_out, squares_ref = refs[5:8]
    near_all, rest_all, total, core_in, table_sem, *sems = refs[8:]
    ids = (ids_near, ids_rest)
    wholes = (near_all, rest_all)
    spot = Spot(size)
    spot.meet(True)
    height, length = table_out.shape[0], near.shape[0]
    block = height // 4
    first = pltpu.make_async_copy(start.at[pl.ds(0, height)], total, table_sem.at[0])
    first.start()
    swap = pltpu.make_async_remote_copy(
        src_ref=start.at[pl.ds(height, height)],
        dst_ref=core_in,
        send_sem=table_sem.at[1],
        recv_sem=table_sem.at[2],
        device_id=spot.to_core,
        device_id_type=MESH,
    )
    swap.start()
    place_out[...] = jnp.zeros_like(place_out)
    device = (2 * spot.half + spot.core) * size + spot.wide
    own_place = pl.ds(pl.multiple_of(lax.rem(device * shared, length), 16), shared)
    waiting = []
    state = {"started": False}

    def spread():
        pieces = list(waiting)
        waiting.clear()
        if not state["started"]:
            first.wait()
            state["started"] = True

        def one(number, nothing):
            window = pl.ds(pl.multiple_of(number * block, 16), block)
            row = number * block + lax.broadcasted_iota(jnp.int32, (block, length), 0)
            value = total[window, :]
            for at, piece in pieces:
                hot = jnp.where(row == ids[at][piece], 1.0, 0.0).astype(jnp.bfloat16)
                value = value + jnp.dot(
                    hot, wholes[at][piece], preferred_element_type=jnp.float32
                )
            total[window, :] = value
            return nothing

        lax.fori_loop(0, 4, one, 0)
        for at, piece in pieces:
            place_out[at] += wholes[at][piece, own_place, :].astype(jnp.float32)

    def ready(at, turned, offset, other):
        waiting.append((at, spot.index(turned, other, offset % size)))

    def tick():
        if len(waiting) >= 6:
            spread()

    gather_steps(size, (True, False), True, (near, rest), wholes, sems, spot, tick, ready)
    if waiting:
        spread()
    swap.wait_recv()
    step = height // 4

    def add(number, squares):
        window = pl.ds(pl.multiple_of(number * step, 16), step)
        value = total[window, :] + core_in[window, :]
        total[window, :] = value
        return squares + jnp.sum(value * value, axis=0, keepdims=True)

    squares = lax.fori_loop(0, 4, add, jnp.zeros((1, D), jnp.float32))
    squares_ref[...] = jnp.broadcast_to(squares, squares_ref.shape)
    out = pltpu.make_async_copy(total, table_out, table_sem.at[0])
    out.start()
    swap.wait_send()
    out.wait()


def spread_call(size, near, rest, ids, start, shared, number):
    height = start.shape[0] // 2
    pieces = (4 * size,) + near.shape
    return pl.pallas_call(
        functools.partial(spread_body, size, shared),
        out_shape=[
            jax.ShapeDtypeStruct((height, D), jnp.float32),
            jax.ShapeDtypeStruct((2, shared, D), jnp.float32),
            jax.ShapeDtypeStruct((8, D), jnp.float32),
        ],
        in_specs=[pl.BlockSpec(memory_space=pl.ANY)] * 2
        + [pl.BlockSpec(memory_space=pltpu.VMEM)] * 2
        + [pl.BlockSpec(memory_space=pl.ANY)],
        out_specs=[
            pl.BlockSpec(memory_space=pl.ANY),
            pl.BlockSpec(memory_space=pltpu.VMEM),
            pl.BlockSpec(memory_space=pltpu.VMEM),
        ],
        scratch_shapes=[
            pltpu.VMEM(pieces, near.dtype),
            pltpu.VMEM(pieces, near.dtype),
            pltpu.VMEM((height, D), jnp.float32),
            pltpu.VMEM((height, D), jnp.float32),
            pltpu.SemaphoreType.DMA((3,)),
        ]
        + gather_sems(2, size),
        compiler_params=pltpu.CompilerParams(
            collective_id=number, has_side_effects=True, vmem_limit_bytes=60 * 1024 * 1024
        ),
    )(near, rest, *ids, start)


def plain_gather_body(size, ring_first, across, *refs):
    count = len(ring_first)
    spot = Spot(size)
    spot.meet(across)
    gather_steps(
        size,
        ring_first,
        across,
        refs[:count],
        refs[count : 2 * count],
        refs[2 * count :],
        spot,
        lambda: None,
        lambda at, turned, offset, other: None,
    )


def gather_call(size, shards, ring_first, across, number):
    count = len(shards)
    total = (4 if across else 2) * size
    return pl.pallas_call(
        functools.partial(plain_gather_body, size, ring_first, across),
        out_shape=[jax.ShapeDtypeStruct((total,) + a.shape, a.dtype) for a in shards],
        in_specs=[pl.BlockSpec(memory_space=pl.ANY)] * count,
        out_specs=[pl.BlockSpec(memory_space=pl.ANY)] * count,
        scratch_shapes=gather_sems(count, size),
        compiler_params=pltpu.CompilerParams(collective_id=number, has_side_effects=True),
    )(*shards)


def cast_body(size, everyone, own_ref, out_ref, come_sem, send_sem, local_sem):
    spot = Spot(size)
    group = (4 if everyone else 2) * size
    narrow = lax.axis_index("narrow")
    mine = (narrow if everyone else spot.half) * size + spot.wide

    def device(step):
        at = lax.rem(mine + step, group)
        block = lax.div(at, size)
        return (block if everyone else 2 * block + spot.core, lax.rem(at, size))

    barrier = pltpu.get_barrier_semaphore()

    def greet(step, nothing):
        pl.semaphore_signal(barrier, inc=1, device_id=device(step), device_id_type=MESH)
        return nothing

    def tell(step, nothing):
        pltpu.make_async_remote_copy(
            src_ref=own_ref,
            dst_ref=out_ref.at[mine],
            send_sem=send_sem,
            recv_sem=come_sem,
            device_id=device(step),
            device_id_type=MESH,
        ).start()
        return nothing

    lax.fori_loop(1, group, greet, 0)
    keep = pltpu.make_async_copy(own_ref, out_ref.at[mine], local_sem)
    keep.start()
    pl.semaphore_wait(barrier, group - 1)
    lax.fori_loop(1, group, tell, 0)
    others = out_ref.at[pl.ds(0, group - 1)]
    pltpu.make_async_copy(others, others, come_sem).wait()
    pltpu.make_async_copy(others, others, send_sem).wait()
    keep.wait()


def cast_call(size, block, everyone, number):
    group = (4 if everyone else 2) * size
    return pl.pallas_call(
        functools.partial(cast_body, size, everyone),
        out_shape=jax.ShapeDtypeStruct((group,) + block.shape, block.dtype),
        in_specs=[pl.BlockSpec(memory_space=pltpu.VMEM)],
        out_specs=pl.BlockSpec(memory_space=pltpu.VMEM),
        scratch_shapes=[pltpu.SemaphoreType.DMA] * 3,
        compiler_params=pltpu.CompilerParams(collective_id=number, has_side_effects=True),
    )(block)


def scatter_body(size, half_first, across, bases, working, *refs):
    count = len(half_first)
    extra_in = FeedBack.INPUTS if working else 0
    extra_out = FeedBack.OUTPUTS if working else 0
    arrays, refs = refs[:count], refs[count:]
    work_in, refs = refs[:extra_in], refs[extra_in:]
    outs, squares_ref, refs = refs[:count], refs[count], refs[count + 1 :]
    work_out, refs = refs[:extra_out], refs[extra_out:]
    own, core_in, half_in, ring_in = (
        refs[part * count : (1 + part) * count] for part in range(4)
    )
    local_sem, core_sem, half_sem, ring_sem, send_sem = refs[4 * count : 4 * count + 5]
    work = FeedBack(work_in, work_out, refs[4 * count + 5 :]) if working else None
    squares = []
    spot = Spot(size)
    far = size // 2
    slots = [far] + [o for at in range(far - 1, 0, -1) for o in (at, -at)] + [0]
    sent = []

    def landed(region, sem):
        pltpu.make_async_copy(region, region, sem).wait()

    def send(source, target, device, number, at, sem):
        copy = pltpu.make_async_remote_copy(
            src_ref=source,
            dst_ref=target,
            send_sem=send_sem.at[at, number],
            recv_sem=sem,
            device_id=device,
            device_id_type=MESH,
        )
        copy.start()
        sent.append(copy)

    def source_of(at, turned, other_core, offset):
        if across:
            return arrays[at].at[spot.index(turned, other_core, offset % size)]
        base, stride = bases[at]
        return arrays[at].at[base + stride * (turned * size + offset % size)]

    def add(target, parts):
        rows, columns = target.shape
        width = 512 if columns % 512 == 0 else 256 if columns % 256 == 0 else 128

        def one(step, nothing):
            window = pl.ds(pl.multiple_of(step * width, width), width)
            if len(parts) == 2 and parts[1][1:] == (0, rows):
                one, two = parts[0][0][:, window], parts[1][0][:, window]
                if one.dtype == target.dtype:
                    target[:, window] = one + two
                    return nothing
            total = parts[0][0][:, window].astype(jnp.float32)
            for part, first, last in parts[1:]:
                if first == 0 and last == rows:
                    total = total + part[:, window].astype(jnp.float32)
            target[:, window] = total.astype(target.dtype)
            for part, first, last in parts[1:]:
                if first != 0 or last != rows:
                    span = pl.ds(first, last - first)
                    target[span, window] = (
                        total[first:last] + part[span, window].astype(jnp.float32)
                    ).astype(target.dtype)
            return nothing

        lax.fori_loop(0, columns // width, one, 0)

    def square_sum(ref):
        width = 128

        def one(step, total):
            part = ref[:, pl.ds(pl.multiple_of(step * width, width), width)].astype(jnp.float32)
            return total + jnp.sum(part * part, axis=0, keepdims=True)

        return lax.fori_loop(
            0, ref.shape[1] // width, one, jnp.zeros((1, width), jnp.float32)
        )

    def ring_slot(way, step):
        return way * far + step - 1

    def base(at, turned, offset):
        k = offset % size
        rows = own[at].shape[1]
        here = own[at].at[turned * size + k]
        landed(here, local_sem.at[at, turned * size + k])
        parts = [(here, 0, rows)]
        if across:
            there = core_in[at].at[turned * size + k]
            landed(there, core_sem.at[at, turned * size + k])
            parts.append((there, 0, rows))
        return here, parts

    def ring_parts(at, turned, offset):
        parts = []
        rows = own[at].shape[1]
        cut = cut_of(rows)
        ways = (0, 1) if offset == 0 else (0,) if offset > 0 else (1,)
        for way in ways:
            step = far - abs(offset)
            slot = ring_slot(way, step)
            if half_first[at]:
                if step == 1:
                    first, last = (0, cut) if way == 0 else (cut, rows)
                else:
                    first, last = 0, rows
                if first == last:
                    continue
                region = ring_in[at].at[slot]
                span = region if (first, last) == (0, rows) else region.at[pl.ds(first, last - first)]
                landed(span, ring_sem.at[at, slot])
                parts.append((region, first, last))
            else:
                if step == 1 and turned != way:
                    continue
                region = ring_in[at].at[turned * 2 * far + slot]
                landed(region, ring_sem.at[at, turned * 2 * far + slot])
                parts.append((region, 0, rows))
        return parts

    def ring_send(at, turned, offset):
        here = own[at].at[turned * size + offset % size]
        rows = own[at].shape[1]
        cut = cut_of(rows)
        step = far - abs(offset) + 1
        if offset == far:
            if half_first[at]:
                spans = [(0, pl.ds(0, cut))] + ([(1, pl.ds(cut, rows - cut))] if cut < rows else [])
                for way, span in spans:
                    slot = ring_slot(way, 1)
                    send(
                        here.at[span],
                        ring_in[at].at[slot].at[span],
                        (spot.right, spot.left)[way],
                        slot,
                        at,
                        ring_sem.at[at, slot],
                    )
                return
            ways = (turned,)
        else:
            ways = (0,) if offset > 0 else (1,)
        for way in ways:
            slot = ring_slot(way, step) + (0 if half_first[at] else turned * 2 * far)
            send(
                here,
                ring_in[at].at[slot],
                (spot.right, spot.left)[way],
                slot,
                at,
                ring_sem.at[at, slot],
            )

    spot.meet(across)
    core_base = 4 * far + size
    for offset in slots:
        k = offset % size
        for turned in (1, 0):
            for at in range(count):
                if across:
                    send(
                        source_of(at, turned, 1, offset),
                        core_in[at].at[turned * size + k],
                        spot.to_core,
                        core_base + turned * size + k,
                        at,
                        core_sem.at[at, turned * size + k],
                    )
                pltpu.make_async_copy(
                    source_of(at, turned, 0, offset),
                    own[at].at[turned * size + k],
                    local_sem.at[at, turned * size + k],
                ).start()

    if working:
        work.start()

    def turned_half(offset):
        for at in range(count):
            if half_first[at]:
                here, parts = base(at, 1, offset)
                k = offset % size
                if across:
                    add(here, parts)
                send(here, half_in[at].at[k], spot.to_half, 4 * far + k, at, half_sem.at[at, k])

    def straight(offset):
        for at in range(count):
            if half_first[at]:
                here, parts = base(at, 0, offset)
                k = offset % size
                landed(half_in[at].at[k], half_sem.at[at, k])
                parts.append((half_in[at].at[k], 0, own[at].shape[1]))
                parts += ring_parts(at, 0, offset) if offset != far else []
                if offset == 0:
                    add(outs[at], parts)
                    squares.append(square_sum(outs[at]))
                else:
                    add(here, parts)
                    ring_send(at, 0, offset)

    def both(offset):
        for at in range(count):
            if not half_first[at]:
                for turned in (1, 0):
                    here, parts = base(at, turned, offset)
                    parts += ring_parts(at, turned, offset) if offset != far else []
                    if offset == 0 and turned == 0:
                        landed(half_in[at].at[0], half_sem.at[at, 0])
                        parts.append((half_in[at].at[0], 0, own[at].shape[1]))
                        add(outs[at], parts)
                        squares.append(square_sum(outs[at]))
                        continue
                    if len(parts) > 1:
                        add(here, parts)
                    if offset == 0:
                        send(here, half_in[at].at[0], spot.to_half, 4 * far, at, half_sem.at[at, 0])
                    else:
                        ring_send(at, turned, offset)

    groups = [[far]] + [[at, -at] for at in range(far - 1, 0, -1)] + [[0]]
    def tick():
        if working:
            work.tick()

    tick()
    for number, group in enumerate(groups):
        for offset in group:
            turned_half(offset)
        tick()
        for offset in group:
            both(offset)
        tick()
        if number > 0:
            for offset in groups[number - 1]:
                straight(offset)
            tick()
    for offset in groups[-1]:
        straight(offset)
    total = squares[0]
    for one in squares[1:]:
        total = total + one
    squares_ref[...] = jnp.broadcast_to(total, squares_ref.shape)
    if working:
        work.finish()
    for copy in sent:
        copy.wait_send()


def scatter_call(size, arrays, half_first, across, out_type, number, bases=None, work=None):
    count = len(arrays)
    far = size // 2
    pieces = [a.shape[1:] for a in arrays]
    own = [pltpu.VMEM((2 * size,) + p, a.dtype) for p, a in zip(pieces, arrays)]
    core_in = [
        pltpu.VMEM((2 * size if across else 1,) + p, a.dtype) for p, a in zip(pieces, arrays)
    ]
    half_in = [
        pltpu.VMEM((size if first else 1,) + p, a.dtype)
        for p, a, first in zip(pieces, arrays, half_first)
    ]
    ring_in = [
        pltpu.VMEM((2 * far if first else 4 * far,) + p, a.dtype)
        for p, a, first in zip(pieces, arrays, half_first)
    ]
    outs = [jax.ShapeDtypeStruct(p, out_type) for p in pieces]
    outs.append(jax.ShapeDtypeStruct((8, 128), jnp.float32))
    in_specs = [pl.BlockSpec(memory_space=pl.ANY)] * count
    out_specs = [pl.BlockSpec(memory_space=pltpu.VMEM)] * (count + 1)
    scratch = (
        own
        + core_in
        + half_in
        + ring_in
        + [
            pltpu.SemaphoreType.DMA((count, 2 * size)),
            pltpu.SemaphoreType.DMA((count, 2 * size)),
            pltpu.SemaphoreType.DMA((count, size)),
            pltpu.SemaphoreType.DMA((count, 4 * far)),
            pltpu.SemaphoreType.DMA((count, 4 * far + 3 * size)),
        ]
    )
    if work is not None:
        in_specs += FeedBack.in_specs()
        outs += FeedBack.out_shape(work[0], work[4])
        out_specs += FeedBack.out_specs()
        scratch += FeedBack.scratch(work[0].shape[0])
    return pl.pallas_call(
        functools.partial(
            scatter_body, size, half_first, across, bases or ((0, 1),) * count, work is not None
        ),
        out_shape=outs,
        in_specs=in_specs,
        out_specs=out_specs,
        scratch_shapes=scratch,
        compiler_params=pltpu.CompilerParams(
            collective_id=number, has_side_effects=True, vmem_limit_bytes=60 * 1024 * 1024
        ),
    )(*arrays, *(work or ()))


def layer_norm(values, gain, shift):
    center = values - jnp.mean(values, axis=-1, keepdims=True)
    spread = jnp.mean(center * center, axis=-1, keepdims=True)
    return center * lax.rsqrt(spread + 1e-05) * gain + shift


def gelu_tanh(values):
    return jax.nn.gelu(values, approximate=True)


INNER = (((1,), (1,)), ((), ()))
OUTER = (((0,), (0,)), ((), ()))


def dot_inner(one, two):
    return lax.dot_general(one, two, INNER, preferred_element_type=jnp.float32)


def dot_outer(one, two):
    return lax.dot_general(one, two, OUTER, preferred_element_type=jnp.float32)


def fill_mask(mask_ref, length):
    key = lax.broadcasted_iota(jnp.int32, mask_ref.shape, 0)
    query = lax.broadcasted_iota(jnp.int32, mask_ref.shape, 1)
    mask_ref[...] = jnp.where((key <= query) & (key < length), 0.0, -1e30)


def probs_by_key(query, key, mask):
    scores = dot_inner(key, query * 0.125) + mask
    raised = jnp.exp(scores - jnp.max(scores, axis=0, keepdims=True))
    return raised * (1.0 / jnp.sum(raised, axis=0, keepdims=True))


def attend_body(length_ref, query_ref, key_ref, value_ref, mixed_ref, mask_ref):
    @pl.when(pl.program_id(0) == 0)
    def _():
        fill_mask(mask_ref, length_ref[0])

    rows = query_ref.shape[0]
    block = rows // 2
    for at in range(2):
        here, seen = slice(at * block, (at + 1) * block), slice(0, (at + 1) * block)
        mixed = []
        for head in range(2):
            lanes = slice(head * HD, (head + 1) * HD)
            probs = probs_by_key(query_ref[here, lanes], key_ref[seen, lanes], mask_ref[seen, here])
            mixed.append(dot_outer(value_ref[seen, lanes], probs.astype(jnp.bfloat16)))
        mixed_ref[here, :] = jnp.concatenate(mixed).T.astype(jnp.bfloat16)


def attend(projected, seq_lengths):
    rows = projected.shape[0]
    pairs = HEADS // 2
    return pl.pallas_call(
        attend_body,
        grid=(pairs,),
        out_shape=jax.ShapeDtypeStruct((rows, D), jnp.bfloat16),
        in_specs=[
            pl.BlockSpec(memory_space=pltpu.SMEM),
            pl.BlockSpec((rows, 2 * HD), lambda p: (0, p)),
            pl.BlockSpec((rows, 2 * HD), lambda p: (0, pairs + p)),
            pl.BlockSpec((rows, 2 * HD), lambda p: (0, 2 * pairs + p)),
        ],
        out_specs=pl.BlockSpec((rows, 2 * HD), lambda p: (0, p)),
        scratch_shapes=[pltpu.VMEM((rows, rows), jnp.float32)],
        compiler_params=pltpu.CompilerParams(vmem_limit_bytes=32 * 1024 * 1024),
        cost_estimate=pl.CostEstimate(
            flops=4 * HEADS * rows * rows * HD, bytes_accessed=8 * rows * D, transcendentals=0
        ),
    )(seq_lengths, projected, projected, projected)


def attend_back_body(length_ref, query_ref, key_ref, value_ref, grad_ref, out_ref, mask_ref):
    @pl.when(pl.program_id(0) == 0)
    def _():
        fill_mask(mask_ref, length_ref[0])

    rows = query_ref.shape[0]
    block = rows // 2
    pair = pl.program_id(0)
    low = jnp.bfloat16
    grad_query, grad_key, grad_value = [], [], []
    for at in range(2):
        here, seen = slice(at * block, (at + 1) * block), slice(0, (at + 1) * block)
        heads = []
        for head in range(2):
            lanes = slice(head * HD, (head + 1) * HD)
            query, key = query_ref[here, lanes], key_ref[seen, lanes]
            grad = grad_ref[here, lanes]
            probs = probs_by_key(query, key, mask_ref[seen, here])
            grad_probs = dot_inner(value_ref[seen, lanes], grad)
            value_part = jnp.dot(probs.astype(low), grad, preferred_element_type=jnp.float32)
            key_dot = jnp.sum(grad_probs * probs, axis=0, keepdims=True)
            scores_low = (probs * (grad_probs - key_dot)).astype(low)
            key_part = jnp.dot(scores_low, query, preferred_element_type=jnp.float32) * 0.125
            heads.append((dot_outer(key, scores_low) * 0.125, key_part, value_part))
        grad_query.append(jnp.concatenate([part[0] for part in heads]).T)
        grad_key.append(jnp.concatenate([part[1] for part in heads], axis=1))
        grad_value.append(jnp.concatenate([part[2] for part in heads], axis=1))
    for part, parts in enumerate((grad_query, grad_key, grad_value)):
        window = pl.ds(pl.multiple_of(part * D + pair * 2 * HD, 2 * HD), 2 * HD)
        first = parts[0] if part == 0 else parts[0] + parts[1][:block]
        out_ref[:block, window] = first.astype(low)
        second = parts[1] if part == 0 else parts[1][block:]
        out_ref[block:, window] = second.astype(low)


def attend_back(projected, grad_mixed, seq_lengths):
    rows = projected.shape[0]
    pairs = HEADS // 2
    return pl.pallas_call(
        attend_back_body,
        grid=(pairs,),
        out_shape=jax.ShapeDtypeStruct((rows, 3 * D), jnp.bfloat16),
        in_specs=[
            pl.BlockSpec(memory_space=pltpu.SMEM),
            pl.BlockSpec((rows, 2 * HD), lambda p: (0, p)),
            pl.BlockSpec((rows, 2 * HD), lambda p: (0, pairs + p)),
            pl.BlockSpec((rows, 2 * HD), lambda p: (0, 2 * pairs + p)),
            pl.BlockSpec((rows, 2 * HD), lambda p: (0, p)),
        ],
        out_specs=pl.BlockSpec((rows, 3 * D), lambda p: (0, 0)),
        scratch_shapes=[pltpu.VMEM((rows, rows), jnp.float32)],
        compiler_params=pltpu.CompilerParams(vmem_limit_bytes=48 * 1024 * 1024),
        cost_estimate=pl.CostEstimate(
            flops=10 * HEADS * rows * rows * HD, bytes_accessed=16 * rows * D, transcendentals=0
        ),
    )(seq_lengths, projected, projected, projected, grad_mixed)


class FeedBack:
    CHUNK = 256
    INPUTS = 6
    OUTPUTS = 4

    def __init__(self, ins, outs, scratch):
        self.branch, self.turned, pre, hidden, w_fc, w_proj = ins
        self.grad_normed, self.bias, self.grad_fc, self.grad_proj = outs
        pre_in, hidden_in, fc_in, proj_in, self.fc_out, self.proj_out, self.in_sem, self.out_sem = scratch
        self.chunks = w_proj.shape[0] // self.CHUNK
        self.sources = (pre, hidden, w_fc, w_proj)
        self.slots = (pre_in, hidden_in, fc_in, proj_in)
        self.done = 0

    def span(self, number):
        return pl.ds(pl.multiple_of(number * self.CHUNK, self.CHUNK), self.CHUNK)

    def loads(self, number):
        slot = lax.rem(number, 2)
        for at, (source, place) in enumerate(zip(self.sources, self.slots)):
            here = source.at[self.span(number)] if at == 3 else source.at[:, self.span(number)]
            yield pltpu.make_async_copy(here, place.at[slot], self.in_sem.at[at, slot])

    def stores(self, number):
        slot = lax.rem(number, 2)
        yield pltpu.make_async_copy(
            self.fc_out.at[slot], self.grad_fc.at[:, self.span(number)], self.out_sem.at[0, slot]
        )
        yield pltpu.make_async_copy(
            self.proj_out.at[slot], self.grad_proj.at[self.span(number)], self.out_sem.at[1, slot]
        )

    def start(self):
        self.grad_normed[...] = jnp.zeros_like(self.grad_normed)
        for copy in self.loads(0):
            copy.start()

    def run(self, first, last):
        def one(number, nothing):
            slot = lax.rem(number, 2)
            for copy in self.loads(number):
                copy.wait()

            @pl.when(number + 1 < self.chunks)
            def _():
                for copy in self.loads(number + 1):
                    copy.start()

            @pl.when(number >= 2)
            def _():
                for copy in self.stores(number - 2):
                    copy.wait()

            low = jnp.bfloat16
            pre_in, hidden_in, fc_in, proj_in = self.slots
            grad_hidden = dot_inner(self.branch[...], proj_in[slot])
            value = pre_in[slot]
            square = value * value
            bent = jnp.tanh(0.7978845608 * value * (1.0 + 0.044715 * square))
            slope = 0.5 * (1.0 + bent) + 0.5 * value * (1.0 - bent * bent) * (
                0.7978845608 * (1.0 + 3.0 * 0.044715 * square)
            )
            pre_low = (grad_hidden * slope).astype(low)
            self.bias[:, self.span(number)] = jnp.sum(
                pre_low.astype(jnp.float32), axis=0, keepdims=True
            )
            self.grad_normed[...] += dot_inner(pre_low, fc_in[slot])
            self.fc_out[slot] = jnp.dot(
                self.turned[...], pre_low, preferred_element_type=jnp.float32
            ).astype(low)
            self.proj_out[slot] = dot_outer(hidden_in[slot], self.branch[...]).astype(low)
            for copy in self.stores(number):
                copy.start()
            return nothing

        lax.fori_loop(first, last, one, 0)

    def tick(self):
        if self.done < self.chunks:
            self.run(self.done, self.done + 1)
            self.done += 1

    def finish(self):
        if self.done < self.chunks:
            self.run(self.done, self.chunks)
        for number in (self.chunks - 2, self.chunks - 1):
            for copy in self.stores(jnp.int32(number)):
                copy.wait()

    @classmethod
    def in_specs(cls):
        return [pl.BlockSpec(memory_space=pltpu.VMEM)] * 2 + [pl.BlockSpec(memory_space=pl.ANY)] * 4

    @classmethod
    def out_specs(cls):
        return [pl.BlockSpec(memory_space=pltpu.VMEM)] * 2 + [pl.BlockSpec(memory_space=pl.ANY)] * 2

    @classmethod
    def out_shape(cls, branch, w_fc):
        hidden = w_fc.shape[1]
        return [
            jax.ShapeDtypeStruct(branch.shape, jnp.float32),
            jax.ShapeDtypeStruct((1, hidden), jnp.float32),
            jax.ShapeDtypeStruct((D, hidden), jnp.bfloat16),
            jax.ShapeDtypeStruct((hidden, D), jnp.bfloat16),
        ]

    @classmethod
    def scratch(cls, rows):
        low, chunk = jnp.bfloat16, cls.CHUNK
        return [
            pltpu.VMEM((2, rows, chunk), jnp.float32),
            pltpu.VMEM((2, rows, chunk), low),
            pltpu.VMEM((2, D, chunk), low),
            pltpu.VMEM((2, chunk, D), low),
            pltpu.VMEM((2, D, chunk), low),
            pltpu.VMEM((2, chunk, D), low),
            pltpu.SemaphoreType.DMA((4, 2)),
            pltpu.SemaphoreType.DMA((2, 2)),
        ]


def feed_back_body(*refs):
    ins, outs = FeedBack.INPUTS, FeedBack.OUTPUTS
    work = FeedBack(refs[:ins], refs[ins : ins + outs], refs[ins + outs :])
    work.start()
    work.finish()


def feed_back(operands):
    branch, w_fc = operands[0], operands[4]
    return pl.pallas_call(
        feed_back_body,
        out_shape=FeedBack.out_shape(branch, w_fc),
        in_specs=FeedBack.in_specs(),
        out_specs=FeedBack.out_specs(),
        scratch_shapes=FeedBack.scratch(branch.shape[0]),
        compiler_params=pltpu.CompilerParams(vmem_limit_bytes=40 * 1024 * 1024),
    )(*operands)


def layer_forward(stream, weights, vector, seq_lengths):
    w_qkv, w_out, w_fc, w_proj = weights
    normed_low = layer_norm(stream, vector[0:D], vector[D : 2 * D]).astype(jnp.bfloat16)
    qkv_bias = jnp.concatenate(
        [vector[4 * D : 5 * D], jnp.zeros((D,), jnp.float32), vector[5 * D : 6 * D]]
    )
    projected = (jnp.dot(normed_low, w_qkv, preferred_element_type=jnp.float32) + qkv_bias).astype(
        jnp.bfloat16
    )
    mixed_low = attend(projected, seq_lengths)
    stream_mid = (
        stream
        + jnp.dot(mixed_low, w_out, preferred_element_type=jnp.float32)
        + vector[6 * D : 7 * D]
    )
    normed_two = layer_norm(stream_mid, vector[2 * D : 3 * D], vector[3 * D : 4 * D]).astype(
        jnp.bfloat16
    )
    hidden_pre = (
        jnp.dot(normed_two, w_fc, preferred_element_type=jnp.float32) + vector[8 * D : 8 * D + FF]
    )
    hidden_low = gelu_tanh(hidden_pre).astype(jnp.bfloat16)
    stream_out = (
        stream_mid
        + jnp.dot(hidden_low, w_proj, preferred_element_type=jnp.float32)
        + vector[7 * D : 8 * D]
    )
    return (
        stream_out,
        (
            stream,
            normed_low,
            projected,
            mixed_low,
            stream_mid,
            normed_two,
            hidden_pre,
            hidden_low,
        ),
    )


def feed_plain(operands):
    branch_low, normed_turned, hidden_pre, hidden_low, w_fc, w_proj = operands
    grad_wproj = jnp.dot(hidden_low.T, branch_low, preferred_element_type=jnp.bfloat16)
    grad_hidden = jnp.dot(branch_low, w_proj.T, preferred_element_type=jnp.float32)
    pre_low = jax.vjp(gelu_tanh, hidden_pre)[1](grad_hidden)[0].astype(jnp.bfloat16)
    grad_wfc = jnp.dot(normed_turned, pre_low, preferred_element_type=jnp.bfloat16)
    grad_normed_two = jnp.dot(pre_low, w_fc.T, preferred_element_type=jnp.float32)
    bias = jnp.sum(pre_low.astype(jnp.float32), axis=0)
    return grad_normed_two, bias, grad_wfc, grad_wproj


def layer_backward(grad_out, saved_acts, weights, vector, seq_lengths, feed):
    (
        stream,
        normed_low,
        projected,
        mixed_low,
        stream_mid,
        normed_two,
        hidden_pre,
        hidden_low,
    ) = saved_acts
    w_qkv, w_out, w_fc, w_proj = weights
    branch_low = grad_out.astype(jnp.bfloat16)
    grad_normed_two, grad_bias, grad_wfc, grad_wproj = feed(
        (branch_low, normed_two.T, hidden_pre, hidden_low, w_fc, w_proj)
    )
    grad_mid, grad_gain_two, grad_shift_two = jax.vjp(
        layer_norm, stream_mid, vector[2 * D : 3 * D], vector[3 * D : 4 * D]
    )[1](grad_normed_two)
    grad_mid = grad_mid + grad_out
    attn_low = grad_mid.astype(jnp.bfloat16)
    grad_wout = jnp.dot(mixed_low.T, attn_low, preferred_element_type=jnp.bfloat16)
    grad_mixed = jnp.dot(attn_low, w_out.T, preferred_element_type=jnp.float32).astype(
        jnp.bfloat16
    )
    qkv_low = attend_back(projected, grad_mixed, seq_lengths)
    grad_wqkv = jnp.dot(normed_low.T, qkv_low, preferred_element_type=jnp.bfloat16)
    grad_normed = jnp.dot(qkv_low, w_qkv.T, preferred_element_type=jnp.float32)
    grad_input, grad_gain_one, grad_shift_one = jax.vjp(
        layer_norm, stream, vector[0:D], vector[D : 2 * D]
    )[1](grad_normed)
    bias_qkv = jnp.sum(qkv_low.astype(jnp.float32), axis=0)
    grad_vector = jnp.concatenate(
        [
            grad_gain_one,
            grad_shift_one,
            grad_gain_two,
            grad_shift_two,
            bias_qkv[0:D],
            bias_qkv[2 * D : 3 * D],
            jnp.sum(attn_low.astype(jnp.float32), axis=0),
            jnp.sum(branch_low.astype(jnp.float32), axis=0),
            grad_bias.reshape(-1),
        ]
    )
    return (grad_input + grad_mid, (grad_wqkv, grad_wout, grad_wfc, grad_wproj), grad_vector)


def adamw(weight, moment_one, moment_two, gradient, step_rate, decay_rate, step_float):
    one_new = 0.5 * moment_one + 0.5 * gradient
    two_new = 0.5 * moment_two + 0.5 * gradient * gradient
    fix_scale = 1.0 - jnp.power(0.5, step_float)
    update = one_new / fix_scale / (jnp.sqrt(two_new / fix_scale) + 1e-08)
    return (weight - step_rate * (update + decay_rate * weight), one_new, two_new)


def on_device(
    token_ids,
    seq_lengths,
    loss_slots,
    target_ids,
    step_count,
    w_qkv,
    w_out,
    w_fc,
    w_proj,
    vectors,
    pos_table,
    embed_table,
    mom_qkv,
    mom_out,
    mom_fc,
    mom_proj,
    mom_vectors,
    mom_pos,
    mom_embed,
    sec_qkv,
    sec_out,
    sec_fc,
    sec_proj,
    sec_vectors,
    sec_pos,
    sec_embed,
):
    per_layer = 8 * D + FF
    net = Net()
    size, halves = net.size, net.halves
    same_core = halves * size
    devices = 2 * same_core
    low = jnp.bfloat16
    near = LEN // 2
    fused = size <= 8
    rest = LEN - near
    slots = loss_slots.shape[0]

    half_of = jnp.arange(halves)[:, None]
    wide_index = jnp.arange(size)[None, :]
    place_of = jnp.where(wide_index % 2 == 0, wide_index // 2, size - 1 - (wide_index - 1) // 2)
    to_device = ((half_of ^ net.half) * size + (place_of - net.place) % size).reshape(-1)
    offsets = (net.place + wide_index) % size
    wide_there = jnp.where(offsets < size // 2, 2 * offsets, 2 * (size - 1 - offsets) + 1)
    from_device = ((half_of ^ net.half) * size + wide_there).reshape(-1)

    numbers = jnp.concatenate([token_ids, loss_slots, target_ids, seq_lengths])
    numbers = jnp.pad(numbers, (0, -numbers.shape[0] % 1024)).reshape(-1, 128)
    numbers = cast_call(size, numbers, True, 5).reshape(devices, -1)
    all_tokens = numbers[:, :LEN]
    token_total = jnp.sum(numbers[:, LEN + 2 * slots].astype(jnp.float32))
    on_core = from_device + (from_device // size + net.core) * size
    numbers = jnp.take(numbers, on_core, axis=0).reshape(halves, size, -1)
    group_tokens = numbers[:, :, :LEN]
    group_slots = numbers[:, :, LEN : LEN + slots].reshape(same_core * slots)
    group_targets = numbers[:, :, LEN + slots : LEN + 2 * slots].reshape(same_core * slots)

    own_rows = embed_table.shape[0]
    height = own_rows + -own_rows % 64
    chip_rows = 2 * height
    table_own = jnp.pad(embed_table.astype(low), ((0, height - own_rows), (0, 0)))
    own_start = net.device * own_rows
    other_start = (net.device + (1 - 2 * net.core) * size) * own_rows

    def locate(ids):
        mine = ids - own_start
        other = ids - other_start
        return jnp.where(
            (mine >= 0) & (mine < own_rows),
            mine,
            jnp.where((other >= 0) & (other < own_rows), other + height, -1),
        )

    def one_hot(ids):
        return (ids[:, None] == jnp.arange(chip_rows)[None, :]).astype(low)

    local_tokens = locate(group_tokens).reshape(same_core, LEN)
    ids_near, ids_rest = local_tokens[:, :near], local_tokens[:, near:]

    shared = pos_table.shape[0]
    vector_rows = -(-vectors.shape[0] // D)
    padded = jnp.pad(vectors, (0, vector_rows * D - vectors.shape[0])).reshape(vector_rows, D)
    spare = -(shared + vector_rows) % 16
    small_own = jnp.concatenate([pos_table, padded, jnp.zeros((spare, D), jnp.float32)])
    shards_low = []
    for layer_at in range(LAYERS):
        shards_low += [part[layer_at].astype(low) for part in (w_qkv, w_fc, w_proj, w_out)]
    shards_low.append(small_own.astype(low))
    ring_first = (True, True, False, False) * LAYERS + (False,)
    if fused:
        *gathered, table_low, found = look_up_call(
            size, shards_low, ring_first, table_own, jnp.concatenate([ids_near, ids_rest])[..., None], 1
        )
        stream = scatter_call(
            size, [found, found], (True, False), False, low, 2, ((0, 1), (same_core, 1))
        )
        stream = jnp.concatenate(stream[:2])
    else:
        gathered = gather_call(size, shards_low, ring_first, True, 1)
        table_low = jnp.concatenate([table_own, net.swap_core(table_own)])
        found = [
            jnp.dot(
                one_hot(ids.reshape(-1)), table_low, preferred_element_type=jnp.float32
            ).astype(low).reshape(same_core, -1, D)
            for ids in (ids_near, ids_rest)
        ]
        bands = max(1, same_core // 16)
        band = D // bands
        parts = []
        for at in range(bands):
            window = [part[:, :, at * band : (at + 1) * band] for part in found]
            parts.append(
                jnp.concatenate(scatter_call(size, window, (True, False), False, low, 2)[:2])
            )
        stream = jnp.concatenate(parts, axis=1)
    small_low = gathered[-1]
    pos_low = small_low[:, :shared].reshape(devices * shared, D)
    vector_all = (
        small_low[:, shared : shared + vector_rows]
        .reshape(devices, vector_rows * D)[:, : vectors.shape[0]]
        .reshape(-1)
        .astype(jnp.float32)
    )

    stream = stream.astype(jnp.float32) + pos_low[:LEN].astype(jnp.float32)

    kept_weights = []
    saved_list = []
    for layer_at in range(LAYERS):
        w_a, w_c, w_d, w_b = (
            part.reshape(-1, part.shape[2]) for part in gathered[layer_at * 4 : layer_at * 4 + 4]
        )
        weights = (w_a, w_b, w_c, w_d)
        kept_weights.append(weights)
        stream, saved_acts = layer_forward(
            stream, weights, vector_all[layer_at * per_layer : (layer_at + 1) * per_layer], seq_lengths
        )
        saved_list.append(saved_acts)
    tail_start = LAYERS * per_layer
    final_norm, final_pull = jax.vjp(
        layer_norm,
        stream,
        vector_all[tail_start : tail_start + D],
        vector_all[tail_start + D : tail_start + 2 * D],
    )
    slot_rows = jnp.maximum(loss_slots, 0)
    own_picked = final_norm[slot_rows].astype(low)
    some = slots // 2
    group_rows = jnp.concatenate(
        gather_call(size, [own_picked[:some], own_picked[some:]], (True, False), False, 6), axis=1
    ).reshape(same_core * slots, D)
    real = jnp.arange(chip_rows) % height < own_rows
    logits = jnp.where(
        real, jnp.dot(group_rows, table_low.T, preferred_element_type=jnp.float32), -1e30
    )
    target_onehot = locate(group_targets)[:, None] == jnp.arange(chip_rows)[None, :]
    row_max = jnp.max(logits, axis=-1)
    row_total = jnp.sum(jnp.exp(logits - row_max[:, None]), axis=-1)
    target_logit = jnp.sum(jnp.where(target_onehot, logits, 0.0), axis=-1)
    stats = jnp.stack([row_max, row_total, target_logit], axis=-1)
    stats = jnp.take(stats.reshape(same_core, slots * 3), to_device, axis=0)
    stats = stats.reshape(same_core * slots, 3).T.reshape(-1)
    entries = stats.shape[0]
    stats = jnp.pad(stats, (0, -entries % 1024)).reshape(-1, 128)
    stats = cast_call(size, stats, False, 7).reshape(same_core, -1)[:, :entries]
    stats = stats.reshape(same_core, 3, same_core * slots)
    joint_max = jnp.max(stats[:, 0], axis=0)
    joint_total = jnp.sum(stats[:, 1] * jnp.exp(stats[:, 0] - joint_max), axis=0)
    stats = jnp.stack([joint_max + jnp.log(joint_total), jnp.sum(stats[:, 2], axis=0)])
    stats = stats.reshape(2, same_core, slots)
    stats = jnp.take(stats, from_device, axis=1).reshape(2, same_core * slots)
    log_total, merged_target = stats[0], stats[1]
    group_used = (group_slots >= 0).astype(jnp.float32)
    own_loss = jnp.sum(((log_total - merged_target) * group_used)[:slots])
    grad_logits = (
        (jnp.exp(logits - log_total[:, None]) - target_onehot.astype(jnp.float32))
        * (group_used / token_total)[:, None]
    ).astype(low)
    grad_rows = jnp.dot(grad_logits, table_low, preferred_element_type=jnp.float32)
    grad_rows = grad_rows.reshape(2 * same_core, some, D)
    grad_rows = jnp.concatenate(
        scatter_call(
            size,
            [grad_rows, grad_rows],
            (True, False),
            False,
            jnp.float32,
            8,
            ((0, 2), (1, 2)),
        )[:2]
    )
    grad_final = jnp.zeros((LEN, D), jnp.float32).at[slot_rows].add(grad_rows)
    grad_stream, grad_gain_final, grad_shift_final = final_pull(grad_final)
    layer_shards = []
    vector_grads = []
    squares = jnp.float32(0)
    pending = None

    def reduce_layers(full_grads, number, more=(), work=None):
        grad_a, grad_b, grad_c, grad_d = full_grads
        arrays = [part.reshape(devices, -1, part.shape[1]) for part in (grad_a, grad_c, grad_d, grad_b)]
        arrays += more
        outs = scatter_call(
            size,
            arrays,
            (True, True, False, False) + (False,) * len(more),
            True,
            jnp.float32,
            number,
            work=work,
        )
        shard_a, shard_c, shard_d, shard_b, *rest = outs
        layer_shards.insert(0, (shard_a, shard_b, shard_c, shard_d))
        return rest

    for layer_at in reversed(range(LAYERS)):
        feed = feed_plain
        if pending is not None:
            held = []

            def feed(operands):
                sums, *results = reduce_layers(pending, 3, work=operands)
                held.append(jnp.sum(sums[0]))
                return results

        grad_stream, full_grads, grad_vector = layer_backward(
            grad_stream,
            saved_list[layer_at],
            kept_weights[layer_at],
            vector_all[layer_at * per_layer : (layer_at + 1) * per_layer],
            seq_lengths,
            feed,
        )
        if pending is not None:
            squares = squares + held[0]
        pending = full_grads
        vector_grads.insert(0, grad_vector)
    grad_low = grad_stream.astype(low)
    grad_near, grad_rest = grad_low[:near], grad_low[near:]
    grad_table = jnp.dot(grad_logits.T, group_rows, preferred_element_type=jnp.float32)
    if fused:
        ids = all_tokens - own_start
        ids = jnp.where((ids >= 0) & (ids < own_rows), ids, -1)[:, None]
        ids = [ids[:, :, :near], ids[:, :, near:]]
        grad_table, places, sums = spread_call(
            size, grad_near, grad_rest, ids, grad_table, shared, 4
        )
        squares = squares + jnp.sum(sums[0])
        first_place = net.device * shared
        pos_shard = jnp.where(
            first_place < near, places[0], jnp.where(first_place < LEN, places[1], 0.0)
        )
    else:
        wholes = gather_call(size, [grad_near, grad_rest], (True, False), False, 4)
        for ids, whole in zip((ids_near, ids_rest), wholes):
            grad_table = grad_table + jnp.dot(
                one_hot(ids.reshape(-1)).T, whole.reshape(-1, D), preferred_element_type=jnp.float32
            )
        grad_table = grad_table[:height] + net.swap_core(grad_table[height:])
        squares = squares + jnp.sum(grad_table * grad_table)
        grad_pos = jnp.concatenate(
            [jnp.sum(whole.astype(jnp.float32), axis=0) for whole in wholes]
        )
        grad_pos = jnp.pad(grad_pos, ((0, POS - LEN), (0, 0)))
        other_device = net.device + (1 - 2 * net.core) * size
        pos_shard = lax.dynamic_slice_in_dim(grad_pos, net.device * shared, shared) + net.swap_core(
            lax.dynamic_slice_in_dim(grad_pos, other_device * shared, shared)
        )
    table_shard = grad_table[:own_rows]
    grad_small = jnp.concatenate(vector_grads + [grad_gain_final, grad_shift_final])
    own_small = vectors.shape[0]
    grad_small = jnp.pad(grad_small.reshape(devices, own_small), ((0, 0), (0, -own_small % 1024)))
    small_shard, sums = reduce_layers(pending, 10, [grad_small.reshape(devices, -1, 128)])
    small_shard = small_shard.reshape(-1)[:own_small]
    squares = squares + jnp.sum(sums[0]) + jnp.sum(pos_shard * pos_shard)
    qkv_shard = jnp.stack([member[0] for member in layer_shards])
    out_shard = jnp.stack([member[1] for member in layer_shards])
    fc_shard = jnp.stack([member[2] for member in layer_shards])
    proj_shard = jnp.stack([member[3] for member in layer_shards])
    shards = (qkv_shard, out_shard, fc_shard, proj_shard, small_shard, pos_shard, table_shard)
    sums = jnp.pad(jnp.stack([own_loss, squares]), (0, 1022)).reshape(8, 128)
    sums = jnp.sum(cast_call(size, sums, True, 9), axis=0)
    loss_total, square_total = sums[0, 0], sums[0, 1]
    loss_value = loss_total / token_total
    grad_norm = jnp.sqrt(square_total)
    factor = CLIP_LIMIT / jnp.maximum(grad_norm, CLIP_LIMIT)
    step_float = step_count.astype(jnp.float32)
    params = (w_qkv, w_out, w_fc, w_proj, vectors, pos_table, embed_table)
    moments_one = (mom_qkv, mom_out, mom_fc, mom_proj, mom_vectors, mom_pos, mom_embed)
    moments_two = (sec_qkv, sec_out, sec_fc, sec_proj, sec_vectors, sec_pos, sec_embed)
    step_rates = (
        RATE_MATRIX,
        RATE_MATRIX,
        RATE_MATRIX,
        RATE_MATRIX,
        RATE_VECTOR,
        RATE_MATRIX,
        RATE_MATRIX,
    )
    decay_rates = (
        DECAY_MATRIX,
        DECAY_MATRIX,
        DECAY_MATRIX,
        DECAY_MATRIX,
        0.0,
        DECAY_MATRIX,
        DECAY_MATRIX,
    )
    results = [
        adamw(
            params[where_at],
            moments_one[where_at],
            moments_two[where_at],
            shards[where_at] * factor,
            step_rates[where_at],
            decay_rates[where_at],
            step_float,
        )
        for where_at in range(7)
    ]
    return (
        loss_value,
        grad_norm,
        results[0][0],
        results[1][0],
        results[2][0],
        results[3][0],
        results[4][0],
        results[5][0],
        results[6][0],
        results[0][1],
        results[1][1],
        results[2][1],
        results[3][1],
        results[4][1],
        results[5][1],
        results[6][1],
        results[0][2],
        results[1][2],
        results[2][2],
        results[3][2],
        results[4][2],
        results[5][2],
        results[6][2],
    )


def solution(mesh):
    return jax.shard_map(
        on_device,
        mesh=mesh,
        in_specs=(
            P(("narrow", "wide")),
            P(("narrow", "wide")),
            P(("narrow", "wide")),
            P(("narrow", "wide")),
            P(),
            P(None, ("narrow", "wide"), None),
            P(None, ("narrow", "wide"), None),
            P(None, ("narrow", "wide"), None),
            P(None, ("narrow", "wide"), None),
            P(("narrow", "wide")),
            P(("narrow", "wide"), None),
            P(("narrow", "wide"), None),
            P(None, ("narrow", "wide"), None),
            P(None, ("narrow", "wide"), None),
            P(None, ("narrow", "wide"), None),
            P(None, ("narrow", "wide"), None),
            P(("narrow", "wide")),
            P(("narrow", "wide"), None),
            P(("narrow", "wide"), None),
            P(None, ("narrow", "wide"), None),
            P(None, ("narrow", "wide"), None),
            P(None, ("narrow", "wide"), None),
            P(None, ("narrow", "wide"), None),
            P(("narrow", "wide")),
            P(("narrow", "wide"), None),
            P(("narrow", "wide"), None),
        ),
        out_specs=(
            P(),
            P(),
            P(None, ("narrow", "wide"), None),
            P(None, ("narrow", "wide"), None),
            P(None, ("narrow", "wide"), None),
            P(None, ("narrow", "wide"), None),
            P(("narrow", "wide")),
            P(("narrow", "wide"), None),
            P(("narrow", "wide"), None),
            P(None, ("narrow", "wide"), None),
            P(None, ("narrow", "wide"), None),
            P(None, ("narrow", "wide"), None),
            P(None, ("narrow", "wide"), None),
            P(("narrow", "wide")),
            P(("narrow", "wide"), None),
            P(("narrow", "wide"), None),
            P(None, ("narrow", "wide"), None),
            P(None, ("narrow", "wide"), None),
            P(None, ("narrow", "wide"), None),
            P(None, ("narrow", "wide"), None),
            P(("narrow", "wide")),
            P(("narrow", "wide"), None),
            P(("narrow", "wide"), None),
        ),
        check_vma=False,
    )
```

```python
import functools

import jax
import jax.numpy as jnp
from jax import lax
from jax.experimental import pallas as pl
from jax.experimental.pallas import tpu as pltpu
from jax.sharding import PartitionSpec as P

D = 1024
HEADS = 16
HD = 64
FF = 4096
POS = 1024
LAYERS = 2
LEN = 512
LOSS_DEV = 32


CLIP_LIMIT = 0.002
RATE_MATRIX = 0.03
RATE_VECTOR = 0.3
DECAY_MATRIX = 0.1


class Net:
    def __init__(self):
        self.narrow_at = lax.axis_index("narrow")
        self.wide_at = lax.axis_index("wide")
        self.narrow_size = lax.axis_size("narrow")
        self.size = lax.axis_size("wide")
        size = self.size
        self.core = self.narrow_at % 2
        self.half = self.narrow_at // 2
        self.halves = self.narrow_size // 2
        self.place = jnp.where(
            self.wide_at % 2 == 0, self.wide_at // 2, size - 1 - (self.wide_at - 1) // 2
        )
        self.device = self.narrow_at * size + self.wide_at
        order = list(range(0, size, 2)) + list(range(size - 1, 0, -2))
        pairs = [(n, w) for n in range(self.narrow_size) for w in range(size)]
        self.core_pairs = [(n * size + w, (n ^ 1) * size + w) for n, w in pairs]
        self.half_pairs = [(n * size + w, (n ^ 2) * size + w) for n, w in pairs]
        self.right = [
            (n * size + order[i], n * size + order[(i + 1) % size])
            for n in range(self.narrow_size)
            for i in range(size)
        ]
        self.left = [(later, earlier) for earlier, later in self.right]

    def step(self, array, pairs):
        return lax.ppermute(array, ("narrow", "wide"), pairs)

    def swap_core(self, array):
        return self.step(array, self.core_pairs)

    def swap_half(self, array):
        return self.step(array, self.half_pairs)

    def wide_of(self, offset):
        size = self.size
        at = lax.rem(self.place + offset, size)
        return jnp.where(at < size // 2, 2 * at, 2 * (size - 1 - at) + 1)


MESH = pl.DeviceIdType.MESH


class Spot:
    def __init__(self, size):
        self.size = size
        narrow, wide = lax.axis_index("narrow"), lax.axis_index("wide")
        odd = lax.rem(wide, 2)
        self.core, self.half = lax.rem(narrow, 2), lax.div(narrow, 2)
        self.wide = wide
        self.place = (1 - odd) * lax.div(wide, 2) + odd * (size - 1 - lax.div(wide, 2))
        self.to_core = (narrow + 1 - 2 * self.core, wide)
        self.to_half = (narrow + 2 - 4 * self.half, wide)
        self.right = (narrow, self.wide_of(1))
        self.left = (narrow, self.wide_of(size - 1))

    def wide_of(self, offset):
        at = lax.rem(self.place + offset, self.size)
        late = lax.div(at, self.size // 2)
        return (1 - late) * 2 * at + late * (2 * (self.size - 1 - at) + 1)

    def index(self, turned, other_core, offset):
        half = self.half + turned * (1 - 2 * self.half)
        core = self.core + other_core * (1 - 2 * self.core)
        return (2 * half + core) * self.size + self.wide_of(offset)

    def meet(self, with_core):
        barrier = pltpu.get_barrier_semaphore()
        peers = [self.to_half, self.right, self.left] + ([self.to_core] if with_core else [])
        for peer in peers:
            pl.semaphore_signal(barrier, inc=1, device_id=peer, device_id_type=MESH)
        pl.semaphore_wait(barrier, len(peers))


def cut_of(rows):
    return rows // 2 if rows % 32 == 0 else rows


def gather_steps(size, ring_first, across, shards, wholes, sems, spot, tick, ready):
    count = len(ring_first)
    ring_sem, half_sem, core_sem, send_sem, local_sem = sems
    far = size // 2

    def index(turned, offset, toward=None):
        if across:
            return spot.index(turned, 0, offset % size)
        if toward == "half":
            turned = 1 - turned
        offset = offset + {"right": -1, "left": 1}.get(toward, 0)
        return turned * size + offset % size

    def send(at, source, turned, offset, toward, sem, rows=None):
        target = wholes[at].at[index(turned, offset, toward)]
        if rows is not None:
            source, target = source.at[rows], target.at[rows]
        device = {
            "half": spot.to_half,
            "right": spot.right,
            "left": spot.left,
            "core": spot.to_core,
        }[toward]
        pltpu.make_async_remote_copy(
            src_ref=source,
            dst_ref=target,
            send_sem=send_sem.at[at],
            recv_sem=sem,
            device_id=device,
            device_id_type=MESH,
        ).start()

    def landed(region, sem):
        pltpu.make_async_copy(region, region, sem).wait()

    def piece(at, turned, offset):
        return wholes[at].at[index(turned, offset)]

    expected, due = [], []

    def on_core(at, source, turned, offset):
        if across:
            number = turned * size + offset % size
            send(at, source, turned, offset, "core", core_sem.at[at, number])
            expected.append((at, turned, offset))

    def core_arrivals():
        for at, turned, offset in due:
            region = wholes[at].at[spot.index(turned, 1, offset % size)]
            landed(region, core_sem.at[at, turned * size + offset % size])
            ready(at, turned, offset, 1)
        due[:] = expected
        expected.clear()

    def on_ring(at, turned, source, offset, way, step, rows=None):
        toward = ("right", "left")[way]
        send(at, source, turned, offset, toward, ring_sem.at[at, turned, way, step], rows)

    locals_ = []
    for at in range(count):
        copy = pltpu.make_async_copy(shards[at], piece(at, 0, 0), local_sem.at[at])
        copy.start()
        locals_.append(copy)
    for at in range(count):
        if not ring_first[at]:
            send(at, shards[at], 0, 0, "half", half_sem.at[at, 0])
    for at in range(count):
        if ring_first[at]:
            on_ring(at, 0, shards[at], 0, 0, 1)
            on_ring(at, 0, shards[at], 0, 1, 1)
            send(at, shards[at], 0, 0, "half", half_sem.at[at, 0])
    for at in range(count):
        on_core(at, shards[at], 0, 0)
    for at in range(count):
        if not ring_first[at]:
            landed(piece(at, 1, 0), half_sem.at[at, 0])
            for way in (0, 1):
                on_ring(at, 0, shards[at], 0, way, 1)
                on_ring(at, 1, piece(at, 1, 0), 0, way, 1)
            on_core(at, piece(at, 1, 0), 1, 0)
    for at in range(count):
        locals_[at].wait()
        ready(at, 0, 0, 0)
        if not ring_first[at]:
            ready(at, 1, 0, 0)
        tick()

    def turned_arrivals(at, step):
        offsets = (0,) if step == 0 else (far,) if step == far else (-step, step)
        for offset in offsets:
            landed(piece(at, 1, offset), half_sem.at[at, offset % size])
            on_core(at, piece(at, 1, offset), 1, offset)
            came.append((at, 1, offset))

    came = []

    def flush():
        for one in came:
            ready(*one, 0)
        came.clear()
        core_arrivals()
        tick()

    for step in range(1, far + 1):
        for at in range(count):
            rows = shards[at].shape[0]
            cut = cut_of(rows)
            if ring_first[at]:
                if step < far:
                    for way in (0, 1):
                        offset = (-step, step)[way]
                        here = piece(at, 0, offset)
                        landed(here, ring_sem.at[at, 0, way, step])
                        if step < far - 1:
                            on_ring(at, 0, here, offset, way, step + 1)
                        elif way == 0:
                            on_ring(at, 0, here, offset, way, step + 1, pl.ds(0, cut))
                        elif cut < rows:
                            on_ring(at, 0, here, offset, way, step + 1, pl.ds(cut, rows - cut))
                        send(at, here, 0, offset, "half", half_sem.at[at, offset % size])
                        on_core(at, here, 0, offset)
                        came.append((at, 0, offset))
                else:
                    here = piece(at, 0, far)
                    landed(here.at[pl.ds(0, cut)], ring_sem.at[at, 0, 0, step])
                    if cut < rows:
                        landed(here.at[pl.ds(cut, rows - cut)], ring_sem.at[at, 0, 1, step])
                    send(at, here, 0, far, "half", half_sem.at[at, far])
                    on_core(at, here, 0, far)
                    came.append((at, 0, far))
                turned_arrivals(at, step - 1)
            else:
                for way in (0, 1):
                    for turned in (0, 1):
                        if step == far and turned != way:
                            continue
                        offset = (-step, step)[way]
                        here = piece(at, turned, offset)
                        landed(here, ring_sem.at[at, turned, way, step])
                        if step < far - 1 or (step == far - 1 and turned == way):
                            on_ring(at, turned, here, offset, way, step + 1)
                        on_core(at, here, turned, offset)
                        came.append((at, turned, offset))
            flush()
    for at in range(count):
        if ring_first[at]:
            turned_arrivals(at, far)
            flush()
    core_arrivals()
    core_arrivals()
    for at in range(count):
        sent = 4 * size - 1 if across else 2 * size - 1
        landed(wholes[at].at[pl.ds(0, sent)], send_sem.at[at])


def gather_sems(count, size):
    return [
        pltpu.SemaphoreType.DMA((count, 2, 2, size // 2 + 1)),
        pltpu.SemaphoreType.DMA((count, size)),
        pltpu.SemaphoreType.DMA((count, 2 * size)),
        pltpu.SemaphoreType.DMA((count,)),
        pltpu.SemaphoreType.DMA((count,)),
    ]


def look_up_body(size, ring_first, *refs):
    count = len(ring_first)
    shards, (table_own, ids) = refs[:count], refs[count : count + 2]
    refs = refs[count + 2 :]
    wholes, (table_out, found) = refs[:count], refs[count : count + 2]
    table, hot, stage, table_sem, stage_sem, *sems = refs[count + 2 :]
    spot = Spot(size)
    spot.meet(True)
    height = table_own.shape[0]
    mine = pltpu.make_async_copy(table_own, table.at[pl.ds(0, height)], table_sem.at[0])
    mine.start()
    swap = pltpu.make_async_remote_copy(
        src_ref=table_own,
        dst_ref=table.at[pl.ds(height, height)],
        send_sem=table_sem.at[1],
        recv_sem=table_sem.at[2],
        device_id=spot.to_core,
        device_id_type=MESH,
    )
    swap.start()
    out = pltpu.make_async_copy(table, table_out, table_sem.at[3])
    pieces, rows = found.shape[:2]
    width = 256
    state = {"ticks": 0, "done": 0}

    def copy_out(number):
        slot = lax.rem(number, 2)
        return pltpu.make_async_copy(stage.at[slot], found.at[number], stage_sem.at[slot])

    def work(first, last):
        def one(number, nothing):
            columns = lax.broadcasted_iota(jnp.int32, (rows, 2 * height), 1)
            hot[...] = jnp.where(columns == ids[number], 1.0, 0.0).astype(jnp.bfloat16)

            @pl.when(number >= 2)
            def _():
                copy_out(number - 2).wait()

            def part(at, nothing):
                window = pl.ds(pl.multiple_of(at * width, width), width)
                stage[lax.rem(number, 2), :, window] = jnp.dot(
                    hot[...], table[:, window], preferred_element_type=jnp.float32
                ).astype(jnp.bfloat16)
                return nothing

            lax.fori_loop(0, D // width, part, 0)
            copy_out(number).start()
            return nothing

        lax.fori_loop(first, last, one, 0)

    def tick(share=1):
        if state["done"] == pieces:
            return
        if state["done"] == 0:
            mine.wait()
            swap.wait_recv()
            out.start()
        last = min(pieces, state["done"] + share)
        work(state["done"], last)
        state["done"] = last

    gather_steps(
        size, ring_first, True, shards, wholes, sems, spot, tick, lambda at, turned, offset, other: None
    )
    tick(pieces)
    copy_out(pieces - 2).wait()
    copy_out(pieces - 1).wait()
    out.wait()
    swap.wait_send()


def look_up_call(size, shards, ring_first, table_own, ids, number):
    count = len(shards)
    height = table_own.shape[0]
    found = ids.shape[:2] + (D,)
    outs = [jax.ShapeDtypeStruct((4 * size,) + a.shape, a.dtype) for a in shards]
    outs.append(jax.ShapeDtypeStruct((2 * height, D), table_own.dtype))
    outs.append(jax.ShapeDtypeStruct(found, table_own.dtype))
    return pl.pallas_call(
        functools.partial(look_up_body, size, ring_first),
        out_shape=outs,
        in_specs=[pl.BlockSpec(memory_space=pl.ANY)] * (count + 1)
        + [pl.BlockSpec(memory_space=pltpu.VMEM)],
        out_specs=[pl.BlockSpec(memory_space=pl.ANY)] * (count + 2),
        scratch_shapes=[
            pltpu.VMEM((2 * height, D), table_own.dtype),
            pltpu.VMEM((ids.shape[1], 2 * height), table_own.dtype),
            pltpu.VMEM((2,) + found[1:], table_own.dtype),
            pltpu.SemaphoreType.DMA((4,)),
            pltpu.SemaphoreType.DMA((2,)),
        ]
        + gather_sems(count, size),
        compiler_params=pltpu.CompilerParams(
            collective_id=number, has_side_effects=True, vmem_limit_bytes=48 * 1024 * 1024
        ),
    )(*shards, table_own, ids)


def spread_body(size, shared, *refs):
    near, rest, ids_near, ids_rest, start = refs[:5]
    table_out, place_out, squares_ref = refs[5:8]
    near_all, rest_all, total, core_in, table_sem, *sems = refs[8:]
    ids = (ids_near, ids_rest)
    wholes = (near_all, rest_all)
    spot = Spot(size)
    spot.meet(True)
    height, length = table_out.shape[0], near.shape[0]
    block = height // 4
    first = pltpu.make_async_copy(start.at[pl.ds(0, height)], total, table_sem.at[0])
    first.start()
    swap = pltpu.make_async_remote_copy(
        src_ref=start.at[pl.ds(height, height)],
        dst_ref=core_in,
        send_sem=table_sem.at[1],
        recv_sem=table_sem.at[2],
        device_id=spot.to_core,
        device_id_type=MESH,
    )
    swap.start()
    place_out[...] = jnp.zeros_like(place_out)
    device = (2 * spot.half + spot.core) * size + spot.wide
    own_place = pl.ds(pl.multiple_of(lax.rem(device * shared, length), 16), shared)
    waiting = []
    state = {"started": False}

    def spread():
        pieces = list(waiting)
        waiting.clear()
        if not state["started"]:
            first.wait()
            state["started"] = True

        def one(number, nothing):
            window = pl.ds(pl.multiple_of(number * block, 16), block)
            row = number * block + lax.broadcasted_iota(jnp.int32, (block, length), 0)
            value = total[window, :]
            for at, piece in pieces:
                hot = jnp.where(row == ids[at][piece], 1.0, 0.0).astype(jnp.bfloat16)
                value = value + jnp.dot(
                    hot, wholes[at][piece], preferred_element_type=jnp.float32
                )
            total[window, :] = value
            return nothing

        lax.fori_loop(0, 4, one, 0)
        for at, piece in pieces:
            place_out[at] += wholes[at][piece, own_place, :].astype(jnp.float32)

    def ready(at, turned, offset, other):
        waiting.append((at, spot.index(turned, other, offset % size)))

    def tick():
        if len(waiting) >= 4:
            spread()

    gather_steps(size, (True, False), True, (near, rest), wholes, sems, spot, tick, ready)
    if waiting:
        spread()
    swap.wait_recv()
    step = height // 4

    def add(number, squares):
        window = pl.ds(pl.multiple_of(number * step, 16), step)
        value = total[window, :] + core_in[window, :]
        total[window, :] = value
        return squares + jnp.sum(value * value, axis=0, keepdims=True)

    squares = lax.fori_loop(0, 4, add, jnp.zeros((1, D), jnp.float32))
    squares_ref[...] = jnp.broadcast_to(squares, squares_ref.shape)
    out = pltpu.make_async_copy(total, table_out, table_sem.at[0])
    out.start()
    swap.wait_send()
    out.wait()


def spread_call(size, near, rest, ids, start, shared, number):
    height = start.shape[0] // 2
    pieces = (4 * size,) + near.shape
    return pl.pallas_call(
        functools.partial(spread_body, size, shared),
        out_shape=[
            jax.ShapeDtypeStruct((height, D), jnp.float32),
            jax.ShapeDtypeStruct((2, shared, D), jnp.float32),
            jax.ShapeDtypeStruct((8, D), jnp.float32),
        ],
        in_specs=[pl.BlockSpec(memory_space=pl.ANY)] * 2
        + [pl.BlockSpec(memory_space=pltpu.VMEM)] * 2
        + [pl.BlockSpec(memory_space=pl.ANY)],
        out_specs=[
            pl.BlockSpec(memory_space=pl.ANY),
            pl.BlockSpec(memory_space=pltpu.VMEM),
            pl.BlockSpec(memory_space=pltpu.VMEM),
        ],
        scratch_shapes=[
            pltpu.VMEM(pieces, near.dtype),
            pltpu.VMEM(pieces, near.dtype),
            pltpu.VMEM((height, D), jnp.float32),
            pltpu.VMEM((height, D), jnp.float32),
            pltpu.SemaphoreType.DMA((3,)),
        ]
        + gather_sems(2, size),
        compiler_params=pltpu.CompilerParams(
            collective_id=number, has_side_effects=True, vmem_limit_bytes=60 * 1024 * 1024
        ),
    )(near, rest, *ids, start)


def plain_gather_body(size, ring_first, across, *refs):
    count = len(ring_first)
    spot = Spot(size)
    spot.meet(across)
    gather_steps(
        size,
        ring_first,
        across,
        refs[:count],
        refs[count : 2 * count],
        refs[2 * count :],
        spot,
        lambda: None,
        lambda at, turned, offset, other: None,
    )


def gather_call(size, shards, ring_first, across, number):
    count = len(shards)
    total = (4 if across else 2) * size
    return pl.pallas_call(
        functools.partial(plain_gather_body, size, ring_first, across),
        out_shape=[jax.ShapeDtypeStruct((total,) + a.shape, a.dtype) for a in shards],
        in_specs=[pl.BlockSpec(memory_space=pl.ANY)] * count,
        out_specs=[pl.BlockSpec(memory_space=pl.ANY)] * count,
        scratch_shapes=gather_sems(count, size),
        compiler_params=pltpu.CompilerParams(collective_id=number, has_side_effects=True),
    )(*shards)


def cast_body(size, everyone, own_ref, out_ref, come_sem, send_sem, local_sem):
    spot = Spot(size)
    group = (4 if everyone else 2) * size
    narrow = lax.axis_index("narrow")
    mine = (narrow if everyone else spot.half) * size + spot.wide

    def device(step):
        at = lax.rem(mine + step, group)
        block = lax.div(at, size)
        return (block if everyone else 2 * block + spot.core, lax.rem(at, size))

    barrier = pltpu.get_barrier_semaphore()

    def greet(step, nothing):
        pl.semaphore_signal(barrier, inc=1, device_id=device(step), device_id_type=MESH)
        return nothing

    def tell(step, nothing):
        pltpu.make_async_remote_copy(
            src_ref=own_ref,
            dst_ref=out_ref.at[mine],
            send_sem=send_sem,
            recv_sem=come_sem,
            device_id=device(step),
            device_id_type=MESH,
        ).start()
        return nothing

    lax.fori_loop(1, group, greet, 0)
    keep = pltpu.make_async_copy(own_ref, out_ref.at[mine], local_sem)
    keep.start()
    pl.semaphore_wait(barrier, group - 1)
    lax.fori_loop(1, group, tell, 0)
    others = out_ref.at[pl.ds(0, group - 1)]
    pltpu.make_async_copy(others, others, come_sem).wait()
    pltpu.make_async_copy(others, others, send_sem).wait()
    keep.wait()


def cast_call(size, block, everyone, number):
    group = (4 if everyone else 2) * size
    return pl.pallas_call(
        functools.partial(cast_body, size, everyone),
        out_shape=jax.ShapeDtypeStruct((group,) + block.shape, block.dtype),
        in_specs=[pl.BlockSpec(memory_space=pltpu.VMEM)],
        out_specs=pl.BlockSpec(memory_space=pltpu.VMEM),
        scratch_shapes=[pltpu.SemaphoreType.DMA] * 3,
        compiler_params=pltpu.CompilerParams(collective_id=number, has_side_effects=True),
    )(block)


def scatter_body(size, half_first, across, bases, working, *refs):
    count = len(half_first)
    extra_in = FeedBack.INPUTS if working else 0
    extra_out = FeedBack.OUTPUTS if working else 0
    arrays, refs = refs[:count], refs[count:]
    work_in, refs = refs[:extra_in], refs[extra_in:]
    outs, squares_ref, refs = refs[:count], refs[count], refs[count + 1 :]
    work_out, refs = refs[:extra_out], refs[extra_out:]
    own, core_in, half_in, ring_in = (
        refs[part * count : (1 + part) * count] for part in range(4)
    )
    local_sem, core_sem, half_sem, ring_sem, send_sem = refs[4 * count : 4 * count + 5]
    work = FeedBack(work_in, work_out, refs[4 * count + 5 :]) if working else None
    squares = []
    spot = Spot(size)
    far = size // 2
    slots = [far] + [o for at in range(far - 1, 0, -1) for o in (at, -at)] + [0]
    sent = []

    def landed(region, sem):
        pltpu.make_async_copy(region, region, sem).wait()

    def send(source, target, device, number, at, sem):
        copy = pltpu.make_async_remote_copy(
            src_ref=source,
            dst_ref=target,
            send_sem=send_sem.at[at, number],
            recv_sem=sem,
            device_id=device,
            device_id_type=MESH,
        )
        copy.start()
        sent.append(copy)

    def source_of(at, turned, other_core, offset):
        if across:
            return arrays[at].at[spot.index(turned, other_core, offset % size)]
        base, stride = bases[at]
        return arrays[at].at[base + stride * (turned * size + offset % size)]

    def add(target, parts):
        rows, columns = target.shape
        width = 512 if columns % 512 == 0 else 256 if columns % 256 == 0 else 128

        def one(step, nothing):
            window = pl.ds(pl.multiple_of(step * width, width), width)
            if len(parts) == 2 and parts[1][1:] == (0, rows):
                one, two = parts[0][0][:, window], parts[1][0][:, window]
                if one.dtype == target.dtype:
                    target[:, window] = one + two
                    return nothing
            total = parts[0][0][:, window].astype(jnp.float32)
            for part, first, last in parts[1:]:
                if first == 0 and last == rows:
                    total = total + part[:, window].astype(jnp.float32)
            target[:, window] = total.astype(target.dtype)
            for part, first, last in parts[1:]:
                if first != 0 or last != rows:
                    span = pl.ds(first, last - first)
                    target[span, window] = (
                        total[first:last] + part[span, window].astype(jnp.float32)
                    ).astype(target.dtype)
            return nothing

        lax.fori_loop(0, columns // width, one, 0)

    def square_sum(ref):
        width = 128

        def one(step, total):
            part = ref[:, pl.ds(pl.multiple_of(step * width, width), width)].astype(jnp.float32)
            return total + jnp.sum(part * part, axis=0, keepdims=True)

        return lax.fori_loop(
            0, ref.shape[1] // width, one, jnp.zeros((1, width), jnp.float32)
        )

    def ring_slot(way, step):
        return way * far + step - 1

    def base(at, turned, offset):
        k = offset % size
        rows = own[at].shape[1]
        here = own[at].at[turned * size + k]
        landed(here, local_sem.at[at, turned * size + k])
        parts = [(here, 0, rows)]
        if across:
            there = core_in[at].at[turned * size + k]
            landed(there, core_sem.at[at, turned * size + k])
            parts.append((there, 0, rows))
        return here, parts

    def ring_parts(at, turned, offset):
        parts = []
        rows = own[at].shape[1]
        cut = cut_of(rows)
        ways = (0, 1) if offset == 0 else (0,) if offset > 0 else (1,)
        for way in ways:
            step = far - abs(offset)
            slot = ring_slot(way, step)
            if half_first[at]:
                if step == 1:
                    first, last = (0, cut) if way == 0 else (cut, rows)
                else:
                    first, last = 0, rows
                if first == last:
                    continue
                region = ring_in[at].at[slot]
                span = region if (first, last) == (0, rows) else region.at[pl.ds(first, last - first)]
                landed(span, ring_sem.at[at, slot])
                parts.append((region, first, last))
            else:
                if step == 1 and turned != way:
                    continue
                region = ring_in[at].at[turned * 2 * far + slot]
                landed(region, ring_sem.at[at, turned * 2 * far + slot])
                parts.append((region, 0, rows))
        return parts

    def ring_send(at, turned, offset):
        here = own[at].at[turned * size + offset % size]
        rows = own[at].shape[1]
        cut = cut_of(rows)
        step = far - abs(offset) + 1
        if offset == far:
            if half_first[at]:
                spans = [(0, pl.ds(0, cut))] + ([(1, pl.ds(cut, rows - cut))] if cut < rows else [])
                for way, span in spans:
                    slot = ring_slot(way, 1)
                    send(
                        here.at[span],
                        ring_in[at].at[slot].at[span],
                        (spot.right, spot.left)[way],
                        slot,
                        at,
                        ring_sem.at[at, slot],
                    )
                return
            ways = (turned,)
        else:
            ways = (0,) if offset > 0 else (1,)
        for way in ways:
            slot = ring_slot(way, step) + (0 if half_first[at] else turned * 2 * far)
            send(
                here,
                ring_in[at].at[slot],
                (spot.right, spot.left)[way],
                slot,
                at,
                ring_sem.at[at, slot],
            )

    spot.meet(across)
    core_base = 4 * far + size
    for offset in slots:
        k = offset % size
        for turned in (1, 0):
            for at in range(count):
                if across:
                    send(
                        source_of(at, turned, 1, offset),
                        core_in[at].at[turned * size + k],
                        spot.to_core,
                        core_base + turned * size + k,
                        at,
                        core_sem.at[at, turned * size + k],
                    )
                pltpu.make_async_copy(
                    source_of(at, turned, 0, offset),
                    own[at].at[turned * size + k],
                    local_sem.at[at, turned * size + k],
                ).start()

    if working:
        work.start()

    def turned_half(offset):
        for at in range(count):
            if half_first[at]:
                here, parts = base(at, 1, offset)
                k = offset % size
                if across:
                    add(here, parts)
                send(here, half_in[at].at[k], spot.to_half, 4 * far + k, at, half_sem.at[at, k])

    def straight(offset):
        for at in range(count):
            if half_first[at]:
                here, parts = base(at, 0, offset)
                k = offset % size
                landed(half_in[at].at[k], half_sem.at[at, k])
                parts.append((half_in[at].at[k], 0, own[at].shape[1]))
                parts += ring_parts(at, 0, offset) if offset != far else []
                if offset == 0:
                    add(outs[at], parts)
                    squares.append(square_sum(outs[at]))
                else:
                    add(here, parts)
                    ring_send(at, 0, offset)

    def both(offset):
        for at in range(count):
            if not half_first[at]:
                for turned in (1, 0):
                    here, parts = base(at, turned, offset)
                    parts += ring_parts(at, turned, offset) if offset != far else []
                    if offset == 0 and turned == 0:
                        landed(half_in[at].at[0], half_sem.at[at, 0])
                        parts.append((half_in[at].at[0], 0, own[at].shape[1]))
                        add(outs[at], parts)
                        squares.append(square_sum(outs[at]))
                        continue
                    if len(parts) > 1:
                        add(here, parts)
                    if offset == 0:
                        send(here, half_in[at].at[0], spot.to_half, 4 * far, at, half_sem.at[at, 0])
                    else:
                        ring_send(at, turned, offset)

    groups = [[far]] + [[at, -at] for at in range(far - 1, 0, -1)] + [[0]]
    def tick():
        if working:
            work.tick()

    tick()
    for number, group in enumerate(groups):
        for offset in group:
            turned_half(offset)
        tick()
        for offset in group:
            both(offset)
        tick()
        if number > 0:
            for offset in groups[number - 1]:
                straight(offset)
            tick()
    for offset in groups[-1]:
        straight(offset)
    total = squares[0]
    for one in squares[1:]:
        total = total + one
    squares_ref[...] = jnp.broadcast_to(total, squares_ref.shape)
    if working:
        work.finish()
    for copy in sent:
        copy.wait_send()


def scatter_call(size, arrays, half_first, across, out_type, number, bases=None, work=None):
    count = len(arrays)
    far = size // 2
    pieces = [a.shape[1:] for a in arrays]
    own = [pltpu.VMEM((2 * size,) + p, a.dtype) for p, a in zip(pieces, arrays)]
    core_in = [
        pltpu.VMEM((2 * size if across else 1,) + p, a.dtype) for p, a in zip(pieces, arrays)
    ]
    half_in = [
        pltpu.VMEM((size if first else 1,) + p, a.dtype)
        for p, a, first in zip(pieces, arrays, half_first)
    ]
    ring_in = [
        pltpu.VMEM((2 * far if first else 4 * far,) + p, a.dtype)
        for p, a, first in zip(pieces, arrays, half_first)
    ]
    outs = [jax.ShapeDtypeStruct(p, out_type) for p in pieces]
    outs.append(jax.ShapeDtypeStruct((8, 128), jnp.float32))
    in_specs = [pl.BlockSpec(memory_space=pl.ANY)] * count
    out_specs = [pl.BlockSpec(memory_space=pltpu.VMEM)] * (count + 1)
    scratch = (
        own
        + core_in
        + half_in
        + ring_in
        + [
            pltpu.SemaphoreType.DMA((count, 2 * size)),
            pltpu.SemaphoreType.DMA((count, 2 * size)),
            pltpu.SemaphoreType.DMA((count, size)),
            pltpu.SemaphoreType.DMA((count, 4 * far)),
            pltpu.SemaphoreType.DMA((count, 4 * far + 3 * size)),
        ]
    )
    if work is not None:
        in_specs += FeedBack.in_specs()
        outs += FeedBack.out_shape(work[0], work[4])
        out_specs += FeedBack.out_specs()
        scratch += FeedBack.scratch(work[0].shape[0])
    return pl.pallas_call(
        functools.partial(
            scatter_body, size, half_first, across, bases or ((0, 1),) * count, work is not None
        ),
        out_shape=outs,
        in_specs=in_specs,
        out_specs=out_specs,
        scratch_shapes=scratch,
        compiler_params=pltpu.CompilerParams(
            collective_id=number, has_side_effects=True, vmem_limit_bytes=60 * 1024 * 1024
        ),
    )(*arrays, *(work or ()))


def layer_norm(values, gain, shift):
    center = values - jnp.mean(values, axis=-1, keepdims=True)
    spread = jnp.mean(center * center, axis=-1, keepdims=True)
    return center * lax.rsqrt(spread + 1e-05) * gain + shift


def gelu_tanh(values):
    return jax.nn.gelu(values, approximate=True)


INNER = (((1,), (1,)), ((), ()))
OUTER = (((0,), (0,)), ((), ()))
GROUP = 8


def dot_inner(one, two):
    return lax.dot_general(one, two, INNER, preferred_element_type=jnp.float32)


def dot_outer(one, two):
    return lax.dot_general(one, two, OUTER, preferred_element_type=jnp.float32)


def fill_mask(mask_ref, length):
    key = lax.broadcasted_iota(jnp.int32, mask_ref.shape, 0)
    query = lax.broadcasted_iota(jnp.int32, mask_ref.shape, 1)
    mask_ref[...] = jnp.where((key <= query) & (key < length), 0.0, -1e30)


def probs_by_key(query, key, mask):
    scores = dot_inner(key, query * 0.125) + mask
    raised = jnp.exp(scores - jnp.max(scores, axis=0, keepdims=True))
    return raised * (1.0 / jnp.sum(raised, axis=0, keepdims=True))


def attend_body(length_ref, query_ref, key_ref, value_ref, mixed_ref, mask_ref):
    @pl.when(pl.program_id(0) == 0)
    def _():
        fill_mask(mask_ref, length_ref[0])

    mixed = []
    for head in range(GROUP):
        lanes = slice(head * HD, (head + 1) * HD)
        probs = probs_by_key(query_ref[:, lanes], key_ref[:, lanes], mask_ref[...])
        mixed.append(dot_outer(value_ref[:, lanes], probs.astype(jnp.bfloat16)))
    mixed_ref[...] = jnp.concatenate(mixed).T.astype(jnp.bfloat16)


def attend_specs(rows, steps):
    return [pl.BlockSpec(memory_space=pltpu.SMEM)] + [
        pl.BlockSpec((rows, GROUP * HD), lambda p, part=part: (0, part * steps + p))
        for part in range(3)
    ]


def attend(projected, seq_lengths):
    rows = projected.shape[0]
    steps = HEADS // GROUP
    return pl.pallas_call(
        attend_body,
        grid=(steps,),
        out_shape=jax.ShapeDtypeStruct((rows, D), jnp.bfloat16),
        in_specs=attend_specs(rows, steps),
        out_specs=pl.BlockSpec((rows, GROUP * HD), lambda p: (0, p)),
        scratch_shapes=[pltpu.VMEM((rows, rows), jnp.float32)],
        compiler_params=pltpu.CompilerParams(vmem_limit_bytes=32 * 1024 * 1024),
        cost_estimate=pl.CostEstimate(
            flops=4 * HEADS * rows * rows * HD, bytes_accessed=8 * rows * D, transcendentals=0
        ),
    )(seq_lengths, projected, projected, projected)


def attend_back_body(length_ref, query_ref, key_ref, value_ref, grad_ref, out_ref, mask_ref):
    @pl.when(pl.program_id(0) == 0)
    def _():
        fill_mask(mask_ref, length_ref[0])

    step = pl.program_id(0)
    low = jnp.bfloat16
    grad_query, grad_key, grad_value = [], [], []
    for head in range(GROUP):
        lanes = slice(head * HD, (head + 1) * HD)
        query, key, grad = query_ref[:, lanes], key_ref[:, lanes], grad_ref[:, lanes]
        probs = probs_by_key(query, key, mask_ref[...])
        grad_probs = dot_inner(value_ref[:, lanes], grad)
        grad_value.append(jnp.dot(probs.astype(low), grad, preferred_element_type=jnp.float32))
        key_dot = jnp.sum(grad_probs * probs, axis=0, keepdims=True)
        scores_low = (probs * (grad_probs - key_dot)).astype(low)
        grad_key.append(jnp.dot(scores_low, query, preferred_element_type=jnp.float32) * 0.125)
        grad_query.append(dot_outer(key, scores_low) * 0.125)
    results = (
        jnp.concatenate(grad_query).T,
        jnp.concatenate(grad_key, axis=1),
        jnp.concatenate(grad_value, axis=1),
    )
    for part, value in enumerate(results):
        window = pl.ds(pl.multiple_of(part * D + step * GROUP * HD, GROUP * HD), GROUP * HD)
        out_ref[:, window] = value.astype(low)


def attend_back(projected, grad_mixed, seq_lengths):
    rows = projected.shape[0]
    steps = HEADS // GROUP
    return pl.pallas_call(
        attend_back_body,
        grid=(steps,),
        out_shape=jax.ShapeDtypeStruct((rows, 3 * D), jnp.bfloat16),
        in_specs=attend_specs(rows, steps)
        + [pl.BlockSpec((rows, GROUP * HD), lambda p: (0, p))],
        out_specs=pl.BlockSpec((rows, 3 * D), lambda p: (0, 0)),
        scratch_shapes=[pltpu.VMEM((rows, rows), jnp.float32)],
        compiler_params=pltpu.CompilerParams(vmem_limit_bytes=48 * 1024 * 1024),
        cost_estimate=pl.CostEstimate(
            flops=10 * HEADS * rows * rows * HD, bytes_accessed=16 * rows * D, transcendentals=0
        ),
    )(seq_lengths, projected, projected, projected, grad_mixed)


class FeedBack:
    CHUNK = 256
    INPUTS = 6
    OUTPUTS = 4

    def __init__(self, ins, outs, scratch):
        self.branch, self.turned, pre, hidden, w_fc, w_proj = ins
        self.grad_normed, self.bias, self.grad_fc, self.grad_proj = outs
        pre_in, hidden_in, fc_in, proj_in, self.fc_out, self.proj_out, self.in_sem, self.out_sem = scratch
        self.chunks = w_proj.shape[0] // self.CHUNK
        self.sources = (pre, hidden, w_fc, w_proj)
        self.slots = (pre_in, hidden_in, fc_in, proj_in)
        self.done = 0

    def span(self, number):
        return pl.ds(pl.multiple_of(number * self.CHUNK, self.CHUNK), self.CHUNK)

    def loads(self, number):
        slot = lax.rem(number, 2)
        for at, (source, place) in enumerate(zip(self.sources, self.slots)):
            here = source.at[self.span(number)] if at == 3 else source.at[:, self.span(number)]
            yield pltpu.make_async_copy(here, place.at[slot], self.in_sem.at[at, slot])

    def stores(self, number):
        slot = lax.rem(number, 2)
        yield pltpu.make_async_copy(
            self.fc_out.at[slot], self.grad_fc.at[:, self.span(number)], self.out_sem.at[0, slot]
        )
        yield pltpu.make_async_copy(
            self.proj_out.at[slot], self.grad_proj.at[self.span(number)], self.out_sem.at[1, slot]
        )

    def start(self):
        self.grad_normed[...] = jnp.zeros_like(self.grad_normed)
        for copy in self.loads(0):
            copy.start()

    def run(self, first, last):
        def one(number, nothing):
            slot = lax.rem(number, 2)
            for copy in self.loads(number):
                copy.wait()

            @pl.when(number + 1 < self.chunks)
            def _():
                for copy in self.loads(number + 1):
                    copy.start()

            @pl.when(number >= 2)
            def _():
                for copy in self.stores(number - 2):
                    copy.wait()

            low = jnp.bfloat16
            pre_in, hidden_in, fc_in, proj_in = self.slots
            grad_hidden = dot_inner(self.branch[...], proj_in[slot])
            value = pre_in[slot]
            square = value * value
            bent = jnp.tanh(0.7978845608 * value * (1.0 + 0.044715 * square))
            slope = 0.5 * (1.0 + bent) + 0.5 * value * (1.0 - bent * bent) * (
                0.7978845608 * (1.0 + 3.0 * 0.044715 * square)
            )
            pre_low = (grad_hidden * slope).astype(low)
            self.bias[:, self.span(number)] = jnp.sum(
                pre_low.astype(jnp.float32), axis=0, keepdims=True
            )
            self.grad_normed[...] += dot_inner(pre_low, fc_in[slot])
            self.fc_out[slot] = jnp.dot(
                self.turned[...], pre_low, preferred_element_type=jnp.float32
            ).astype(low)
            self.proj_out[slot] = dot_outer(hidden_in[slot], self.branch[...]).astype(low)
            for copy in self.stores(number):
                copy.start()
            return nothing

        lax.fori_loop(first, last, one, 0)

    def tick(self):
        if self.done < self.chunks:
            self.run(self.done, self.done + 1)
            self.done += 1

    def finish(self):
        if self.done < self.chunks:
            self.run(self.done, self.chunks)
        for number in (self.chunks - 2, self.chunks - 1):
            for copy in self.stores(jnp.int32(number)):
                copy.wait()

    @classmethod
    def in_specs(cls):
        return [pl.BlockSpec(memory_space=pltpu.VMEM)] * 2 + [pl.BlockSpec(memory_space=pl.ANY)] * 4

    @classmethod
    def out_specs(cls):
        return [pl.BlockSpec(memory_space=pltpu.VMEM)] * 2 + [pl.BlockSpec(memory_space=pl.ANY)] * 2

    @classmethod
    def out_shape(cls, branch, w_fc):
        hidden = w_fc.shape[1]
        return [
            jax.ShapeDtypeStruct(branch.shape, jnp.float32),
            jax.ShapeDtypeStruct((1, hidden), jnp.float32),
            jax.ShapeDtypeStruct((D, hidden), jnp.bfloat16),
            jax.ShapeDtypeStruct((hidden, D), jnp.bfloat16),
        ]

    @classmethod
    def scratch(cls, rows):
        low, chunk = jnp.bfloat16, cls.CHUNK
        return [
            pltpu.VMEM((2, rows, chunk), jnp.float32),
            pltpu.VMEM((2, rows, chunk), low),
            pltpu.VMEM((2, D, chunk), low),
            pltpu.VMEM((2, chunk, D), low),
            pltpu.VMEM((2, D, chunk), low),
            pltpu.VMEM((2, chunk, D), low),
            pltpu.SemaphoreType.DMA((4, 2)),
            pltpu.SemaphoreType.DMA((2, 2)),
        ]


def feed_back_body(*refs):
    ins, outs = FeedBack.INPUTS, FeedBack.OUTPUTS
    work = FeedBack(refs[:ins], refs[ins : ins + outs], refs[ins + outs :])
    work.start()
    work.finish()


def feed_back(operands):
    branch, w_fc = operands[0], operands[4]
    return pl.pallas_call(
        feed_back_body,
        out_shape=FeedBack.out_shape(branch, w_fc),
        in_specs=FeedBack.in_specs(),
        out_specs=FeedBack.out_specs(),
        scratch_shapes=FeedBack.scratch(branch.shape[0]),
        compiler_params=pltpu.CompilerParams(vmem_limit_bytes=40 * 1024 * 1024),
    )(*operands)


def layer_forward(stream, weights, vector, seq_lengths):
    w_qkv, w_out, w_fc, w_proj = weights
    normed_low = layer_norm(stream, vector[0:D], vector[D : 2 * D]).astype(jnp.bfloat16)
    qkv_bias = jnp.concatenate(
        [vector[4 * D : 5 * D], jnp.zeros((D,), jnp.float32), vector[5 * D : 6 * D]]
    )
    projected = (jnp.dot(normed_low, w_qkv, preferred_element_type=jnp.float32) + qkv_bias).astype(
        jnp.bfloat16
    )
    mixed_low = attend(projected, seq_lengths)
    stream_mid = (
        stream
        + jnp.dot(mixed_low, w_out, preferred_element_type=jnp.float32)
        + vector[6 * D : 7 * D]
    )
    normed_two = layer_norm(stream_mid, vector[2 * D : 3 * D], vector[3 * D : 4 * D]).astype(
        jnp.bfloat16
    )
    hidden_pre = (
        jnp.dot(normed_two, w_fc, preferred_element_type=jnp.float32) + vector[8 * D : 8 * D + FF]
    )
    hidden_low = gelu_tanh(hidden_pre).astype(jnp.bfloat16)
    stream_out = (
        stream_mid
        + jnp.dot(hidden_low, w_proj, preferred_element_type=jnp.float32)
        + vector[7 * D : 8 * D]
    )
    return (
        stream_out,
        (
            stream,
            normed_low,
            projected,
            mixed_low,
            stream_mid,
            normed_two,
            hidden_pre,
            hidden_low,
        ),
    )


def feed_plain(operands):
    branch_low, normed_turned, hidden_pre, hidden_low, w_fc, w_proj = operands
    grad_wproj = jnp.dot(hidden_low.T, branch_low, preferred_element_type=jnp.bfloat16)
    grad_hidden = jnp.dot(branch_low, w_proj.T, preferred_element_type=jnp.float32)
    pre_low = jax.vjp(gelu_tanh, hidden_pre)[1](grad_hidden)[0].astype(jnp.bfloat16)
    grad_wfc = jnp.dot(normed_turned, pre_low, preferred_element_type=jnp.bfloat16)
    grad_normed_two = jnp.dot(pre_low, w_fc.T, preferred_element_type=jnp.float32)
    bias = jnp.sum(pre_low.astype(jnp.float32), axis=0)
    return grad_normed_two, bias, grad_wfc, grad_wproj


def layer_backward(grad_out, saved_acts, weights, vector, seq_lengths, feed):
    (
        stream,
        normed_low,
        projected,
        mixed_low,
        stream_mid,
        normed_two,
        hidden_pre,
        hidden_low,
    ) = saved_acts
    w_qkv, w_out, w_fc, w_proj = weights
    branch_low = grad_out.astype(jnp.bfloat16)
    grad_normed_two, grad_bias, grad_wfc, grad_wproj = feed(
        (branch_low, normed_two.T, hidden_pre, hidden_low, w_fc, w_proj)
    )
    grad_mid, grad_gain_two, grad_shift_two = jax.vjp(
        layer_norm, stream_mid, vector[2 * D : 3 * D], vector[3 * D : 4 * D]
    )[1](grad_normed_two)
    grad_mid = grad_mid + grad_out
    attn_low = grad_mid.astype(jnp.bfloat16)
    grad_wout = jnp.dot(mixed_low.T, attn_low, preferred_element_type=jnp.bfloat16)
    grad_mixed = jnp.dot(attn_low, w_out.T, preferred_element_type=jnp.float32).astype(
        jnp.bfloat16
    )
    qkv_low = attend_back(projected, grad_mixed, seq_lengths)
    grad_wqkv = jnp.dot(normed_low.T, qkv_low, preferred_element_type=jnp.bfloat16)
    grad_normed = jnp.dot(qkv_low, w_qkv.T, preferred_element_type=jnp.float32)
    grad_input, grad_gain_one, grad_shift_one = jax.vjp(
        layer_norm, stream, vector[0:D], vector[D : 2 * D]
    )[1](grad_normed)
    bias_qkv = jnp.sum(qkv_low.astype(jnp.float32), axis=0)
    grad_vector = jnp.concatenate(
        [
            grad_gain_one,
            grad_shift_one,
            grad_gain_two,
            grad_shift_two,
            bias_qkv[0:D],
            bias_qkv[2 * D : 3 * D],
            jnp.sum(attn_low.astype(jnp.float32), axis=0),
            jnp.sum(branch_low.astype(jnp.float32), axis=0),
            grad_bias.reshape(-1),
        ]
    )
    return (grad_input + grad_mid, (grad_wqkv, grad_wout, grad_wfc, grad_wproj), grad_vector)


def adamw(weight, moment_one, moment_two, gradient, step_rate, decay_rate, step_float):
    one_new = 0.5 * moment_one + 0.5 * gradient
    two_new = 0.5 * moment_two + 0.5 * gradient * gradient
    fix_scale = 1.0 - jnp.power(0.5, step_float)
    update = one_new / fix_scale / (jnp.sqrt(two_new / fix_scale) + 1e-08)
    return (weight - step_rate * (update + decay_rate * weight), one_new, two_new)


def on_device(
    token_ids,
    seq_lengths,
    loss_slots,
    target_ids,
    step_count,
    w_qkv,
    w_out,
    w_fc,
    w_proj,
    vectors,
    pos_table,
    embed_table,
    mom_qkv,
    mom_out,
    mom_fc,
    mom_proj,
    mom_vectors,
    mom_pos,
    mom_embed,
    sec_qkv,
    sec_out,
    sec_fc,
    sec_proj,
    sec_vectors,
    sec_pos,
    sec_embed,
):
    per_layer = 8 * D + FF
    net = Net()
    size, halves = net.size, net.halves
    same_core = halves * size
    devices = 2 * same_core
    low = jnp.bfloat16
    near = LEN // 2
    fused = size <= 8
    rest = LEN - near
    slots = loss_slots.shape[0]

    half_of = jnp.arange(halves)[:, None]
    wide_index = jnp.arange(size)[None, :]
    place_of = jnp.where(wide_index % 2 == 0, wide_index // 2, size - 1 - (wide_index - 1) // 2)
    to_device = ((half_of ^ net.half) * size + (place_of - net.place) % size).reshape(-1)
    offsets = (net.place + wide_index) % size
    wide_there = jnp.where(offsets < size // 2, 2 * offsets, 2 * (size - 1 - offsets) + 1)
    from_device = ((half_of ^ net.half) * size + wide_there).reshape(-1)

    numbers = jnp.concatenate([token_ids, loss_slots, target_ids, seq_lengths])
    numbers = jnp.pad(numbers, (0, -numbers.shape[0] % 1024)).reshape(-1, 128)
    numbers = cast_call(size, numbers, True, 5).reshape(devices, -1)
    all_tokens = numbers[:, :LEN]
    token_total = jnp.sum(numbers[:, LEN + 2 * slots].astype(jnp.float32))
    on_core = from_device + (from_device // size + net.core) * size
    numbers = jnp.take(numbers, on_core, axis=0).reshape(halves, size, -1)
    group_tokens = numbers[:, :, :LEN]
    group_slots = numbers[:, :, LEN : LEN + slots].reshape(same_core * slots)
    group_targets = numbers[:, :, LEN + slots : LEN + 2 * slots].reshape(same_core * slots)

    own_rows = embed_table.shape[0]
    height = own_rows + -own_rows % 64
    chip_rows = 2 * height
    table_own = jnp.pad(embed_table.astype(low), ((0, height - own_rows), (0, 0)))
    own_start = net.device * own_rows
    other_start = (net.device + (1 - 2 * net.core) * size) * own_rows

    def locate(ids):
        mine = ids - own_start
        other = ids - other_start
        return jnp.where(
            (mine >= 0) & (mine < own_rows),
            mine,
            jnp.where((other >= 0) & (other < own_rows), other + height, -1),
        )

    def one_hot(ids):
        return (ids[:, None] == jnp.arange(chip_rows)[None, :]).astype(low)

    local_tokens = locate(group_tokens).reshape(same_core, LEN)
    ids_near, ids_rest = local_tokens[:, :near], local_tokens[:, near:]

    shared = pos_table.shape[0]
    vector_rows = -(-vectors.shape[0] // D)
    padded = jnp.pad(vectors, (0, vector_rows * D - vectors.shape[0])).reshape(vector_rows, D)
    spare = -(shared + vector_rows) % 16
    small_own = jnp.concatenate([pos_table, padded, jnp.zeros((spare, D), jnp.float32)])
    shards_low = []
    for layer_at in range(LAYERS):
        shards_low += [part[layer_at].astype(low) for part in (w_qkv, w_fc, w_proj, w_out)]
    shards_low.append(small_own.astype(low))
    ring_first = (True, True, False, False) * LAYERS + (False,)
    if fused:
        *gathered, table_low, found = look_up_call(
            size, shards_low, ring_first, table_own, jnp.concatenate([ids_near, ids_rest])[..., None], 1
        )
        stream = scatter_call(
            size, [found, found], (True, False), False, low, 2, ((0, 1), (same_core, 1))
        )
        stream = jnp.concatenate(stream[:2])
    else:
        gathered = gather_call(size, shards_low, ring_first, True, 1)
        table_low = jnp.concatenate([table_own, net.swap_core(table_own)])
        found = [
            jnp.dot(
                one_hot(ids.reshape(-1)), table_low, preferred_element_type=jnp.float32
            ).astype(low).reshape(same_core, -1, D)
            for ids in (ids_near, ids_rest)
        ]
        bands = max(1, same_core // 16)
        band = D // bands
        parts = []
        for at in range(bands):
            window = [part[:, :, at * band : (at + 1) * band] for part in found]
            parts.append(
                jnp.concatenate(scatter_call(size, window, (True, False), False, low, 2)[:2])
            )
        stream = jnp.concatenate(parts, axis=1)
    small_low = gathered[-1]
    pos_low = small_low[:, :shared].reshape(devices * shared, D)
    vector_all = (
        small_low[:, shared : shared + vector_rows]
        .reshape(devices, vector_rows * D)[:, : vectors.shape[0]]
        .reshape(-1)
        .astype(jnp.float32)
    )

    stream = stream.astype(jnp.float32) + pos_low[:LEN].astype(jnp.float32)

    kept_weights = []
    saved_list = []
    for layer_at in range(LAYERS):
        w_a, w_c, w_d, w_b = (
            part.reshape(-1, part.shape[2]) for part in gathered[layer_at * 4 : layer_at * 4 + 4]
        )
        weights = (w_a, w_b, w_c, w_d)
        kept_weights.append(weights)
        stream, saved_acts = layer_forward(
            stream, weights, vector_all[layer_at * per_layer : (layer_at + 1) * per_layer], seq_lengths
        )
        saved_list.append(saved_acts)
    tail_start = LAYERS * per_layer
    final_norm, final_pull = jax.vjp(
        layer_norm,
        stream,
        vector_all[tail_start : tail_start + D],
        vector_all[tail_start + D : tail_start + 2 * D],
    )
    slot_rows = jnp.maximum(loss_slots, 0)
    own_picked = final_norm[slot_rows].astype(low)
    some = slots // 2
    group_rows = jnp.concatenate(
        gather_call(size, [own_picked[:some], own_picked[some:]], (True, False), False, 6), axis=1
    ).reshape(same_core * slots, D)
    real = jnp.arange(chip_rows) % height < own_rows
    logits = jnp.where(
        real, jnp.dot(group_rows, table_low.T, preferred_element_type=jnp.float32), -1e30
    )
    target_onehot = locate(group_targets)[:, None] == jnp.arange(chip_rows)[None, :]
    row_max = jnp.max(logits, axis=-1)
    row_total = jnp.sum(jnp.exp(logits - row_max[:, None]), axis=-1)
    target_logit = jnp.sum(jnp.where(target_onehot, logits, 0.0), axis=-1)
    stats = jnp.stack([row_max, row_total, target_logit], axis=-1)
    stats = jnp.take(stats.reshape(same_core, slots * 3), to_device, axis=0)
    stats = stats.reshape(same_core * slots, 3).T.reshape(-1)
    entries = stats.shape[0]
    stats = jnp.pad(stats, (0, -entries % 1024)).reshape(-1, 128)
    stats = cast_call(size, stats, False, 7).reshape(same_core, -1)[:, :entries]
    stats = stats.reshape(same_core, 3, same_core * slots)
    joint_max = jnp.max(stats[:, 0], axis=0)
    joint_total = jnp.sum(stats[:, 1] * jnp.exp(stats[:, 0] - joint_max), axis=0)
    stats = jnp.stack([joint_max + jnp.log(joint_total), jnp.sum(stats[:, 2], axis=0)])
    stats = stats.reshape(2, same_core, slots)
    stats = jnp.take(stats, from_device, axis=1).reshape(2, same_core * slots)
    log_total, merged_target = stats[0], stats[1]
    group_used = (group_slots >= 0).astype(jnp.float32)
    own_loss = jnp.sum(((log_total - merged_target) * group_used)[:slots])
    grad_logits = (
        (jnp.exp(logits - log_total[:, None]) - target_onehot.astype(jnp.float32))
        * (group_used / token_total)[:, None]
    ).astype(low)
    grad_rows = jnp.dot(grad_logits, table_low, preferred_element_type=jnp.float32)
    grad_rows = grad_rows.reshape(2 * same_core, some, D)
    grad_rows = jnp.concatenate(
        scatter_call(
            size,
            [grad_rows, grad_rows],
            (True, False),
            False,
            jnp.float32,
            8,
            ((0, 2), (1, 2)),
        )[:2]
    )
    grad_final = jnp.zeros((LEN, D), jnp.float32).at[slot_rows].add(grad_rows)
    grad_stream, grad_gain_final, grad_shift_final = final_pull(grad_final)
    layer_shards = []
    vector_grads = []
    squares = jnp.zeros((128,), jnp.float32)
    pending = None

    def reduce_layers(full_grads, number, more=(), work=None):
        grad_a, grad_b, grad_c, grad_d = full_grads
        arrays = [part.reshape(devices, -1, part.shape[1]) for part in (grad_a, grad_c, grad_d, grad_b)]
        arrays += more
        outs = scatter_call(
            size,
            arrays,
            (True, True, False, False) + (False,) * len(more),
            True,
            jnp.float32,
            number,
            work=work,
        )
        shard_a, shard_c, shard_d, shard_b, *rest = outs
        layer_shards.insert(0, (shard_a, shard_b, shard_c, shard_d))
        return rest

    for layer_at in reversed(range(LAYERS)):
        feed = feed_plain
        if pending is not None:
            held = []

            def feed(operands):
                sums, *results = reduce_layers(pending, 3, work=operands)
                held.append(sums[0])
                return results

        grad_stream, full_grads, grad_vector = layer_backward(
            grad_stream,
            saved_list[layer_at],
            kept_weights[layer_at],
            vector_all[layer_at * per_layer : (layer_at + 1) * per_layer],
            seq_lengths,
            feed,
        )
        if pending is not None:
            squares = squares + held[0]
        pending = full_grads
        vector_grads.insert(0, grad_vector)
    grad_low = grad_stream.astype(low)
    grad_near, grad_rest = grad_low[:near], grad_low[near:]
    grad_table = jnp.dot(grad_logits.T, group_rows, preferred_element_type=jnp.float32)
    if fused:
        ids = all_tokens - own_start
        ids = jnp.where((ids >= 0) & (ids < own_rows), ids, -1)[:, None]
        ids = [ids[:, :, :near], ids[:, :, near:]]
        grad_table, places, sums = spread_call(
            size, grad_near, grad_rest, ids, grad_table, shared, 4
        )
        squares = squares + jnp.sum(sums[0].reshape(-1, 128), axis=0)
        first_place = net.device * shared
        pos_shard = jnp.where(
            first_place < near, places[0], jnp.where(first_place < LEN, places[1], 0.0)
        )
    else:
        wholes = gather_call(size, [grad_near, grad_rest], (True, False), False, 4)
        for ids, whole in zip((ids_near, ids_rest), wholes):
            grad_table = grad_table + jnp.dot(
                one_hot(ids.reshape(-1)).T, whole.reshape(-1, D), preferred_element_type=jnp.float32
            )
        grad_table = grad_table[:height] + net.swap_core(grad_table[height:])
        squares = squares + jnp.sum(grad_table * grad_table, axis=0).reshape(-1, 128).sum(axis=0)
        grad_pos = jnp.concatenate(
            [jnp.sum(whole.astype(jnp.float32), axis=0) for whole in wholes]
        )
        grad_pos = jnp.pad(grad_pos, ((0, POS - LEN), (0, 0)))
        other_device = net.device + (1 - 2 * net.core) * size
        pos_shard = lax.dynamic_slice_in_dim(grad_pos, net.device * shared, shared) + net.swap_core(
            lax.dynamic_slice_in_dim(grad_pos, other_device * shared, shared)
        )
    table_shard = grad_table[:own_rows]
    grad_small = jnp.concatenate(vector_grads + [grad_gain_final, grad_shift_final])
    own_small = vectors.shape[0]
    grad_small = jnp.pad(grad_small.reshape(devices, own_small), ((0, 0), (0, -own_small % 1024)))
    small_shard, sums = reduce_layers(pending, 10, [grad_small.reshape(devices, -1, 128)])
    small_shard = small_shard.reshape(-1)[:own_small]
    pos_squares = jnp.sum(pos_shard * pos_shard, axis=0).reshape(-1, 128)
    squares = squares + sums[0] + jnp.sum(pos_squares, axis=0)
    qkv_shard = jnp.stack([member[0] for member in layer_shards])
    out_shard = jnp.stack([member[1] for member in layer_shards])
    fc_shard = jnp.stack([member[2] for member in layer_shards])
    proj_shard = jnp.stack([member[3] for member in layer_shards])
    shards = (qkv_shard, out_shard, fc_shard, proj_shard, small_shard, pos_shard, table_shard)
    sums = jnp.stack([squares, jnp.pad(own_loss[None], (0, 127))])
    sums = cast_call(size, jnp.pad(sums, ((0, 6), (0, 0))), True, 9)
    square_total, loss_total = jnp.sum(sums[:, 0]), jnp.sum(sums[:, 1])
    loss_value = loss_total / token_total
    grad_norm = jnp.sqrt(square_total)
    factor = CLIP_LIMIT / jnp.maximum(grad_norm, CLIP_LIMIT)
    step_float = step_count.astype(jnp.float32)
    params = (w_qkv, w_out, w_fc, w_proj, vectors, pos_table, embed_table)
    moments_one = (mom_qkv, mom_out, mom_fc, mom_proj, mom_vectors, mom_pos, mom_embed)
    moments_two = (sec_qkv, sec_out, sec_fc, sec_proj, sec_vectors, sec_pos, sec_embed)
    step_rates = (
        RATE_MATRIX,
        RATE_MATRIX,
        RATE_MATRIX,
        RATE_MATRIX,
        RATE_VECTOR,
        RATE_MATRIX,
        RATE_MATRIX,
    )
    decay_rates = (
        DECAY_MATRIX,
        DECAY_MATRIX,
        DECAY_MATRIX,
        DECAY_MATRIX,
        0.0,
        DECAY_MATRIX,
        DECAY_MATRIX,
    )
    results = [
        adamw(
            params[where_at],
            moments_one[where_at],
            moments_two[where_at],
            shards[where_at] * factor,
            step_rates[where_at],
            decay_rates[where_at],
            step_float,
        )
        for where_at in range(7)
    ]
    return (
        loss_value,
        grad_norm,
        results[0][0],
        results[1][0],
        results[2][0],
        results[3][0],
        results[4][0],
        results[5][0],
        results[6][0],
        results[0][1],
        results[1][1],
        results[2][1],
        results[3][1],
        results[4][1],
        results[5][1],
        results[6][1],
        results[0][2],
        results[1][2],
        results[2][2],
        results[3][2],
        results[4][2],
        results[5][2],
        results[6][2],
    )


def solution(mesh):
    return jax.shard_map(
        on_device,
        mesh=mesh,
        in_specs=(
            P(("narrow", "wide")),
            P(("narrow", "wide")),
            P(("narrow", "wide")),
            P(("narrow", "wide")),
            P(),
            P(None, ("narrow", "wide"), None),
            P(None, ("narrow", "wide"), None),
            P(None, ("narrow", "wide"), None),
            P(None, ("narrow", "wide"), None),
            P(("narrow", "wide")),
            P(("narrow", "wide"), None),
            P(("narrow", "wide"), None),
            P(None, ("narrow", "wide"), None),
            P(None, ("narrow", "wide"), None),
            P(None, ("narrow", "wide"), None),
            P(None, ("narrow", "wide"), None),
            P(("narrow", "wide")),
            P(("narrow", "wide"), None),
            P(("narrow", "wide"), None),
            P(None, ("narrow", "wide"), None),
            P(None, ("narrow", "wide"), None),
            P(None, ("narrow", "wide"), None),
            P(None, ("narrow", "wide"), None),
            P(("narrow", "wide")),
            P(("narrow", "wide"), None),
            P(("narrow", "wide"), None),
        ),
        out_specs=(
            P(),
            P(),
            P(None, ("narrow", "wide"), None),
            P(None, ("narrow", "wide"), None),
            P(None, ("narrow", "wide"), None),
            P(None, ("narrow", "wide"), None),
            P(("narrow", "wide")),
            P(("narrow", "wide"), None),
            P(("narrow", "wide"), None),
            P(None, ("narrow", "wide"), None),
            P(None, ("narrow", "wide"), None),
            P(None, ("narrow", "wide"), None),
            P(None, ("narrow", "wide"), None),
            P(("narrow", "wide")),
            P(("narrow", "wide"), None),
            P(("narrow", "wide"), None),
            P(None, ("narrow", "wide"), None),
            P(None, ("narrow", "wide"), None),
            P(None, ("narrow", "wide"), None),
            P(None, ("narrow", "wide"), None),
            P(("narrow", "wide")),
            P(("narrow", "wide"), None),
            P(("narrow", "wide"), None),
        ),
        check_vma=False,
    )
```

```python
import functools

import jax
import jax.numpy as jnp
from jax import lax
from jax.experimental import pallas as pl
from jax.experimental.pallas import tpu as pltpu
from jax.sharding import PartitionSpec as P

D = 1024
HEADS = 16
HD = 64
FF = 4096
POS = 1024
LAYERS = 2
LEN = 512
LOSS_DEV = 32


CLIP_LIMIT = 0.002
RATE_MATRIX = 0.03
RATE_VECTOR = 0.3
DECAY_MATRIX = 0.1


class Net:
    def __init__(self):
        self.narrow_at = lax.axis_index("narrow")
        self.wide_at = lax.axis_index("wide")
        self.narrow_size = lax.axis_size("narrow")
        self.size = lax.axis_size("wide")
        size = self.size
        self.core = self.narrow_at % 2
        self.half = self.narrow_at // 2
        self.halves = self.narrow_size // 2
        self.place = jnp.where(
            self.wide_at % 2 == 0, self.wide_at // 2, size - 1 - (self.wide_at - 1) // 2
        )
        self.device = self.narrow_at * size + self.wide_at
        order = list(range(0, size, 2)) + list(range(size - 1, 0, -2))
        pairs = [(n, w) for n in range(self.narrow_size) for w in range(size)]
        self.core_pairs = [(n * size + w, (n ^ 1) * size + w) for n, w in pairs]
        self.half_pairs = [(n * size + w, (n ^ 2) * size + w) for n, w in pairs]
        self.right = [
            (n * size + order[i], n * size + order[(i + 1) % size])
            for n in range(self.narrow_size)
            for i in range(size)
        ]
        self.left = [(later, earlier) for earlier, later in self.right]

    def step(self, array, pairs):
        return lax.ppermute(array, ("narrow", "wide"), pairs)

    def swap_core(self, array):
        return self.step(array, self.core_pairs)

    def swap_half(self, array):
        return self.step(array, self.half_pairs)

    def wide_of(self, offset):
        size = self.size
        at = lax.rem(self.place + offset, size)
        return jnp.where(at < size // 2, 2 * at, 2 * (size - 1 - at) + 1)


MESH = pl.DeviceIdType.MESH


class Spot:
    def __init__(self, size):
        self.size = size
        narrow, wide = lax.axis_index("narrow"), lax.axis_index("wide")
        odd = lax.rem(wide, 2)
        self.core, self.half = lax.rem(narrow, 2), lax.div(narrow, 2)
        self.wide = wide
        self.place = (1 - odd) * lax.div(wide, 2) + odd * (size - 1 - lax.div(wide, 2))
        self.to_core = (narrow + 1 - 2 * self.core, wide)
        self.to_half = (narrow + 2 - 4 * self.half, wide)
        self.right = (narrow, self.wide_of(1))
        self.left = (narrow, self.wide_of(size - 1))

    def wide_of(self, offset):
        at = lax.rem(self.place + offset, self.size)
        late = lax.div(at, self.size // 2)
        return (1 - late) * 2 * at + late * (2 * (self.size - 1 - at) + 1)

    def index(self, turned, other_core, offset):
        half = self.half + turned * (1 - 2 * self.half)
        core = self.core + other_core * (1 - 2 * self.core)
        return (2 * half + core) * self.size + self.wide_of(offset)

    def meet(self, with_core):
        barrier = pltpu.get_barrier_semaphore()
        peers = [self.to_half, self.right, self.left] + ([self.to_core] if with_core else [])
        for peer in peers:
            pl.semaphore_signal(barrier, inc=1, device_id=peer, device_id_type=MESH)
        pl.semaphore_wait(barrier, len(peers))


def cut_of(rows):
    return rows // 2 if rows % 32 == 0 else rows


def gather_steps(size, ring_first, across, shards, wholes, sems, spot, tick, ready):
    count = len(ring_first)
    ring_sem, half_sem, core_sem, send_sem, local_sem = sems
    far = size // 2

    def index(turned, offset, toward=None):
        if across:
            return spot.index(turned, 0, offset % size)
        if toward == "half":
            turned = 1 - turned
        offset = offset + {"right": -1, "left": 1}.get(toward, 0)
        return turned * size + offset % size

    def send(at, source, turned, offset, toward, sem, rows=None):
        target = wholes[at].at[index(turned, offset, toward)]
        if rows is not None:
            source, target = source.at[rows], target.at[rows]
        device = {
            "half": spot.to_half,
            "right": spot.right,
            "left": spot.left,
            "core": spot.to_core,
        }[toward]
        pltpu.make_async_remote_copy(
            src_ref=source,
            dst_ref=target,
            send_sem=send_sem.at[at],
            recv_sem=sem,
            device_id=device,
            device_id_type=MESH,
        ).start()

    def landed(region, sem):
        pltpu.make_async_copy(region, region, sem).wait()

    def piece(at, turned, offset):
        return wholes[at].at[index(turned, offset)]

    expected, due = [], []

    def on_core(at, source, turned, offset):
        if across:
            number = turned * size + offset % size
            send(at, source, turned, offset, "core", core_sem.at[at, number])
            expected.append((at, turned, offset))

    def core_arrivals():
        for at, turned, offset in due:
            region = wholes[at].at[spot.index(turned, 1, offset % size)]
            landed(region, core_sem.at[at, turned * size + offset % size])
            ready(at, turned, offset, 1)
        due[:] = expected
        expected.clear()

    def on_ring(at, turned, source, offset, way, step, rows=None):
        toward = ("right", "left")[way]
        send(at, source, turned, offset, toward, ring_sem.at[at, turned, way, step], rows)

    locals_ = []
    for at in range(count):
        copy = pltpu.make_async_copy(shards[at], piece(at, 0, 0), local_sem.at[at])
        copy.start()
        locals_.append(copy)
    for at in range(count):
        if not ring_first[at]:
            send(at, shards[at], 0, 0, "half", half_sem.at[at, 0])
    for at in range(count):
        if ring_first[at]:
            on_ring(at, 0, shards[at], 0, 0, 1)
            on_ring(at, 0, shards[at], 0, 1, 1)
            send(at, shards[at], 0, 0, "half", half_sem.at[at, 0])
    for at in range(count):
        on_core(at, shards[at], 0, 0)
    for at in range(count):
        if not ring_first[at]:
            landed(piece(at, 1, 0), half_sem.at[at, 0])
            for way in (0, 1):
                on_ring(at, 0, shards[at], 0, way, 1)
                on_ring(at, 1, piece(at, 1, 0), 0, way, 1)
            on_core(at, piece(at, 1, 0), 1, 0)
    for at in range(count):
        locals_[at].wait()
        ready(at, 0, 0, 0)
        if not ring_first[at]:
            ready(at, 1, 0, 0)
        tick()

    def turned_arrivals(at, step):
        offsets = (0,) if step == 0 else (far,) if step == far else (-step, step)
        for offset in offsets:
            landed(piece(at, 1, offset), half_sem.at[at, offset % size])
            on_core(at, piece(at, 1, offset), 1, offset)
            came.append((at, 1, offset))

    came = []

    def flush():
        for one in came:
            ready(*one, 0)
        came.clear()
        core_arrivals()
        tick()

    for step in range(1, far + 1):
        for at in range(count):
            rows = shards[at].shape[0]
            cut = cut_of(rows)
            if ring_first[at]:
                if step < far:
                    for way in (0, 1):
                        offset = (-step, step)[way]
                        here = piece(at, 0, offset)
                        landed(here, ring_sem.at[at, 0, way, step])
                        if step < far - 1:
                            on_ring(at, 0, here, offset, way, step + 1)
                        elif way == 0:
                            on_ring(at, 0, here, offset, way, step + 1, pl.ds(0, cut))
                        elif cut < rows:
                            on_ring(at, 0, here, offset, way, step + 1, pl.ds(cut, rows - cut))
                        send(at, here, 0, offset, "half", half_sem.at[at, offset % size])
                        on_core(at, here, 0, offset)
                        came.append((at, 0, offset))
                else:
                    here = piece(at, 0, far)
                    landed(here.at[pl.ds(0, cut)], ring_sem.at[at, 0, 0, step])
                    if cut < rows:
                        landed(here.at[pl.ds(cut, rows - cut)], ring_sem.at[at, 0, 1, step])
                    send(at, here, 0, far, "half", half_sem.at[at, far])
                    on_core(at, here, 0, far)
                    came.append((at, 0, far))
                turned_arrivals(at, step - 1)
            else:
                for way in (0, 1):
                    for turned in (0, 1):
                        if step == far and turned != way:
                            continue
                        offset = (-step, step)[way]
                        here = piece(at, turned, offset)
                        landed(here, ring_sem.at[at, turned, way, step])
                        if step < far - 1 or (step == far - 1 and turned == way):
                            on_ring(at, turned, here, offset, way, step + 1)
                        on_core(at, here, turned, offset)
                        came.append((at, turned, offset))
            flush()
    for at in range(count):
        if ring_first[at]:
            turned_arrivals(at, far)
            flush()
    core_arrivals()
    core_arrivals()
    for at in range(count):
        sent = 4 * size - 1 if across else 2 * size - 1
        landed(wholes[at].at[pl.ds(0, sent)], send_sem.at[at])


def gather_sems(count, size):
    return [
        pltpu.SemaphoreType.DMA((count, 2, 2, size // 2 + 1)),
        pltpu.SemaphoreType.DMA((count, size)),
        pltpu.SemaphoreType.DMA((count, 2 * size)),
        pltpu.SemaphoreType.DMA((count,)),
        pltpu.SemaphoreType.DMA((count,)),
    ]


def look_up_body(size, ring_first, *refs):
    count = len(ring_first)
    shards, (table_own, ids) = refs[:count], refs[count : count + 2]
    refs = refs[count + 2 :]
    wholes, (table_out, found) = refs[:count], refs[count : count + 2]
    table, hot, stage, table_sem, stage_sem, *sems = refs[count + 2 :]
    spot = Spot(size)
    spot.meet(True)
    height = table_own.shape[0]
    mine = pltpu.make_async_copy(table_own, table.at[pl.ds(0, height)], table_sem.at[0])
    mine.start()
    swap = pltpu.make_async_remote_copy(
        src_ref=table_own,
        dst_ref=table.at[pl.ds(height, height)],
        send_sem=table_sem.at[1],
        recv_sem=table_sem.at[2],
        device_id=spot.to_core,
        device_id_type=MESH,
    )
    swap.start()
    out = pltpu.make_async_copy(table, table_out, table_sem.at[3])
    pieces, rows = found.shape[:2]
    width = 256
    state = {"ticks": 0, "done": 0}

    def copy_out(number):
        slot = lax.rem(number, 2)
        return pltpu.make_async_copy(stage.at[slot], found.at[number], stage_sem.at[slot])

    def work(first, last):
        def one(number, nothing):
            columns = lax.broadcasted_iota(jnp.int32, (rows, 2 * height), 1)
            hot[...] = jnp.where(columns == ids[number], 1.0, 0.0).astype(jnp.bfloat16)

            @pl.when(number >= 2)
            def _():
                copy_out(number - 2).wait()

            def part(at, nothing):
                window = pl.ds(pl.multiple_of(at * width, width), width)
                stage[lax.rem(number, 2), :, window] = jnp.dot(
                    hot[...], table[:, window], preferred_element_type=jnp.float32
                ).astype(jnp.bfloat16)
                return nothing

            lax.fori_loop(0, D // width, part, 0)
            copy_out(number).start()
            return nothing

        lax.fori_loop(first, last, one, 0)

    def tick(share=1):
        if state["done"] == pieces:
            return
        if state["done"] == 0:
            mine.wait()
            swap.wait_recv()
            out.start()
        last = min(pieces, state["done"] + share)
        work(state["done"], last)
        state["done"] = last

    gather_steps(
        size, ring_first, True, shards, wholes, sems, spot, tick, lambda at, turned, offset, other: None
    )
    tick(pieces)
    copy_out(pieces - 2).wait()
    copy_out(pieces - 1).wait()
    out.wait()
    swap.wait_send()


def look_up_call(size, shards, ring_first, table_own, ids, number):
    count = len(shards)
    height = table_own.shape[0]
    found = ids.shape[:2] + (D,)
    outs = [jax.ShapeDtypeStruct((4 * size,) + a.shape, a.dtype) for a in shards]
    outs.append(jax.ShapeDtypeStruct((2 * height, D), table_own.dtype))
    outs.append(jax.ShapeDtypeStruct(found, table_own.dtype))
    return pl.pallas_call(
        functools.partial(look_up_body, size, ring_first),
        out_shape=outs,
        in_specs=[pl.BlockSpec(memory_space=pl.ANY)] * (count + 1)
        + [pl.BlockSpec(memory_space=pltpu.VMEM)],
        out_specs=[pl.BlockSpec(memory_space=pl.ANY)] * (count + 2),
        scratch_shapes=[
            pltpu.VMEM((2 * height, D), table_own.dtype),
            pltpu.VMEM((ids.shape[1], 2 * height), table_own.dtype),
            pltpu.VMEM((2,) + found[1:], table_own.dtype),
            pltpu.SemaphoreType.DMA((4,)),
            pltpu.SemaphoreType.DMA((2,)),
        ]
        + gather_sems(count, size),
        compiler_params=pltpu.CompilerParams(
            collective_id=number, has_side_effects=True, vmem_limit_bytes=48 * 1024 * 1024
        ),
    )(*shards, table_own, ids)


def spread_body(size, shared, *refs):
    near, rest, ids_near, ids_rest, start = refs[:5]
    table_out, place_out, squares_ref = refs[5:8]
    near_all, rest_all, total, core_in, table_sem, *sems = refs[8:]
    ids = (ids_near, ids_rest)
    wholes = (near_all, rest_all)
    spot = Spot(size)
    spot.meet(True)
    height, length = table_out.shape[0], near.shape[0]
    block = height // 4
    first = pltpu.make_async_copy(start.at[pl.ds(0, height)], total, table_sem.at[0])
    first.start()
    swap = pltpu.make_async_remote_copy(
        src_ref=start.at[pl.ds(height, height)],
        dst_ref=core_in,
        send_sem=table_sem.at[1],
        recv_sem=table_sem.at[2],
        device_id=spot.to_core,
        device_id_type=MESH,
    )
    swap.start()
    place_out[...] = jnp.zeros_like(place_out)
    device = (2 * spot.half + spot.core) * size + spot.wide
    own_place = pl.ds(pl.multiple_of(lax.rem(device * shared, length), 16), shared)
    waiting = []
    state = {"started": False}

    def spread():
        pieces = list(waiting)
        waiting.clear()
        if not state["started"]:
            first.wait()
            state["started"] = True

        def one(number, nothing):
            window = pl.ds(pl.multiple_of(number * block, 16), block)
            row = number * block + lax.broadcasted_iota(jnp.int32, (block, length), 0)
            value = total[window, :]
            for at, piece in pieces:
                hot = jnp.where(row == ids[at][piece], 1.0, 0.0).astype(jnp.bfloat16)
                value = value + jnp.dot(
                    hot, wholes[at][piece], preferred_element_type=jnp.float32
                )
            total[window, :] = value
            return nothing

        lax.fori_loop(0, 4, one, 0)
        for at, piece in pieces:
            place_out[at] += wholes[at][piece, own_place, :].astype(jnp.float32)

    def ready(at, turned, offset, other):
        waiting.append((at, spot.index(turned, other, offset % size)))

    def tick():
        if len(waiting) >= 3:
            spread()

    gather_steps(size, (True, False), True, (near, rest), wholes, sems, spot, tick, ready)
    if waiting:
        spread()
    swap.wait_recv()
    step = height // 4

    def add(number, squares):
        window = pl.ds(pl.multiple_of(number * step, 16), step)
        value = total[window, :] + core_in[window, :]
        total[window, :] = value
        return squares + jnp.sum(value * value, axis=0, keepdims=True)

    squares = lax.fori_loop(0, 4, add, jnp.zeros((1, D), jnp.float32))
    squares_ref[...] = jnp.broadcast_to(squares, squares_ref.shape)
    out = pltpu.make_async_copy(total, table_out, table_sem.at[0])
    out.start()
    swap.wait_send()
    out.wait()


def spread_call(size, near, rest, ids, start, shared, number):
    height = start.shape[0] // 2
    pieces = (4 * size,) + near.shape
    return pl.pallas_call(
        functools.partial(spread_body, size, shared),
        out_shape=[
            jax.ShapeDtypeStruct((height, D), jnp.float32),
            jax.ShapeDtypeStruct((2, shared, D), jnp.float32),
            jax.ShapeDtypeStruct((8, D), jnp.float32),
        ],
        in_specs=[pl.BlockSpec(memory_space=pl.ANY)] * 2
        + [pl.BlockSpec(memory_space=pltpu.VMEM)] * 2
        + [pl.BlockSpec(memory_space=pl.ANY)],
        out_specs=[
            pl.BlockSpec(memory_space=pl.ANY),
            pl.BlockSpec(memory_space=pltpu.VMEM),
            pl.BlockSpec(memory_space=pltpu.VMEM),
        ],
        scratch_shapes=[
            pltpu.VMEM(pieces, near.dtype),
            pltpu.VMEM(pieces, near.dtype),
            pltpu.VMEM((height, D), jnp.float32),
            pltpu.VMEM((height, D), jnp.float32),
            pltpu.SemaphoreType.DMA((3,)),
        ]
        + gather_sems(2, size),
        compiler_params=pltpu.CompilerParams(
            collective_id=number, has_side_effects=True, vmem_limit_bytes=60 * 1024 * 1024
        ),
    )(near, rest, *ids, start)


def plain_gather_body(size, ring_first, across, *refs):
    count = len(ring_first)
    spot = Spot(size)
    spot.meet(across)
    gather_steps(
        size,
        ring_first,
        across,
        refs[:count],
        refs[count : 2 * count],
        refs[2 * count :],
        spot,
        lambda: None,
        lambda at, turned, offset, other: None,
    )


def gather_call(size, shards, ring_first, across, number):
    count = len(shards)
    total = (4 if across else 2) * size
    return pl.pallas_call(
        functools.partial(plain_gather_body, size, ring_first, across),
        out_shape=[jax.ShapeDtypeStruct((total,) + a.shape, a.dtype) for a in shards],
        in_specs=[pl.BlockSpec(memory_space=pl.ANY)] * count,
        out_specs=[pl.BlockSpec(memory_space=pl.ANY)] * count,
        scratch_shapes=gather_sems(count, size),
        compiler_params=pltpu.CompilerParams(collective_id=number, has_side_effects=True),
    )(*shards)


def cast_body(size, everyone, own_ref, out_ref, come_sem, send_sem, local_sem):
    spot = Spot(size)
    group = (4 if everyone else 2) * size
    narrow = lax.axis_index("narrow")
    mine = (narrow if everyone else spot.half) * size + spot.wide

    def device(step):
        at = lax.rem(mine + step, group)
        block = lax.div(at, size)
        return (block if everyone else 2 * block + spot.core, lax.rem(at, size))

    barrier = pltpu.get_barrier_semaphore()

    def greet(step, nothing):
        pl.semaphore_signal(barrier, inc=1, device_id=device(step), device_id_type=MESH)
        return nothing

    def tell(step, nothing):
        pltpu.make_async_remote_copy(
            src_ref=own_ref,
            dst_ref=out_ref.at[mine],
            send_sem=send_sem,
            recv_sem=come_sem,
            device_id=device(step),
            device_id_type=MESH,
        ).start()
        return nothing

    lax.fori_loop(1, group, greet, 0)
    keep = pltpu.make_async_copy(own_ref, out_ref.at[mine], local_sem)
    keep.start()
    pl.semaphore_wait(barrier, group - 1)
    lax.fori_loop(1, group, tell, 0)
    others = out_ref.at[pl.ds(0, group - 1)]
    pltpu.make_async_copy(others, others, come_sem).wait()
    pltpu.make_async_copy(others, others, send_sem).wait()
    keep.wait()


def cast_call(size, block, everyone, number):
    group = (4 if everyone else 2) * size
    return pl.pallas_call(
        functools.partial(cast_body, size, everyone),
        out_shape=jax.ShapeDtypeStruct((group,) + block.shape, block.dtype),
        in_specs=[pl.BlockSpec(memory_space=pltpu.VMEM)],
        out_specs=pl.BlockSpec(memory_space=pltpu.VMEM),
        scratch_shapes=[pltpu.SemaphoreType.DMA] * 3,
        compiler_params=pltpu.CompilerParams(collective_id=number, has_side_effects=True),
    )(block)


def scatter_body(size, half_first, across, bases, working, *refs):
    count = len(half_first)
    extra_in = FeedBack.INPUTS if working else 0
    extra_out = FeedBack.OUTPUTS if working else 0
    arrays, refs = refs[:count], refs[count:]
    work_in, refs = refs[:extra_in], refs[extra_in:]
    outs, squares_ref, refs = refs[:count], refs[count], refs[count + 1 :]
    work_out, refs = refs[:extra_out], refs[extra_out:]
    own, core_in, half_in, ring_in = (
        refs[part * count : (1 + part) * count] for part in range(4)
    )
    local_sem, core_sem, half_sem, ring_sem, send_sem = refs[4 * count : 4 * count + 5]
    work = FeedBack(work_in, work_out, refs[4 * count + 5 :]) if working else None
    squares = []
    spot = Spot(size)
    far = size // 2
    slots = [far] + [o for at in range(far - 1, 0, -1) for o in (at, -at)] + [0]
    sent = []

    def landed(region, sem):
        pltpu.make_async_copy(region, region, sem).wait()

    def send(source, target, device, number, at, sem):
        copy = pltpu.make_async_remote_copy(
            src_ref=source,
            dst_ref=target,
            send_sem=send_sem.at[at, number],
            recv_sem=sem,
            device_id=device,
            device_id_type=MESH,
        )
        copy.start()
        sent.append(copy)

    def source_of(at, turned, other_core, offset):
        if across:
            return arrays[at].at[spot.index(turned, other_core, offset % size)]
        base, stride = bases[at]
        return arrays[at].at[base + stride * (turned * size + offset % size)]

    def add(target, parts):
        rows, columns = target.shape
        width = 512 if columns % 512 == 0 else 256 if columns % 256 == 0 else 128

        def one(step, nothing):
            window = pl.ds(pl.multiple_of(step * width, width), width)
            if len(parts) == 2 and parts[1][1:] == (0, rows):
                one, two = parts[0][0][:, window], parts[1][0][:, window]
                if one.dtype == target.dtype:
                    target[:, window] = one + two
                    return nothing
            total = parts[0][0][:, window].astype(jnp.float32)
            for part, first, last in parts[1:]:
                if first == 0 and last == rows:
                    total = total + part[:, window].astype(jnp.float32)
            target[:, window] = total.astype(target.dtype)
            for part, first, last in parts[1:]:
                if first != 0 or last != rows:
                    span = pl.ds(first, last - first)
                    target[span, window] = (
                        total[first:last] + part[span, window].astype(jnp.float32)
                    ).astype(target.dtype)
            return nothing

        lax.fori_loop(0, columns // width, one, 0)

    def square_sum(ref):
        width = 128

        def one(step, total):
            part = ref[:, pl.ds(pl.multiple_of(step * width, width), width)].astype(jnp.float32)
            return total + jnp.sum(part * part, axis=0, keepdims=True)

        return lax.fori_loop(
            0, ref.shape[1] // width, one, jnp.zeros((1, width), jnp.float32)
        )

    def ring_slot(way, step):
        return way * far + step - 1

    def base(at, turned, offset):
        k = offset % size
        rows = own[at].shape[1]
        here = own[at].at[turned * size + k]
        landed(here, local_sem.at[at, turned * size + k])
        parts = [(here, 0, rows)]
        if across:
            there = core_in[at].at[turned * size + k]
            landed(there, core_sem.at[at, turned * size + k])
            parts.append((there, 0, rows))
        return here, parts

    def ring_parts(at, turned, offset):
        parts = []
        rows = own[at].shape[1]
        cut = cut_of(rows)
        ways = (0, 1) if offset == 0 else (0,) if offset > 0 else (1,)
        for way in ways:
            step = far - abs(offset)
            slot = ring_slot(way, step)
            if half_first[at]:
                if step == 1:
                    first, last = (0, cut) if way == 0 else (cut, rows)
                else:
                    first, last = 0, rows
                if first == last:
                    continue
                region = ring_in[at].at[slot]
                span = region if (first, last) == (0, rows) else region.at[pl.ds(first, last - first)]
                landed(span, ring_sem.at[at, slot])
                parts.append((region, first, last))
            else:
                if step == 1 and turned != way:
                    continue
                region = ring_in[at].at[turned * 2 * far + slot]
                landed(region, ring_sem.at[at, turned * 2 * far + slot])
                parts.append((region, 0, rows))
        return parts

    def ring_send(at, turned, offset):
        here = own[at].at[turned * size + offset % size]
        rows = own[at].shape[1]
        cut = cut_of(rows)
        step = far - abs(offset) + 1
        if offset == far:
            if half_first[at]:
                spans = [(0, pl.ds(0, cut))] + ([(1, pl.ds(cut, rows - cut))] if cut < rows else [])
                for way, span in spans:
                    slot = ring_slot(way, 1)
                    send(
                        here.at[span],
                        ring_in[at].at[slot].at[span],
                        (spot.right, spot.left)[way],
                        slot,
                        at,
                        ring_sem.at[at, slot],
                    )
                return
            ways = (turned,)
        else:
            ways = (0,) if offset > 0 else (1,)
        for way in ways:
            slot = ring_slot(way, step) + (0 if half_first[at] else turned * 2 * far)
            send(
                here,
                ring_in[at].at[slot],
                (spot.right, spot.left)[way],
                slot,
                at,
                ring_sem.at[at, slot],
            )

    spot.meet(across)
    core_base = 4 * far + size
    for offset in slots:
        k = offset % size
        for turned in (1, 0):
            for at in range(count):
                if across:
                    send(
                        source_of(at, turned, 1, offset),
                        core_in[at].at[turned * size + k],
                        spot.to_core,
                        core_base + turned * size + k,
                        at,
                        core_sem.at[at, turned * size + k],
                    )
                pltpu.make_async_copy(
                    source_of(at, turned, 0, offset),
                    own[at].at[turned * size + k],
                    local_sem.at[at, turned * size + k],
                ).start()

    if working:
        work.start()

    def turned_half(offset):
        for at in range(count):
            if half_first[at]:
                here, parts = base(at, 1, offset)
                k = offset % size
                if across:
                    add(here, parts)
                send(here, half_in[at].at[k], spot.to_half, 4 * far + k, at, half_sem.at[at, k])

    def straight(offset):
        for at in range(count):
            if half_first[at]:
                here, parts = base(at, 0, offset)
                k = offset % size
                landed(half_in[at].at[k], half_sem.at[at, k])
                parts.append((half_in[at].at[k], 0, own[at].shape[1]))
                parts += ring_parts(at, 0, offset) if offset != far else []
                if offset == 0:
                    add(outs[at], parts)
                    squares.append(square_sum(outs[at]))
                else:
                    add(here, parts)
                    ring_send(at, 0, offset)

    def both(offset):
        for at in range(count):
            if not half_first[at]:
                for turned in (1, 0):
                    here, parts = base(at, turned, offset)
                    parts += ring_parts(at, turned, offset) if offset != far else []
                    if offset == 0 and turned == 0:
                        landed(half_in[at].at[0], half_sem.at[at, 0])
                        parts.append((half_in[at].at[0], 0, own[at].shape[1]))
                        add(outs[at], parts)
                        squares.append(square_sum(outs[at]))
                        continue
                    if len(parts) > 1:
                        add(here, parts)
                    if offset == 0:
                        send(here, half_in[at].at[0], spot.to_half, 4 * far, at, half_sem.at[at, 0])
                    else:
                        ring_send(at, turned, offset)

    groups = [[far]] + [[at, -at] for at in range(far - 1, 0, -1)] + [[0]]
    def tick():
        if working:
            work.tick()

    tick()
    for number, group in enumerate(groups):
        for offset in group:
            turned_half(offset)
        tick()
        for offset in group:
            both(offset)
        tick()
        if number > 0:
            for offset in groups[number - 1]:
                straight(offset)
            tick()
    for offset in groups[-1]:
        straight(offset)
    total = squares[0]
    for one in squares[1:]:
        total = total + one
    squares_ref[...] = jnp.broadcast_to(total, squares_ref.shape)
    if working:
        work.finish()
    for copy in sent:
        copy.wait_send()


def scatter_call(size, arrays, half_first, across, out_type, number, bases=None, work=None):
    count = len(arrays)
    far = size // 2
    pieces = [a.shape[1:] for a in arrays]
    own = [pltpu.VMEM((2 * size,) + p, a.dtype) for p, a in zip(pieces, arrays)]
    core_in = [
        pltpu.VMEM((2 * size if across else 1,) + p, a.dtype) for p, a in zip(pieces, arrays)
    ]
    half_in = [
        pltpu.VMEM((size if first else 1,) + p, a.dtype)
        for p, a, first in zip(pieces, arrays, half_first)
    ]
    ring_in = [
        pltpu.VMEM((2 * far if first else 4 * far,) + p, a.dtype)
        for p, a, first in zip(pieces, arrays, half_first)
    ]
    outs = [jax.ShapeDtypeStruct(p, out_type) for p in pieces]
    outs.append(jax.ShapeDtypeStruct((8, 128), jnp.float32))
    in_specs = [pl.BlockSpec(memory_space=pl.ANY)] * count
    out_specs = [pl.BlockSpec(memory_space=pltpu.VMEM)] * (count + 1)
    scratch = (
        own
        + core_in
        + half_in
        + ring_in
        + [
            pltpu.SemaphoreType.DMA((count, 2 * size)),
            pltpu.SemaphoreType.DMA((count, 2 * size)),
            pltpu.SemaphoreType.DMA((count, size)),
            pltpu.SemaphoreType.DMA((count, 4 * far)),
            pltpu.SemaphoreType.DMA((count, 4 * far + 3 * size)),
        ]
    )
    if work is not None:
        in_specs += FeedBack.in_specs()
        outs += FeedBack.out_shape(work[0], work[4])
        out_specs += FeedBack.out_specs()
        scratch += FeedBack.scratch(work[0].shape[0])
    return pl.pallas_call(
        functools.partial(
            scatter_body, size, half_first, across, bases or ((0, 1),) * count, work is not None
        ),
        out_shape=outs,
        in_specs=in_specs,
        out_specs=out_specs,
        scratch_shapes=scratch,
        compiler_params=pltpu.CompilerParams(
            collective_id=number, has_side_effects=True, vmem_limit_bytes=60 * 1024 * 1024
        ),
    )(*arrays, *(work or ()))


def layer_norm(values, gain, shift):
    center = values - jnp.mean(values, axis=-1, keepdims=True)
    spread = jnp.mean(center * center, axis=-1, keepdims=True)
    return center * lax.rsqrt(spread + 1e-05) * gain + shift


def gelu_tanh(values):
    return jax.nn.gelu(values, approximate=True)


INNER = (((1,), (1,)), ((), ()))
OUTER = (((0,), (0,)), ((), ()))
GROUP = 8


def dot_inner(one, two):
    return lax.dot_general(one, two, INNER, preferred_element_type=jnp.float32)


def dot_outer(one, two):
    return lax.dot_general(one, two, OUTER, preferred_element_type=jnp.float32)


def fill_mask(mask_ref, length):
    key = lax.broadcasted_iota(jnp.int32, mask_ref.shape, 0)
    query = lax.broadcasted_iota(jnp.int32, mask_ref.shape, 1)
    mask_ref[...] = jnp.where((key <= query) & (key < length), 0.0, -1e30)


def probs_by_key(query, key, mask):
    scores = dot_inner(key, query * 0.125) + mask
    raised = jnp.exp(scores - jnp.max(scores, axis=0, keepdims=True))
    return raised * (1.0 / jnp.sum(raised, axis=0, keepdims=True))


def attend_body(length_ref, query_ref, key_ref, value_ref, mixed_ref, mask_ref):
    @pl.when(pl.program_id(0) == 0)
    def _():
        fill_mask(mask_ref, length_ref[0])

    mixed = []
    for head in range(GROUP):
        lanes = slice(head * HD, (head + 1) * HD)
        probs = probs_by_key(query_ref[:, lanes], key_ref[:, lanes], mask_ref[...])
        mixed.append(dot_outer(value_ref[:, lanes], probs.astype(jnp.bfloat16)))
    mixed_ref[...] = jnp.concatenate(mixed).T.astype(jnp.bfloat16)


def attend_specs(rows, steps):
    return [pl.BlockSpec(memory_space=pltpu.SMEM)] + [
        pl.BlockSpec((rows, GROUP * HD), lambda p, part=part: (0, part * steps + p))
        for part in range(3)
    ]


def attend(projected, seq_lengths):
    rows = projected.shape[0]
    steps = HEADS // GROUP
    return pl.pallas_call(
        attend_body,
        grid=(steps,),
        out_shape=jax.ShapeDtypeStruct((rows, D), jnp.bfloat16),
        in_specs=attend_specs(rows, steps),
        out_specs=pl.BlockSpec((rows, GROUP * HD), lambda p: (0, p)),
        scratch_shapes=[pltpu.VMEM((rows, rows), jnp.float32)],
        compiler_params=pltpu.CompilerParams(vmem_limit_bytes=32 * 1024 * 1024),
        cost_estimate=pl.CostEstimate(
            flops=4 * HEADS * rows * rows * HD, bytes_accessed=8 * rows * D, transcendentals=0
        ),
    )(seq_lengths, projected, projected, projected)


def attend_back_body(length_ref, query_ref, key_ref, value_ref, grad_ref, out_ref, mask_ref):
    @pl.when(pl.program_id(0) == 0)
    def _():
        fill_mask(mask_ref, length_ref[0])

    step = pl.program_id(0)
    low = jnp.bfloat16
    grad_query, grad_key, grad_value = [], [], []
    for head in range(GROUP):
        lanes = slice(head * HD, (head + 1) * HD)
        query, key, grad = query_ref[:, lanes], key_ref[:, lanes], grad_ref[:, lanes]
        probs = probs_by_key(query, key, mask_ref[...])
        grad_probs = dot_inner(value_ref[:, lanes], grad)
        grad_value.append(jnp.dot(probs.astype(low), grad, preferred_element_type=jnp.float32))
        key_dot = jnp.sum(grad_probs * probs, axis=0, keepdims=True)
        scores_low = (probs * (grad_probs - key_dot)).astype(low)
        grad_key.append(jnp.dot(scores_low, query, preferred_element_type=jnp.float32) * 0.125)
        grad_query.append(dot_outer(key, scores_low) * 0.125)
    results = (
        jnp.concatenate(grad_query).T,
        jnp.concatenate(grad_key, axis=1),
        jnp.concatenate(grad_value, axis=1),
    )
    for part, value in enumerate(results):
        window = pl.ds(pl.multiple_of(part * D + step * GROUP * HD, GROUP * HD), GROUP * HD)
        out_ref[:, window] = value.astype(low)


def attend_back(projected, grad_mixed, seq_lengths):
    rows = projected.shape[0]
    steps = HEADS // GROUP
    return pl.pallas_call(
        attend_back_body,
        grid=(steps,),
        out_shape=jax.ShapeDtypeStruct((rows, 3 * D), jnp.bfloat16),
        in_specs=attend_specs(rows, steps)
        + [pl.BlockSpec((rows, GROUP * HD), lambda p: (0, p))],
        out_specs=pl.BlockSpec((rows, 3 * D), lambda p: (0, 0)),
        scratch_shapes=[pltpu.VMEM((rows, rows), jnp.float32)],
        compiler_params=pltpu.CompilerParams(vmem_limit_bytes=48 * 1024 * 1024),
        cost_estimate=pl.CostEstimate(
            flops=10 * HEADS * rows * rows * HD, bytes_accessed=16 * rows * D, transcendentals=0
        ),
    )(seq_lengths, projected, projected, projected, grad_mixed)


class FeedBack:
    CHUNK = 256
    INPUTS = 6
    OUTPUTS = 4

    def __init__(self, ins, outs, scratch):
        self.branch, self.turned, pre, hidden, w_fc, w_proj = ins
        self.grad_normed, self.bias, self.grad_fc, self.grad_proj = outs
        pre_in, hidden_in, fc_in, proj_in, self.fc_out, self.proj_out, self.in_sem, self.out_sem = scratch
        self.chunks = w_proj.shape[0] // self.CHUNK
        self.sources = (pre, hidden, w_fc, w_proj)
        self.slots = (pre_in, hidden_in, fc_in, proj_in)
        self.done = 0

    def span(self, number):
        return pl.ds(pl.multiple_of(number * self.CHUNK, self.CHUNK), self.CHUNK)

    def loads(self, number):
        slot = lax.rem(number, 2)
        for at, (source, place) in enumerate(zip(self.sources, self.slots)):
            here = source.at[self.span(number)] if at == 3 else source.at[:, self.span(number)]
            yield pltpu.make_async_copy(here, place.at[slot], self.in_sem.at[at, slot])

    def stores(self, number):
        slot = lax.rem(number, 2)
        yield pltpu.make_async_copy(
            self.fc_out.at[slot], self.grad_fc.at[:, self.span(number)], self.out_sem.at[0, slot]
        )
        yield pltpu.make_async_copy(
            self.proj_out.at[slot], self.grad_proj.at[self.span(number)], self.out_sem.at[1, slot]
        )

    def start(self):
        self.grad_normed[...] = jnp.zeros_like(self.grad_normed)
        for copy in self.loads(0):
            copy.start()

    def run(self, first, last):
        def one(number, nothing):
            slot = lax.rem(number, 2)
            for copy in self.loads(number):
                copy.wait()

            @pl.when(number + 1 < self.chunks)
            def _():
                for copy in self.loads(number + 1):
                    copy.start()

            @pl.when(number >= 2)
            def _():
                for copy in self.stores(number - 2):
                    copy.wait()

            low = jnp.bfloat16
            pre_in, hidden_in, fc_in, proj_in = self.slots
            grad_hidden = dot_inner(self.branch[...], proj_in[slot])
            value = pre_in[slot]
            square = value * value
            bent = jnp.tanh(0.7978845608 * value * (1.0 + 0.044715 * square))
            slope = 0.5 * (1.0 + bent) + 0.5 * value * (1.0 - bent * bent) * (
                0.7978845608 * (1.0 + 3.0 * 0.044715 * square)
            )
            pre_low = (grad_hidden * slope).astype(low)
            self.bias[:, self.span(number)] = jnp.sum(
                pre_low.astype(jnp.float32), axis=0, keepdims=True
            )
            self.grad_normed[...] += dot_inner(pre_low, fc_in[slot])
            self.fc_out[slot] = jnp.dot(
                self.turned[...], pre_low, preferred_element_type=jnp.float32
            ).astype(low)
            self.proj_out[slot] = dot_outer(hidden_in[slot], self.branch[...]).astype(low)
            for copy in self.stores(number):
                copy.start()
            return nothing

        lax.fori_loop(first, last, one, 0)

    def tick(self):
        if self.done < self.chunks:
            self.run(self.done, self.done + 1)
            self.done += 1

    def finish(self):
        if self.done < self.chunks:
            self.run(self.done, self.chunks)
        for number in (self.chunks - 2, self.chunks - 1):
            for copy in self.stores(jnp.int32(number)):
                copy.wait()

    @classmethod
    def in_specs(cls):
        return [pl.BlockSpec(memory_space=pltpu.VMEM)] * 2 + [pl.BlockSpec(memory_space=pl.ANY)] * 4

    @classmethod
    def out_specs(cls):
        return [pl.BlockSpec(memory_space=pltpu.VMEM)] * 2 + [pl.BlockSpec(memory_space=pl.ANY)] * 2

    @classmethod
    def out_shape(cls, branch, w_fc):
        hidden = w_fc.shape[1]
        return [
            jax.ShapeDtypeStruct(branch.shape, jnp.float32),
            jax.ShapeDtypeStruct((1, hidden), jnp.float32),
            jax.ShapeDtypeStruct((D, hidden), jnp.bfloat16),
            jax.ShapeDtypeStruct((hidden, D), jnp.bfloat16),
        ]

    @classmethod
    def scratch(cls, rows):
        low, chunk = jnp.bfloat16, cls.CHUNK
        return [
            pltpu.VMEM((2, rows, chunk), jnp.float32),
            pltpu.VMEM((2, rows, chunk), low),
            pltpu.VMEM((2, D, chunk), low),
            pltpu.VMEM((2, chunk, D), low),
            pltpu.VMEM((2, D, chunk), low),
            pltpu.VMEM((2, chunk, D), low),
            pltpu.SemaphoreType.DMA((4, 2)),
            pltpu.SemaphoreType.DMA((2, 2)),
        ]


def feed_back_body(*refs):
    ins, outs = FeedBack.INPUTS, FeedBack.OUTPUTS
    work = FeedBack(refs[:ins], refs[ins : ins + outs], refs[ins + outs :])
    work.start()
    work.finish()


def feed_back(operands):
    branch, w_fc = operands[0], operands[4]
    return pl.pallas_call(
        feed_back_body,
        out_shape=FeedBack.out_shape(branch, w_fc),
        in_specs=FeedBack.in_specs(),
        out_specs=FeedBack.out_specs(),
        scratch_shapes=FeedBack.scratch(branch.shape[0]),
        compiler_params=pltpu.CompilerParams(vmem_limit_bytes=40 * 1024 * 1024),
    )(*operands)


def layer_forward(stream, weights, vector, seq_lengths):
    w_qkv, w_out, w_fc, w_proj = weights
    normed_low = layer_norm(stream, vector[0:D], vector[D : 2 * D]).astype(jnp.bfloat16)
    qkv_bias = jnp.concatenate(
        [vector[4 * D : 5 * D], jnp.zeros((D,), jnp.float32), vector[5 * D : 6 * D]]
    )
    projected = (jnp.dot(normed_low, w_qkv, preferred_element_type=jnp.float32) + qkv_bias).astype(
        jnp.bfloat16
    )
    mixed_low = attend(projected, seq_lengths)
    stream_mid = (
        stream
        + jnp.dot(mixed_low, w_out, preferred_element_type=jnp.float32)
        + vector[6 * D : 7 * D]
    )
    normed_two = layer_norm(stream_mid, vector[2 * D : 3 * D], vector[3 * D : 4 * D]).astype(
        jnp.bfloat16
    )
    hidden_pre = (
        jnp.dot(normed_two, w_fc, preferred_element_type=jnp.float32) + vector[8 * D : 8 * D + FF]
    )
    hidden_low = gelu_tanh(hidden_pre).astype(jnp.bfloat16)
    stream_out = (
        stream_mid
        + jnp.dot(hidden_low, w_proj, preferred_element_type=jnp.float32)
        + vector[7 * D : 8 * D]
    )
    return (
        stream_out,
        (
            stream,
            normed_low,
            projected,
            mixed_low,
            stream_mid,
            normed_two,
            hidden_pre,
            hidden_low,
        ),
    )


def feed_plain(operands):
    branch_low, normed_turned, hidden_pre, hidden_low, w_fc, w_proj = operands
    grad_wproj = jnp.dot(hidden_low.T, branch_low, preferred_element_type=jnp.bfloat16)
    grad_hidden = jnp.dot(branch_low, w_proj.T, preferred_element_type=jnp.float32)
    pre_low = jax.vjp(gelu_tanh, hidden_pre)[1](grad_hidden)[0].astype(jnp.bfloat16)
    grad_wfc = jnp.dot(normed_turned, pre_low, preferred_element_type=jnp.bfloat16)
    grad_normed_two = jnp.dot(pre_low, w_fc.T, preferred_element_type=jnp.float32)
    bias = jnp.sum(pre_low.astype(jnp.float32), axis=0)
    return grad_normed_two, bias, grad_wfc, grad_wproj


def layer_backward(grad_out, saved_acts, weights, vector, seq_lengths, feed):
    (
        stream,
        normed_low,
        projected,
        mixed_low,
        stream_mid,
        normed_two,
        hidden_pre,
        hidden_low,
    ) = saved_acts
    w_qkv, w_out, w_fc, w_proj = weights
    branch_low = grad_out.astype(jnp.bfloat16)
    grad_normed_two, grad_bias, grad_wfc, grad_wproj = feed(
        (branch_low, normed_two.T, hidden_pre, hidden_low, w_fc, w_proj)
    )
    grad_mid, grad_gain_two, grad_shift_two = jax.vjp(
        layer_norm, stream_mid, vector[2 * D : 3 * D], vector[3 * D : 4 * D]
    )[1](grad_normed_two)
    grad_mid = grad_mid + grad_out
    attn_low = grad_mid.astype(jnp.bfloat16)
    grad_wout = jnp.dot(mixed_low.T, attn_low, preferred_element_type=jnp.bfloat16)
    grad_mixed = jnp.dot(attn_low, w_out.T, preferred_element_type=jnp.float32).astype(
        jnp.bfloat16
    )
    qkv_low = attend_back(projected, grad_mixed, seq_lengths)
    grad_wqkv = jnp.dot(normed_low.T, qkv_low, preferred_element_type=jnp.bfloat16)
    grad_normed = jnp.dot(qkv_low, w_qkv.T, preferred_element_type=jnp.float32)
    grad_input, grad_gain_one, grad_shift_one = jax.vjp(
        layer_norm, stream, vector[0:D], vector[D : 2 * D]
    )[1](grad_normed)
    bias_qkv = jnp.sum(qkv_low.astype(jnp.float32), axis=0)
    grad_vector = jnp.concatenate(
        [
            grad_gain_one,
            grad_shift_one,
            grad_gain_two,
            grad_shift_two,
            bias_qkv[0:D],
            bias_qkv[2 * D : 3 * D],
            jnp.sum(attn_low.astype(jnp.float32), axis=0),
            jnp.sum(branch_low.astype(jnp.float32), axis=0),
            grad_bias.reshape(-1),
        ]
    )
    return (grad_input + grad_mid, (grad_wqkv, grad_wout, grad_wfc, grad_wproj), grad_vector)


def adamw(weight, moment_one, moment_two, gradient, step_rate, decay_rate, step_float):
    one_new = 0.5 * moment_one + 0.5 * gradient
    two_new = 0.5 * moment_two + 0.5 * gradient * gradient
    fix_scale = 1.0 - jnp.power(0.5, step_float)
    update = one_new / fix_scale / (jnp.sqrt(two_new / fix_scale) + 1e-08)
    return (weight - step_rate * (update + decay_rate * weight), one_new, two_new)


def on_device(
    token_ids,
    seq_lengths,
    loss_slots,
    target_ids,
    step_count,
    w_qkv,
    w_out,
    w_fc,
    w_proj,
    vectors,
    pos_table,
    embed_table,
    mom_qkv,
    mom_out,
    mom_fc,
    mom_proj,
    mom_vectors,
    mom_pos,
    mom_embed,
    sec_qkv,
    sec_out,
    sec_fc,
    sec_proj,
    sec_vectors,
    sec_pos,
    sec_embed,
):
    per_layer = 8 * D + FF
    net = Net()
    size, halves = net.size, net.halves
    same_core = halves * size
    devices = 2 * same_core
    low = jnp.bfloat16
    near = LEN // 2
    fused = size <= 8
    rest = LEN - near
    slots = loss_slots.shape[0]

    half_of = jnp.arange(halves)[:, None]
    wide_index = jnp.arange(size)[None, :]
    place_of = jnp.where(wide_index % 2 == 0, wide_index // 2, size - 1 - (wide_index - 1) // 2)
    to_device = ((half_of ^ net.half) * size + (place_of - net.place) % size).reshape(-1)
    offsets = (net.place + wide_index) % size
    wide_there = jnp.where(offsets < size // 2, 2 * offsets, 2 * (size - 1 - offsets) + 1)
    from_device = ((half_of ^ net.half) * size + wide_there).reshape(-1)

    numbers = jnp.concatenate([token_ids, loss_slots, target_ids, seq_lengths])
    numbers = jnp.pad(numbers, (0, -numbers.shape[0] % 1024)).reshape(-1, 128)
    numbers = cast_call(size, numbers, True, 5).reshape(devices, -1)
    all_tokens = numbers[:, :LEN]
    token_total = jnp.sum(numbers[:, LEN + 2 * slots].astype(jnp.float32))
    on_core = from_device + (from_device // size + net.core) * size
    numbers = jnp.take(numbers, on_core, axis=0).reshape(halves, size, -1)
    group_tokens = numbers[:, :, :LEN]
    group_slots = numbers[:, :, LEN : LEN + slots].reshape(same_core * slots)
    group_targets = numbers[:, :, LEN + slots : LEN + 2 * slots].reshape(same_core * slots)

    own_rows = embed_table.shape[0]
    height = own_rows + -own_rows % 64
    chip_rows = 2 * height
    table_own = jnp.pad(embed_table.astype(low), ((0, height - own_rows), (0, 0)))
    own_start = net.device * own_rows
    other_start = (net.device + (1 - 2 * net.core) * size) * own_rows

    def locate(ids):
        mine = ids - own_start
        other = ids - other_start
        return jnp.where(
            (mine >= 0) & (mine < own_rows),
            mine,
            jnp.where((other >= 0) & (other < own_rows), other + height, -1),
        )

    def one_hot(ids):
        return (ids[:, None] == jnp.arange(chip_rows)[None, :]).astype(low)

    local_tokens = locate(group_tokens).reshape(same_core, LEN)
    ids_near, ids_rest = local_tokens[:, :near], local_tokens[:, near:]

    shared = pos_table.shape[0]
    vector_rows = -(-vectors.shape[0] // D)
    padded = jnp.pad(vectors, (0, vector_rows * D - vectors.shape[0])).reshape(vector_rows, D)
    spare = -(shared + vector_rows) % 16
    small_own = jnp.concatenate([pos_table, padded, jnp.zeros((spare, D), jnp.float32)])
    shards_low = []
    for layer_at in range(LAYERS):
        shards_low += [part[layer_at].astype(low) for part in (w_qkv, w_fc, w_proj, w_out)]
    shards_low.append(small_own.astype(low))
    ring_first = (True, True, False, False) * LAYERS + (False,)
    if fused:
        *gathered, table_low, found = look_up_call(
            size, shards_low, ring_first, table_own, jnp.concatenate([ids_near, ids_rest])[..., None], 1
        )
        stream = scatter_call(
            size, [found, found], (True, False), False, low, 2, ((0, 1), (same_core, 1))
        )
        stream = jnp.concatenate(stream[:2])
    else:
        gathered = gather_call(size, shards_low, ring_first, True, 1)
        table_low = jnp.concatenate([table_own, net.swap_core(table_own)])
        found = [
            jnp.dot(
                one_hot(ids.reshape(-1)), table_low, preferred_element_type=jnp.float32
            ).astype(low).reshape(same_core, -1, D)
            for ids in (ids_near, ids_rest)
        ]
        bands = max(1, same_core // 16)
        band = D // bands
        parts = []
        for at in range(bands):
            window = [part[:, :, at * band : (at + 1) * band] for part in found]
            parts.append(
                jnp.concatenate(scatter_call(size, window, (True, False), False, low, 2)[:2])
            )
        stream = jnp.concatenate(parts, axis=1)
    small_low = gathered[-1]
    pos_low = small_low[:, :shared].reshape(devices * shared, D)
    vector_all = (
        small_low[:, shared : shared + vector_rows]
        .reshape(devices, vector_rows * D)[:, : vectors.shape[0]]
        .reshape(-1)
        .astype(jnp.float32)
    )

    stream = stream.astype(jnp.float32) + pos_low[:LEN].astype(jnp.float32)

    kept_weights = []
    saved_list = []
    for layer_at in range(LAYERS):
        w_a, w_c, w_d, w_b = (
            part.reshape(-1, part.shape[2]) for part in gathered[layer_at * 4 : layer_at * 4 + 4]
        )
        weights = (w_a, w_b, w_c, w_d)
        kept_weights.append(weights)
        stream, saved_acts = layer_forward(
            stream, weights, vector_all[layer_at * per_layer : (layer_at + 1) * per_layer], seq_lengths
        )
        saved_list.append(saved_acts)
    tail_start = LAYERS * per_layer
    final_norm, final_pull = jax.vjp(
        layer_norm,
        stream,
        vector_all[tail_start : tail_start + D],
        vector_all[tail_start + D : tail_start + 2 * D],
    )
    slot_rows = jnp.maximum(loss_slots, 0)
    own_picked = final_norm[slot_rows].astype(low)
    some = slots // 2
    group_rows = jnp.concatenate(
        gather_call(size, [own_picked[:some], own_picked[some:]], (True, False), False, 6), axis=1
    ).reshape(same_core * slots, D)
    real = jnp.arange(chip_rows) % height < own_rows
    logits = jnp.where(
        real, jnp.dot(group_rows, table_low.T, preferred_element_type=jnp.float32), -1e30
    )
    target_onehot = locate(group_targets)[:, None] == jnp.arange(chip_rows)[None, :]
    row_max = jnp.max(logits, axis=-1)
    row_total = jnp.sum(jnp.exp(logits - row_max[:, None]), axis=-1)
    target_logit = jnp.sum(jnp.where(target_onehot, logits, 0.0), axis=-1)
    stats = jnp.stack([row_max, row_total, target_logit], axis=-1)
    stats = jnp.take(stats.reshape(same_core, slots * 3), to_device, axis=0)
    stats = stats.reshape(same_core * slots, 3).T.reshape(-1)
    entries = stats.shape[0]
    stats = jnp.pad(stats, (0, -entries % 1024)).reshape(-1, 128)
    stats = cast_call(size, stats, False, 7).reshape(same_core, -1)[:, :entries]
    stats = stats.reshape(same_core, 3, same_core * slots)
    joint_max = jnp.max(stats[:, 0], axis=0)
    joint_total = jnp.sum(stats[:, 1] * jnp.exp(stats[:, 0] - joint_max), axis=0)
    stats = jnp.stack([joint_max + jnp.log(joint_total), jnp.sum(stats[:, 2], axis=0)])
    stats = stats.reshape(2, same_core, slots)
    stats = jnp.take(stats, from_device, axis=1).reshape(2, same_core * slots)
    log_total, merged_target = stats[0], stats[1]
    group_used = (group_slots >= 0).astype(jnp.float32)
    own_loss = jnp.sum(((log_total - merged_target) * group_used)[:slots])
    grad_logits = (
        (jnp.exp(logits - log_total[:, None]) - target_onehot.astype(jnp.float32))
        * (group_used / token_total)[:, None]
    ).astype(low)
    grad_rows = jnp.dot(grad_logits, table_low, preferred_element_type=jnp.float32)
    grad_rows = grad_rows.reshape(2 * same_core, some, D)
    grad_rows = jnp.concatenate(
        scatter_call(
            size,
            [grad_rows, grad_rows],
            (True, False),
            False,
            jnp.float32,
            8,
            ((0, 2), (1, 2)),
        )[:2]
    )
    grad_final = jnp.zeros((LEN, D), jnp.float32).at[slot_rows].add(grad_rows)
    grad_stream, grad_gain_final, grad_shift_final = final_pull(grad_final)
    layer_shards = []
    vector_grads = []
    squares = jnp.zeros((128,), jnp.float32)
    pending = None

    def reduce_layers(full_grads, number, more=(), work=None):
        grad_a, grad_b, grad_c, grad_d = full_grads
        arrays = [part.reshape(devices, -1, part.shape[1]) for part in (grad_a, grad_c, grad_d, grad_b)]
        arrays += more
        outs = scatter_call(
            size,
            arrays,
            (True, True, False, False) + (False,) * len(more),
            True,
            jnp.float32,
            number,
            work=work,
        )
        shard_a, shard_c, shard_d, shard_b, *rest = outs
        layer_shards.insert(0, (shard_a, shard_b, shard_c, shard_d))
        return rest

    for layer_at in reversed(range(LAYERS)):
        feed = feed_plain
        if pending is not None:
            held = []

            def feed(operands):
                sums, *results = reduce_layers(pending, 3, work=operands)
                held.append(sums[0])
                return results

        grad_stream, full_grads, grad_vector = layer_backward(
            grad_stream,
            saved_list[layer_at],
            kept_weights[layer_at],
            vector_all[layer_at * per_layer : (layer_at + 1) * per_layer],
            seq_lengths,
            feed,
        )
        if pending is not None:
            squares = squares + held[0]
        pending = full_grads
        vector_grads.insert(0, grad_vector)
    grad_low = grad_stream.astype(low)
    grad_near, grad_rest = grad_low[:near], grad_low[near:]
    grad_table = jnp.dot(grad_logits.T, group_rows, preferred_element_type=jnp.float32)
    if fused:
        ids = all_tokens - own_start
        ids = jnp.where((ids >= 0) & (ids < own_rows), ids, -1)[:, None]
        ids = [ids[:, :, :near], ids[:, :, near:]]
        grad_table, places, sums = spread_call(
            size, grad_near, grad_rest, ids, grad_table, shared, 4
        )
        squares = squares + jnp.sum(sums[0].reshape(-1, 128), axis=0)
        first_place = net.device * shared
        pos_shard = jnp.where(
            first_place < near, places[0], jnp.where(first_place < LEN, places[1], 0.0)
        )
    else:
        wholes = gather_call(size, [grad_near, grad_rest], (True, False), False, 4)
        for ids, whole in zip((ids_near, ids_rest), wholes):
            grad_table = grad_table + jnp.dot(
                one_hot(ids.reshape(-1)).T, whole.reshape(-1, D), preferred_element_type=jnp.float32
            )
        grad_table = grad_table[:height] + net.swap_core(grad_table[height:])
        squares = squares + jnp.sum(grad_table * grad_table, axis=0).reshape(-1, 128).sum(axis=0)
        grad_pos = jnp.concatenate(
            [jnp.sum(whole.astype(jnp.float32), axis=0) for whole in wholes]
        )
        grad_pos = jnp.pad(grad_pos, ((0, POS - LEN), (0, 0)))
        other_device = net.device + (1 - 2 * net.core) * size
        pos_shard = lax.dynamic_slice_in_dim(grad_pos, net.device * shared, shared) + net.swap_core(
            lax.dynamic_slice_in_dim(grad_pos, other_device * shared, shared)
        )
    table_shard = grad_table[:own_rows]
    grad_small = jnp.concatenate(vector_grads + [grad_gain_final, grad_shift_final])
    own_small = vectors.shape[0]
    grad_small = jnp.pad(grad_small.reshape(devices, own_small), ((0, 0), (0, -own_small % 1024)))
    small_shard, sums = reduce_layers(pending, 10, [grad_small.reshape(devices, -1, 128)])
    small_shard = small_shard.reshape(-1)[:own_small]
    pos_squares = jnp.sum(pos_shard * pos_shard, axis=0).reshape(-1, 128)
    squares = squares + sums[0] + jnp.sum(pos_squares, axis=0)
    qkv_shard = jnp.stack([member[0] for member in layer_shards])
    out_shard = jnp.stack([member[1] for member in layer_shards])
    fc_shard = jnp.stack([member[2] for member in layer_shards])
    proj_shard = jnp.stack([member[3] for member in layer_shards])
    shards = (qkv_shard, out_shard, fc_shard, proj_shard, small_shard, pos_shard, table_shard)
    sums = jnp.stack([squares, jnp.pad(own_loss[None], (0, 127))])
    sums = cast_call(size, jnp.pad(sums, ((0, 6), (0, 0))), True, 9)
    square_total, loss_total = jnp.sum(sums[:, 0]), jnp.sum(sums[:, 1])
    loss_value = loss_total / token_total
    grad_norm = jnp.sqrt(square_total)
    factor = CLIP_LIMIT / jnp.maximum(grad_norm, CLIP_LIMIT)
    step_float = step_count.astype(jnp.float32)
    params = (w_qkv, w_out, w_fc, w_proj, vectors, pos_table, embed_table)
    moments_one = (mom_qkv, mom_out, mom_fc, mom_proj, mom_vectors, mom_pos, mom_embed)
    moments_two = (sec_qkv, sec_out, sec_fc, sec_proj, sec_vectors, sec_pos, sec_embed)
    step_rates = (
        RATE_MATRIX,
        RATE_MATRIX,
        RATE_MATRIX,
        RATE_MATRIX,
        RATE_VECTOR,
        RATE_MATRIX,
        RATE_MATRIX,
    )
    decay_rates = (
        DECAY_MATRIX,
        DECAY_MATRIX,
        DECAY_MATRIX,
        DECAY_MATRIX,
        0.0,
        DECAY_MATRIX,
        DECAY_MATRIX,
    )
    results = [
        adamw(
            params[where_at],
            moments_one[where_at],
            moments_two[where_at],
            shards[where_at] * factor,
            step_rates[where_at],
            decay_rates[where_at],
            step_float,
        )
        for where_at in range(7)
    ]
    return (
        loss_value,
        grad_norm,
        results[0][0],
        results[1][0],
        results[2][0],
        results[3][0],
        results[4][0],
        results[5][0],
        results[6][0],
        results[0][1],
        results[1][1],
        results[2][1],
        results[3][1],
        results[4][1],
        results[5][1],
        results[6][1],
        results[0][2],
        results[1][2],
        results[2][2],
        results[3][2],
        results[4][2],
        results[5][2],
        results[6][2],
    )


def solution(mesh):
    return jax.shard_map(
        on_device,
        mesh=mesh,
        in_specs=(
            P(("narrow", "wide")),
            P(("narrow", "wide")),
            P(("narrow", "wide")),
            P(("narrow", "wide")),
            P(),
            P(None, ("narrow", "wide"), None),
            P(None, ("narrow", "wide"), None),
            P(None, ("narrow", "wide"), None),
            P(None, ("narrow", "wide"), None),
            P(("narrow", "wide")),
            P(("narrow", "wide"), None),
            P(("narrow", "wide"), None),
            P(None, ("narrow", "wide"), None),
            P(None, ("narrow", "wide"), None),
            P(None, ("narrow", "wide"), None),
            P(None, ("narrow", "wide"), None),
            P(("narrow", "wide")),
            P(("narrow", "wide"), None),
            P(("narrow", "wide"), None),
            P(None, ("narrow", "wide"), None),
            P(None, ("narrow", "wide"), None),
            P(None, ("narrow", "wide"), None),
            P(None, ("narrow", "wide"), None),
            P(("narrow", "wide")),
            P(("narrow", "wide"), None),
            P(("narrow", "wide"), None),
        ),
        out_specs=(
            P(),
            P(),
            P(None, ("narrow", "wide"), None),
            P(None, ("narrow", "wide"), None),
            P(None, ("narrow", "wide"), None),
            P(None, ("narrow", "wide"), None),
            P(("narrow", "wide")),
            P(("narrow", "wide"), None),
            P(("narrow", "wide"), None),
            P(None, ("narrow", "wide"), None),
            P(None, ("narrow", "wide"), None),
            P(None, ("narrow", "wide"), None),
            P(None, ("narrow", "wide"), None),
            P(("narrow", "wide")),
            P(("narrow", "wide"), None),
            P(("narrow", "wide"), None),
            P(None, ("narrow", "wide"), None),
            P(None, ("narrow", "wide"), None),
            P(None, ("narrow", "wide"), None),
            P(None, ("narrow", "wide"), None),
            P(("narrow", "wide")),
            P(("narrow", "wide"), None),
            P(("narrow", "wide"), None),
        ),
        check_vma=False,
    )
```
